32 devices in a mesh: row: 8 (over z, x), col: 4 (over y, core).
Axes of the slice: x: 2, y: 2, z: 4, core: 2. Of those that a mesh axis runs over, the one named last changes fastest.
Arguments:
- matrix: float32 [2048, 2048], P('row', 'col'), as said below
Outputs:
- factored: float32 [2048, 2048], P('row', 'col')
Inputs may be any that keep to these rules, and one draw needn't show every extreme that they name: `matrix`: each diagonal entry lies between 3 and 6 times the square root of 256; every other entry has magnitude 6 or less.
All inputs are finite; a program needn't handle non-finite values.
Results may differ from the reference program's by a relative error of at most 0.00085.
Values may be sent and summed in bfloat16 or wider, within the bound.
No kernel may reach another device: no remote copies, remote signals or barrier semaphores. Data moves between devices by JAX's collectives and lax.ppermute only.
A program may use at most 64 MiB of HBM per device.

```python
import jax
import jax.numpy as jnp
from jax import lax

NB = 256
TICKS = 1
SWEEPS = 2
ORDER = 2048
N_COL = 4


def draw_matrix(key, part):
    keyed = jax.random.fold_in(key, 7)
    first_key, second_key = jax.random.split(keyed, 2)
    noise = jnp.clip(jax.random.normal(first_key, (ORDER, ORDER), jnp.float32), -6.0, 6.0)
    diagonal = jnp.exp(jax.random.uniform(second_key, (ORDER,), jnp.float32, jnp.log(3.0), jnp.log(6.0))) * jnp.sqrt(jnp.float32(NB))
    positions = jnp.arange(ORDER, dtype=jnp.int32)
    return noise.at[positions, positions].set(diagonal).astype(jnp.float32)


def setup_inputs(seed: int = 0) -> dict:
    keys = jax.random.split(jax.random.key(seed), 2)
    return {
        "matrix": draw_matrix(jax.random.fold_in(keys[1], 71), 0),
    }


def newton(square):
    size = square.shape[0]
    identity = jnp.eye(size, dtype=jnp.float32)
    approx = identity / jnp.diagonal(square)[None, :]
    for sweep in range(SWEEPS):
        product = jnp.dot(square, approx, precision=lax.Precision.HIGHEST)
        approx = jnp.dot(approx, 2.0 * identity - product, precision=lax.Precision.HIGHEST)
    return approx


def reference(matrix):
    width = ORDER // N_COL
    positions = jnp.arange(ORDER, dtype=jnp.int32)
    done = positions < 0
    current = matrix
    for tick in range(TICKS):
        first = tick * (width + NB)
        square = current[first:first + NB, first:first + NB]
        inverse = newton(square)
        done = done | ((positions >= first) & (positions < first + NB))
        lower = jnp.dot(current[:, first:first + NB], inverse, precision=lax.Precision.HIGHEST)
        lower = jnp.where(done[:, None], jnp.zeros_like(lower), lower).astype(jnp.bfloat16)
        upper_rows = current[first:first + NB, :]
        upper = jnp.where(done[None, :], jnp.zeros_like(upper_rows), upper_rows).astype(jnp.bfloat16)
        current = current - jnp.dot(lower, upper, preferred_element_type=jnp.float32)
    return current
```

```python
import jax
import jax.numpy as jnp
from jax import lax
from jax.sharding import PartitionSpec as P

NB = 256
SWEEPS = 2


def spread(value, axis, order):
    here = lax.axis_index(axis)
    size = lax.axis_size(axis)
    holders = [0]
    for stride in order:
        pairs = [(h, h + stride) for h in holders]
        got = lax.ppermute(value, axis, pairs)
        takes = (here & stride) != 0
        below = here & (stride - 1)
        for held in order:
            if held < stride and held not in order[: order.index(stride)]:
                takes = takes & ((here & held) == 0)
        value = jnp.where(takes, got, value)
        holders = holders + [h + stride for h in holders]
    assert len(holders) == size
    return value


def strides(size):
    out, stride = [], size // 2
    while stride:
        out.append(stride)
        stride //= 2
    return out


def newton(square):
    size = square.shape[0]
    identity = jnp.eye(size, dtype=jnp.float32)
    diagonal = jnp.sum(square * identity, axis=0)
    approx = identity / diagonal[None, :]
    for sweep in range(SWEEPS):
        product = jnp.dot(square, approx, precision=lax.Precision.HIGHEST)
        approx = jnp.dot(approx, 2.0 * identity - product, precision=lax.Precision.HIGHEST)
    return approx


def shards(matrix):
    rows_dev, cols_dev = matrix.shape
    row_here = lax.axis_index("row")
    col_here = lax.axis_index("col")
    row_global = row_here * rows_dev + jnp.arange(rows_dev, dtype=jnp.int32)
    col_global = col_here * cols_dev + jnp.arange(cols_dev, dtype=jnp.int32)
    row_done = row_global < NB
    col_done = col_global < NB
    upper_wire = jnp.where(col_done[None, :], 0.0, matrix).astype(jnp.bfloat16)
    pivot_columns = matrix[:, :NB]
    square = spread(pivot_columns, "row", strides(lax.axis_size("row")))
    upper = spread(upper_wire, "row", strides(lax.axis_size("row")))
    inverse = newton(square)
    product = jnp.dot(pivot_columns, inverse, precision=lax.Precision.HIGHEST)
    lower = jnp.where(row_done[:, None], 0.0, product).astype(jnp.bfloat16)
    lower = spread(lower, "col", strides(lax.axis_size("col")))
    return matrix - jnp.dot(lower, upper, preferred_element_type=jnp.float32)


def solution(mesh):
    return jax.shard_map(
        shards,
        mesh=mesh,
        in_specs=(P("row", "col"),),
        out_specs=P("row", "col"),
        check_vma=False,
    )
```

```python
import jax
import jax.numpy as jnp
from jax import lax
from jax.experimental import pallas as pl
from jax.experimental.pallas import tpu as pltpu
from jax.sharding import PartitionSpec as P

NB = 256
HIGHEST = lax.Precision.HIGHEST
VMEM = pl.BlockSpec(memory_space=pltpu.VMEM)


def strides(size):
    out, stride = [], size // 2
    while stride:
        out.append(stride)
        stride //= 2
    return out


def multipliers_kernel(square_ref, columns_ref, lower_ref):
    square = square_ref[...]
    shape = square.shape
    on_diagonal = lax.broadcasted_iota(jnp.int32, shape, 0) == lax.broadcasted_iota(
        jnp.int32, shape, 1
    )
    diagonal = jnp.where(on_diagonal, square, 0.0)
    across = 1.0 / jnp.sum(diagonal, axis=0, keepdims=True)
    down = 1.0 / jnp.sum(diagonal, axis=1, keepdims=True)
    twice = jnp.where(on_diagonal, 2.0, 0.0)
    approx = down * (twice - square * across)
    rest = twice - jnp.dot(square, approx, precision=HIGHEST)
    half = jnp.dot(columns_ref[...], approx, precision=HIGHEST)
    lower_ref[...] = jnp.dot(half, rest, precision=HIGHEST).astype(jnp.bfloat16)


def update_kernel(odd_ref, matrix_ref, lower_ref, part_ref, other_ref, out_ref):
    half = part_ref.shape[1]
    lower = lower_ref[...]

    def change(piece):
        return jnp.dot(lower, piece, preferred_element_type=jnp.float32)

    own, swapped = change(part_ref[...]), change(other_ref[...])
    odd = odd_ref[0] == 1
    out_ref[:, :half] = matrix_ref[:, :half] - jnp.where(odd, swapped, own)
    out_ref[:, half:] = matrix_ref[:, half:] - jnp.where(odd, own, swapped)


def shards(matrix):
    rows_dev, cols_dev = matrix.shape
    n_row, n_col = lax.axis_size("row"), lax.axis_size("col")
    half = cols_dev // 2
    row_here, col_here = lax.axis_index("row"), lax.axis_index("col")
    row_done = row_here * rows_dev + jnp.arange(rows_dev, dtype=jnp.int32) < NB
    col_done = col_here * cols_dev + jnp.arange(cols_dev, dtype=jnp.int32) < NB
    odd = row_here % 2 == 1

    def send(value, pairs):
        flat = [(r0 * n_col + c0, r1 * n_col + c1) for (r0, c0), (r1, c1) in pairs]
        return lax.ppermute(value, ("row", "col"), flat)

    upper = jnp.where(col_done[None, :], 0.0, matrix).astype(jnp.bfloat16)
    left, right = upper[:, :half], upper[:, half:]
    pivot_columns = matrix[:, :NB]
    left_from = 1 if half <= NB else 0

    def pairs_of(step):
        return [((a, c), (b, c)) for a, b in step for c in range(n_col) if a % 2 or c >= left_from]

    square, part = pivot_columns, left
    square_held, part_held = [0], [0, 1]
    part_step = [((0, c), (1, c)) for c in range(n_col)]
    part_sent, part_takes = right, row_here == 1
    for stride in strides(n_row):
        got = send(square, [((h, 0), (h + stride, 0)) for h in square_held])
        got_part = send(part_sent, part_step)
        square = jnp.where((row_here & (2 * stride - 1)) == stride, got, square)
        part = jnp.where(part_takes, got_part, part)
        square, part = lax.optimization_barrier((square, part))
        square_held = square_held + [h + stride for h in square_held]
        if stride > 1:
            part_step = pairs_of([(h, h + stride) for h in part_held])
            part_sent, part_takes = part, (row_here & (2 * stride - 2)) == stride
            part_held = part_held + [h + stride for h in part_held]
    other = send(
        part,
        [
            ((r, c), (r ^ 1, c))
            for r in range(n_row)
            for c in range(n_col)
            if r != 1 and (r % 2 or c >= left_from)
        ],
    )

    def multipliers(square):
        lower = pl.pallas_call(
            multipliers_kernel,
            out_shape=jax.ShapeDtypeStruct((rows_dev, NB), jnp.bfloat16),
            in_specs=[VMEM, VMEM],
            out_specs=VMEM,
            name="multipliers",
        )(square, pivot_columns)
        return jnp.where(row_done[:, None], jnp.zeros_like(lower), lower)

    def none(square):
        return jnp.zeros((rows_dev, NB), jnp.bfloat16)

    lower = lax.cond(col_here == 0, multipliers, none, square)
    held = [0]
    for stride in strides(n_col):
        got = send(lower, [((r, c), (r, c + stride)) for r in range(1, n_row) for c in held])
        lower = jnp.where((col_here & (2 * stride - 1)) == stride, got, lower)
        held = held + [c + stride for c in held]

    return pl.pallas_call(
        update_kernel,
        out_shape=jax.ShapeDtypeStruct((rows_dev, cols_dev), jnp.float32),
        in_specs=[pl.BlockSpec(memory_space=pltpu.SMEM), VMEM, VMEM, VMEM, VMEM],
        out_specs=VMEM,
        name="update",
    )(odd.astype(jnp.int32).reshape(1), matrix, lower, part, other)


def solution(mesh):
    return jax.shard_map(
        shards,
        mesh=mesh,
        in_specs=(P("row", "col"),),
        out_specs=P("row", "col"),
        check_vma=False,
    )
```

```python
import jax
import jax.numpy as jnp
from jax import lax
from jax.sharding import PartitionSpec as P

NB = 256
HIGHEST = lax.Precision.HIGHEST


def strides(size):
    out, stride = [], size // 2
    while stride:
        out.append(stride)
        stride //= 2
    return out


def shards(matrix):
    rows_dev, cols_dev = matrix.shape
    n_row, n_col = lax.axis_size("row"), lax.axis_size("col")
    half = cols_dev // 2
    row_here, col_here = lax.axis_index("row"), lax.axis_index("col")
    row_done = row_here * rows_dev + jnp.arange(rows_dev, dtype=jnp.int32) < NB
    col_done = col_here * cols_dev + jnp.arange(cols_dev, dtype=jnp.int32) < NB
    odd = row_here % 2 == 1

    def send(value, pairs):
        flat = [(r0 * n_col + c0, r1 * n_col + c1) for (r0, c0), (r1, c1) in pairs]
        return lax.ppermute(value, ("row", "col"), flat)

    upper = jnp.where(col_done[None, :], 0.0, matrix).astype(jnp.bfloat16)
    left, right = upper[:, :half], upper[:, half:]
    pivot_columns = matrix[:, :NB]
    left_from = 1 if half <= NB else 0

    def pairs_of(step):
        return [((a, c), (b, c)) for a, b in step for c in range(n_col) if a % 2 or c >= left_from]

    first, second = lax.optimization_barrier((matrix[: NB // 2, :NB], matrix[NB // 2 : NB, :NB]))
    part = left
    square_held, part_held = [0], [0, 1]
    part_step = [((0, c), (1, c)) for c in range(n_col)]
    part_sent, part_takes = right, row_here == 1
    for stride in strides(n_row):
        square_step = [((h, 0), (h + stride, 0)) for h in square_held]
        takes = (row_here & (2 * stride - 1)) == stride
        got_first = send(first, square_step)
        got_second = send(second, square_step)
        got_part = send(part_sent, part_step)
        first = jnp.where(takes, got_first, first)
        second = jnp.where(takes, got_second, second)
        part = jnp.where(part_takes, got_part, part)
        square_held = square_held + [h + stride for h in square_held]
        if stride > 1:
            part_step = pairs_of([(h, h + stride) for h in part_held])
            part_sent, part_takes = part, (row_here & (2 * stride - 2)) == stride
            part_held = part_held + [h + stride for h in part_held]
    other = send(
        part,
        [
            ((r, c), (r ^ 1, c))
            for r in range(n_row)
            for c in range(n_col)
            if r != 1 and (r % 2 or c >= left_from)
        ],
    )

    def multipliers(first, second):
        square = jnp.concatenate([first, second], axis=0)
        identity = jnp.eye(NB, dtype=jnp.float32)
        diagonal = square * identity
        across = 1.0 / jnp.sum(diagonal, axis=0, keepdims=True)
        down = 1.0 / jnp.sum(diagonal, axis=1, keepdims=True)
        approx = down * (2.0 * identity - square * across)
        rest = 2.0 * identity - jnp.dot(square, approx, precision=HIGHEST)
        lower = jnp.dot(jnp.dot(pivot_columns, approx, precision=HIGHEST), rest, precision=HIGHEST)
        return jnp.where(row_done[:, None], 0.0, lower).astype(jnp.bfloat16)

    def none(first, second):
        return jnp.zeros((rows_dev, NB), jnp.bfloat16)

    lower = lax.cond(col_here == 0, multipliers, none, first, second)
    held = [0]
    for stride in strides(n_col):
        got = send(lower, [((r, c), (r, c + stride)) for r in range(1, n_row) for c in held])
        lower = jnp.where((col_here & (2 * stride - 1)) == stride, got, lower)
        held = held + [c + stride for c in held]
        lower, other = lax.optimization_barrier((lower, other))

    upper = jnp.where(
        odd,
        jnp.concatenate([other, part], axis=1),
        jnp.concatenate([part, other], axis=1),
    )
    return matrix - jnp.dot(lower, upper, preferred_element_type=jnp.float32)


def solution(mesh):
    return jax.shard_map(
        shards,
        mesh=mesh,
        in_specs=(P("row", "col"),),
        out_specs=P("row", "col"),
        check_vma=False,
    )
```

```python
import jax
import jax.numpy as jnp
from jax import lax
from jax.sharding import PartitionSpec as P

NB = 256
HIGHEST = lax.Precision.HIGHEST
APART = 2


def strides(size):
    out, stride = [], size // 2
    while stride:
        out.append(stride)
        stride //= 2
    return out


def multipliers(square, columns):
    identity = jnp.eye(NB, dtype=jnp.float32)
    diagonal = square * identity
    across = 1.0 / jnp.sum(diagonal, axis=0, keepdims=True)
    down = 1.0 / jnp.sum(diagonal, axis=1, keepdims=True)
    approx = down * (2.0 * identity - square * across)
    rest = 2.0 * identity - jnp.dot(square, approx, precision=HIGHEST)
    return jnp.dot(jnp.dot(columns, approx, precision=HIGHEST), rest, precision=HIGHEST)


def shards(matrix):
    rows_dev, cols_dev = matrix.shape
    assert rows_dev == NB
    n_row, n_col = lax.axis_size("row"), lax.axis_size("col")
    row_here, col_here = lax.axis_index("row"), lax.axis_index("col")

    def send(value, pairs):
        flat = [(r0 * n_col + c0, r1 * n_col + c1) for (r0, c0), (r1, c1) in pairs]
        return lax.ppermute(value, ("row", "col"), flat)

    upper = matrix.astype(jnp.bfloat16)
    pivot_columns = matrix[:, :NB]

    down = strides(n_row)
    orders = [[down[-1]] + down[:-1], down]
    held = [[0], [0]]

    def upper_step(value, step):
        pairs = []
        takes = []
        for kind in range(2):
            stride = orders[kind][step]
            missing = sum(orders[kind][step + 1 :])
            takes.append((row_here & (stride | missing)) == stride)
            pairs += [
                ((h, c), (h + stride, c)) for h in held[kind] for c in range(1, n_col) if c % 2 == kind
            ]
            held[kind] = held[kind] + [h + stride for h in held[kind]]
        got = send(value, pairs)
        return jnp.where(jnp.where(col_here % 2 == 0, takes[0], takes[1]), got, value)

    workers = [r for r in range(n_row) if r & APART == 0]
    targets = workers[1:]
    square, partner = pivot_columns, pivot_columns
    column_upper = upper[:, NB:]
    near_upper = column_upper
    upper = upper_step(upper, 0)
    for index, target in enumerate(targets):
        pairs = [((0, 0), (target, 0))]
        if index == 0:
            served = [r for r in workers if r != target]
        elif index == 1:
            served = targets[:1]
        else:
            served = []
        pairs += [((r + APART, 0), (r, 0)) for r in served]
        got = send(pivot_columns, pairs)
        square = jnp.where(row_here == target, got, square)
        if index == 0:
            partner = jnp.where(row_here == target, partner, got)
        elif index == 1:
            partner = jnp.where(row_here == targets[0], got, partner)
    for target in targets:
        got = send(column_upper, [((0, 0), (target, 0))])
        near_upper = jnp.where(row_here == target, got, near_upper)
    upper = upper_step(upper, 1)

    def compute(square, partner):
        both = multipliers(square, jnp.concatenate([pivot_columns, partner], axis=0))
        both = both.astype(jnp.bfloat16)
        return both[:NB], both[NB:]

    def none(square, partner):
        zero = jnp.zeros((NB, NB), jnp.bfloat16)
        return zero, zero

    working = (row_here & APART == 0) & (col_here == 0)
    lower, lower_far = lax.cond(working, compute, none, square, partner)
    got_far = send(near_upper, [((r, 0), (r + APART, 0)) for r in workers])
    near_upper = jnp.where(row_here & APART == 0, near_upper, got_far)

    received = lower
    for c in reversed(range(0, n_col, 2)):
        got = send(lower_far, [((r, 0), (r + APART, c)) for r in workers])
        received = jnp.where((row_here & APART != 0) & (col_here == c), got, received)
    for c in range(2, n_col, 2):
        got = send(lower, [((r, 0), (r, c)) for r in targets])
        received = jnp.where((row_here & APART == 0) & (col_here == c), got, received)
    for step in range(2, len(down)):
        upper = upper_step(upper, step)
    got = send(
        received, [((r, c), (r, c + 1)) for r in range(1, n_row) for c in range(0, n_col, 2)]
    )
    received = jnp.where(col_here % 2 == 0, received, got)
    received = jnp.where(row_here == 0, jnp.zeros_like(received), received)

    column_upper = jnp.concatenate([jnp.zeros((NB, NB), jnp.bfloat16), near_upper], axis=1)
    upper = jnp.where(col_here == 0, column_upper, upper)
    return matrix - jnp.dot(received, upper, preferred_element_type=jnp.float32)


def solution(mesh):
    return jax.shard_map(
        shards,
        mesh=mesh,
        in_specs=(P("row", "col"),),
        out_specs=P("row", "col"),
        check_vma=False,
    )
```

```python
import jax
import jax.numpy as jnp
from jax import lax
from jax.sharding import PartitionSpec as P

NB = 256
HIGHEST = lax.Precision.HIGHEST
APART = 2


def strides(size):
    out, stride = [], size // 2
    while stride:
        out.append(stride)
        stride //= 2
    return out


def multipliers(square, columns):
    identity = jnp.eye(NB, dtype=jnp.float32)
    diagonal = square * identity
    across = 1.0 / jnp.sum(diagonal, axis=0, keepdims=True)
    down = 1.0 / jnp.sum(diagonal, axis=1, keepdims=True)
    approx = down * (2.0 * identity - square * across)
    rest = 2.0 * identity - jnp.dot(square, approx, precision=HIGHEST)
    return jnp.dot(jnp.dot(columns, approx, precision=HIGHEST), rest, precision=HIGHEST)


def shards(matrix):
    rows_dev, cols_dev = matrix.shape
    assert rows_dev == NB
    n_row, n_col = lax.axis_size("row"), lax.axis_size("col")
    row_here, col_here = lax.axis_index("row"), lax.axis_index("col")

    def send(value, pairs):
        flat = [(r0 * n_col + c0, r1 * n_col + c1) for (r0, c0), (r1, c1) in pairs]
        return lax.ppermute(value, ("row", "col"), flat)

    upper = matrix.astype(jnp.bfloat16)
    pivot_columns, column_upper = lax.optimization_barrier((matrix[:, :NB], upper[:, NB:]))

    down = strides(n_row)
    orders = [down, [down[-1]] + down[:-1]]
    held = [[0], [0]]

    def upper_step(value, step):
        pairs = []
        takes = []
        for kind in range(2):
            stride = orders[kind][step]
            missing = sum(orders[kind][step + 1 :])
            takes.append((row_here & (stride | missing)) == stride)
            pairs += [
                ((h, c), (h + stride, c)) for h in held[kind] for c in range(1, n_col) if c % 2 == kind
            ]
            held[kind] = held[kind] + [h + stride for h in held[kind]]
        got = send(value, pairs)
        return jnp.where(jnp.where(col_here % 2 == 0, takes[0], takes[1]), got, value)

    workers = [r for r in range(n_row) if r & APART == 0]
    targets = workers[1:]
    square, partner = pivot_columns, pivot_columns
    near_upper = column_upper
    upper = upper_step(upper, 0)
    for index, target in enumerate(targets):
        pairs = [((0, 0), (target, 0))]
        if index == 0:
            served = [r for r in workers if r != target]
        elif index == 1:
            served = targets[:1]
        else:
            served = []
        pairs += [((r + APART, 0), (r, 0)) for r in served]
        got = send(pivot_columns, pairs)
        square = jnp.where(row_here == target, got, square)
        if index == 0:
            partner = jnp.where(row_here == target, partner, got)
        elif index == 1:
            partner = jnp.where(row_here == targets[0], got, partner)
    for target in targets:
        got = send(column_upper, [((0, 0), (target, 0))])
        near_upper = jnp.where(row_here == target, got, near_upper)
    upper = upper_step(upper, 1)

    def compute(square, partner):
        both = multipliers(square, jnp.concatenate([pivot_columns, partner], axis=0))
        both = both.astype(jnp.bfloat16)
        return both[:NB], both[NB:]

    def none(square, partner):
        zero = jnp.zeros((NB, NB), jnp.bfloat16)
        return zero, zero

    working = (row_here & APART == 0) & (col_here == 0)
    lower, lower_far = lax.cond(working, compute, none, square, partner)
    received = lower
    for c in range(2, n_col, 2):
        got = send(lower_far, [((r, 0), (r + APART, c)) for r in workers])
        received = jnp.where((row_here & APART != 0) & (col_here == c), got, received)
    both = jnp.concatenate([lower_far, near_upper], axis=1)
    got = send(both, [((r, 0), (r + APART, 0)) for r in workers])
    received = jnp.where((row_here & APART != 0) & (col_here == 0), got[:, :NB], received)
    near_upper = jnp.where(row_here & APART == 0, near_upper, got[:, NB:])
    for c in range(2, n_col, 2):
        got = send(lower, [((r, 0), (r, c)) for r in targets])
        received = jnp.where((row_here & APART == 0) & (col_here == c), got, received)
    for step in range(2, len(down)):
        upper = upper_step(upper, step)
    got = send(
        received, [((r, c), (r, c + 1)) for r in range(1, n_row) for c in range(0, n_col, 2)]
    )
    received = jnp.where(col_here % 2 == 0, received, got)
    received = jnp.where(row_here == 0, jnp.zeros_like(received), received)

    column_upper = jnp.concatenate([jnp.zeros((NB, NB), jnp.bfloat16), near_upper], axis=1)
    upper = jnp.where(col_here == 0, column_upper, upper)
    return matrix - jnp.dot(received, upper, preferred_element_type=jnp.float32)


def solution(mesh):
    return jax.shard_map(
        shards,
        mesh=mesh,
        in_specs=(P("row", "col"),),
        out_specs=P("row", "col"),
        check_vma=False,
    )
```

```python
import jax
import jax.numpy as jnp
from jax import lax
from jax.sharding import PartitionSpec as P

NB = 256
HIGHEST = lax.Precision.HIGHEST
APART = 2


def strides(size):
    out, stride = [], size // 2
    while stride:
        out.append(stride)
        stride //= 2
    return out


def multipliers(square, columns):
    identity = jnp.eye(NB, dtype=jnp.float32)
    diagonal = square * identity
    across = 1.0 / jnp.sum(diagonal, axis=0, keepdims=True)
    down = 1.0 / jnp.sum(diagonal, axis=1, keepdims=True)
    approx = down * (2.0 * identity - square * across)
    rest = 2.0 * identity - jnp.dot(square, approx, precision=HIGHEST)
    return jnp.dot(jnp.dot(columns, approx, precision=HIGHEST), rest, precision=HIGHEST)


def shards(matrix):
    rows_dev, cols_dev = matrix.shape
    assert rows_dev == NB
    n_row, n_col = lax.axis_size("row"), lax.axis_size("col")
    row_here, col_here = lax.axis_index("row"), lax.axis_index("col")

    def send(value, pairs):
        flat = [(r0 * n_col + c0, r1 * n_col + c1) for (r0, c0), (r1, c1) in pairs]
        return lax.ppermute(value, ("row", "col"), flat)

    upper = matrix.astype(jnp.bfloat16)
    pivot_columns, column_upper = matrix[:, :NB], upper[:, NB:]

    down = strides(n_row)
    orders = [down, [down[-1]] + down[:-1]]
    held = [[0], [0]]

    def upper_step(value, step):
        pairs = []
        takes = []
        for kind in range(2):
            stride = orders[kind][step]
            missing = sum(orders[kind][step + 1 :])
            takes.append((row_here & (stride | missing)) == stride)
            pairs += [
                ((h, c), (h + stride, c)) for h in held[kind] for c in range(1, n_col) if c % 2 == kind
            ]
            held[kind] = held[kind] + [h + stride for h in held[kind]]
        got = send(value, pairs)
        return jnp.where(jnp.where(col_here % 2 == 0, takes[0], takes[1]), got, value)

    workers = [r for r in range(n_row) if r & APART == 0]
    targets = workers[1:]
    square, partner = pivot_columns, pivot_columns
    near_upper = column_upper
    upper, column_upper = lax.optimization_barrier((upper_step(upper, 0), column_upper))
    for index, target in enumerate(targets):
        pairs = [((0, 0), (target, 0))]
        if index == 0:
            served = [r for r in workers if r != target]
        elif index == 1:
            served = targets[:1]
        else:
            served = []
        pairs += [((r + APART, 0), (r, 0)) for r in served]
        got = send(pivot_columns, pairs)
        square = jnp.where(row_here == target, got, square)
        if index == 0:
            partner = jnp.where(row_here == target, partner, got)
        elif index == 1:
            partner = jnp.where(row_here == targets[0], got, partner)
    for target in targets:
        got = send(column_upper, [((0, 0), (target, 0))])
        near_upper = jnp.where(row_here == target, got, near_upper)
    upper = upper_step(upper, 1)

    def compute(square, partner):
        both = multipliers(square, jnp.concatenate([pivot_columns, partner], axis=0))
        both = both.astype(jnp.bfloat16)
        return both[:NB], both[NB:]

    def none(square, partner):
        zero = jnp.zeros((NB, NB), jnp.bfloat16)
        return zero, zero

    working = (row_here & APART == 0) & (col_here == 0)
    lower, lower_far = lax.cond(working, compute, none, square, partner)
    received = lower
    for c in range(2, n_col, 2):
        got = send(lower_far, [((r, 0), (r + APART, c)) for r in workers])
        received = jnp.where((row_here & APART != 0) & (col_here == c), got, received)
    both = jnp.concatenate([lower_far, near_upper], axis=1)
    got = send(both, [((r, 0), (r + APART, 0)) for r in workers])
    received = jnp.where((row_here & APART != 0) & (col_here == 0), got[:, :NB], received)
    near_upper = jnp.where(row_here & APART == 0, near_upper, got[:, NB:])
    for c in range(2, n_col, 2):
        got = send(lower, [((r, 0), (r, c)) for r in targets])
        received = jnp.where((row_here & APART == 0) & (col_here == c), got, received)
    for step in range(2, len(down)):
        upper = upper_step(upper, step)
    got = send(
        received, [((r, c), (r, c + 1)) for r in range(1, n_row) for c in range(0, n_col, 2)]
    )
    received = jnp.where(col_here % 2 == 0, received, got)
    received = jnp.where(row_here == 0, jnp.zeros_like(received), received)

    column_upper = jnp.concatenate([jnp.zeros((NB, NB), jnp.bfloat16), near_upper], axis=1)
    upper = jnp.where(col_here == 0, column_upper, upper)
    return matrix - jnp.dot(received, upper, preferred_element_type=jnp.float32)


def solution(mesh):
    return jax.shard_map(
        shards,
        mesh=mesh,
        in_specs=(P("row", "col"),),
        out_specs=P("row", "col"),
        check_vma=False,
    )
```

```python
import jax
import jax.numpy as jnp
from jax import lax
from jax.sharding import PartitionSpec as P

NB = 256
HIGHEST = lax.Precision.HIGHEST
APART = 2


def strides(size):
    out, stride = [], size // 2
    while stride:
        out.append(stride)
        stride //= 2
    return out


def multipliers(square, columns):
    identity = jnp.eye(NB, dtype=jnp.float32)
    diagonal = square * identity
    across = 1.0 / jnp.sum(diagonal, axis=0, keepdims=True)
    down = 1.0 / jnp.sum(diagonal, axis=1, keepdims=True)
    approx = down * (2.0 * identity - square * across)
    rest = 2.0 * identity - jnp.dot(square, approx, precision=HIGHEST)
    return jnp.dot(jnp.dot(columns, approx, precision=HIGHEST), rest, precision=HIGHEST)


def shards(matrix):
    rows_dev, cols_dev = matrix.shape
    assert rows_dev == NB
    n_row, n_col = lax.axis_size("row"), lax.axis_size("col")
    half = cols_dev // 2
    row_here, col_here = lax.axis_index("row"), lax.axis_index("col")
    col_done = col_here * cols_dev + jnp.arange(cols_dev, dtype=jnp.int32) < NB
    odd = row_here % 2 == 1

    def send(value, pairs):
        flat = [(r0 * n_col + c0, r1 * n_col + c1) for (r0, c0), (r1, c1) in pairs]
        return lax.ppermute(value, ("row", "col"), flat)

    upper = jnp.where(col_done[None, :], 0.0, matrix).astype(jnp.bfloat16)
    left, right = upper[:, :half], upper[:, half:]
    pivot_columns = matrix[:, :NB]
    left_from = 1 if half <= NB else 0

    got = send(right, [((0, c), (1, c)) for c in range(n_col)])
    part = jnp.where(row_here == 1, got, left)
    part_held = [0, 1]

    def part_step(part, stride):
        pairs = [
            ((h, c), (h + stride, c))
            for h in part_held
            for c in range(n_col)
            if h % 2 or c >= left_from
        ]
        got = send(part, pairs)
        part_held.extend([h + stride for h in part_held])
        return jnp.where((row_here & (2 * stride - 2)) == stride, got, part)

    workers = [r for r in range(n_row) if r & APART == 0]
    targets = workers[1:]
    square, partner = pivot_columns, pivot_columns
    for index, target in enumerate(targets):
        pairs = [((0, 0), (target, 0))]
        if index == 0:
            served = [r for r in workers if r != target]
        elif index == 1:
            served = targets[:1]
        else:
            served = []
        pairs += [((r + APART, 0), (r, 0)) for r in served]
        got = send(pivot_columns, pairs)
        square = jnp.where(row_here == target, got, square)
        if index == 0:
            partner = jnp.where(row_here == target, partner, got)
        elif index == 1:
            partner = jnp.where(row_here == targets[0], got, partner)

    middle = strides(n_row)[:-1]
    for stride in middle[:-1]:
        part = part_step(part, stride)
    square, part = lax.optimization_barrier((square, part))
    part = part_step(part, middle[-1])

    def compute(square, partner):
        both = multipliers(square, jnp.concatenate([pivot_columns, partner], axis=0))
        both = both.astype(jnp.bfloat16)
        return both[:NB], both[NB:]

    def none(square, partner):
        zero = jnp.zeros((NB, NB), jnp.bfloat16)
        return zero, zero

    working = (row_here & APART == 0) & (col_here == 0)
    lower, lower_far = lax.cond(working, compute, none, square, partner)

    received = lower
    for c in range(2, n_col, 2):
        got = send(lower_far, [((r, 0), (r + APART, c)) for r in workers])
        received = jnp.where((row_here & APART != 0) & (col_here == c), got, received)
    got = send(lower_far, [((r, 0), (r + APART, 0)) for r in workers])
    received = jnp.where((row_here & APART != 0) & (col_here == 0), got, received)
    for c in range(2, n_col, 2):
        got = send(lower, [((r, 0), (r, c)) for r in targets])
        received = jnp.where((row_here & APART == 0) & (col_here == c), got, received)
    other = send(
        part,
        [
            ((r, c), (r ^ 1, c))
            for r in range(n_row)
            for c in range(n_col)
            if r != 1 and (r % 2 or c >= left_from)
        ],
    )
    received, other = lax.optimization_barrier((received, other))
    got = send(
        received, [((r, c), (r, c + 1)) for r in range(1, n_row) for c in range(0, n_col, 2)]
    )
    received = jnp.where(col_here % 2 == 0, received, got)
    received = jnp.where(row_here == 0, jnp.zeros_like(received), received)

    upper = jnp.where(
        odd,
        jnp.concatenate([other, part], axis=1),
        jnp.concatenate([part, other], axis=1),
    )
    return matrix - jnp.dot(received, upper, preferred_element_type=jnp.float32)


def solution(mesh):
    return jax.shard_map(
        shards,
        mesh=mesh,
        in_specs=(P("row", "col"),),
        out_specs=P("row", "col"),
        check_vma=False,
    )
```

```python
import jax
import jax.numpy as jnp
from jax import lax
from jax.sharding import PartitionSpec as P

NB = 256
HIGHEST = lax.Precision.HIGHEST
APART = 2


def strides(size):
    out, stride = [], size // 2
    while stride:
        out.append(stride)
        stride //= 2
    return out


def multipliers(square, columns):
    identity = jnp.eye(NB, dtype=jnp.float32)
    diagonal = square * identity
    across = 1.0 / jnp.sum(diagonal, axis=0, keepdims=True)
    down = 1.0 / jnp.sum(diagonal, axis=1, keepdims=True)
    approx = down * (2.0 * identity - square * across)
    rest = 2.0 * identity - jnp.dot(square, approx, precision=HIGHEST)
    return jnp.dot(jnp.dot(columns, approx, precision=HIGHEST), rest, precision=HIGHEST)


def shards(matrix):
    rows_dev, cols_dev = matrix.shape
    assert rows_dev == NB
    n_row, n_col = lax.axis_size("row"), lax.axis_size("col")
    row_here, col_here = lax.axis_index("row"), lax.axis_index("col")

    def send(value, pairs):
        flat = [(r0 * n_col + c0, r1 * n_col + c1) for (r0, c0), (r1, c1) in pairs]
        return lax.ppermute(value, ("row", "col"), flat)

    upper = matrix.astype(jnp.bfloat16)
    pivot_columns, column_upper = matrix[:, :NB], upper[:, NB:]

    down = strides(n_row)
    orders = [down, [down[-1]] + down[:-1]]
    held = [[0], [0]]

    def upper_step(value, step):
        pairs = []
        takes = []
        for kind in range(2):
            stride = orders[kind][step]
            missing = sum(orders[kind][step + 1 :])
            takes.append((row_here & (stride | missing)) == stride)
            pairs += [
                ((h, c), (h + stride, c)) for h in held[kind] for c in range(1, n_col) if c % 2 == kind
            ]
            held[kind] = held[kind] + [h + stride for h in held[kind]]
        got = send(value, pairs)
        return jnp.where(jnp.where(col_here % 2 == 0, takes[0], takes[1]), got, value)

    workers = [r for r in range(n_row) if r & APART == 0]
    targets = workers[2:] + workers[1:2]
    square, partner = pivot_columns, pivot_columns
    near_upper = column_upper
    upper, column_upper = lax.optimization_barrier((upper_step(upper, 0), column_upper))
    for index, target in enumerate(targets):
        pairs = [((0, 0), (target, 0))]
        if index == 0:
            served = [r for r in workers if r != target]
        elif index == 1:
            served = targets[:1]
        else:
            served = []
        pairs += [((r + APART, 0), (r, 0)) for r in served]
        got = send(pivot_columns, pairs)
        square = jnp.where(row_here == target, got, square)
        if index == 0:
            partner = jnp.where(row_here == target, partner, got)
        elif index == 1:
            partner = jnp.where(row_here == targets[0], got, partner)
    for target in reversed(workers[1:]):
        got = send(column_upper, [((0, 0), (target, 0))])
        near_upper = jnp.where(row_here == target, got, near_upper)
    upper = upper_step(upper, 1)

    def compute(square, partner):
        both = multipliers(square, jnp.concatenate([pivot_columns, partner], axis=0))
        both = both.astype(jnp.bfloat16)
        return both[:NB], both[NB:]

    def none(square, partner):
        zero = jnp.zeros((NB, NB), jnp.bfloat16)
        return zero, zero

    working = (row_here & APART == 0) & (col_here == 0)
    lower, lower_far = lax.cond(working, compute, none, square, partner)
    received = lower
    for c in range(2, n_col, 2):
        got = send(lower_far, [((r, 0), (r + APART, c)) for r in workers])
        received = jnp.where((row_here & APART != 0) & (col_here == c), got, received)
    got = send(lower_far, [((r, 0), (r + APART, 0)) for r in workers])
    received = jnp.where((row_here & APART != 0) & (col_here == 0), got, received)
    for c in range(2, n_col, 2):
        got = send(lower, [((r, 0), (r, c)) for r in targets])
        received = jnp.where((row_here & APART == 0) & (col_here == c), got, received)
    near_sent, _ = lax.optimization_barrier((near_upper, lower))
    got = send(near_sent, [((r, 0), (r + APART, 0)) for r in workers])
    near_upper = jnp.where(row_here & APART == 0, near_upper, got)
    for step in range(2, len(down)):
        upper = upper_step(upper, step)
    got = send(
        received, [((r, c), (r, c + 1)) for r in range(1, n_row) for c in range(0, n_col, 2)]
    )
    received = jnp.where(col_here % 2 == 0, received, got)
    received = jnp.where(row_here == 0, jnp.zeros_like(received), received)

    column_upper = jnp.concatenate([jnp.zeros((NB, NB), jnp.bfloat16), near_upper], axis=1)
    upper = jnp.where(col_here == 0, column_upper, upper)
    return matrix - jnp.dot(received, upper, preferred_element_type=jnp.float32)


def solution(mesh):
    return jax.shard_map(
        shards,
        mesh=mesh,
        in_specs=(P("row", "col"),),
        out_specs=P("row", "col"),
        check_vma=False,
    )
```

```python
import jax
import jax.numpy as jnp
from jax import lax
from jax.sharding import PartitionSpec as P

NB = 256
HIGH = lax.Precision.HIGH
APART = 2


def strides(size):
    out, stride = [], size // 2
    while stride:
        out.append(stride)
        stride //= 2
    return out


def multipliers(square, columns):
    identity = jnp.eye(NB, dtype=jnp.float32)
    diagonal = square * identity
    across = 1.0 / jnp.sum(diagonal, axis=0, keepdims=True)
    down = 1.0 / jnp.sum(diagonal, axis=1, keepdims=True)
    approx = down * (2.0 * identity - square * across)
    product = jnp.dot(jnp.concatenate([square, columns], axis=0), approx, precision=HIGH)
    return jnp.dot(product[NB:], 2.0 * identity - product[:NB], precision=HIGH)


def shards(matrix):
    rows_dev, cols_dev = matrix.shape
    assert rows_dev == NB
    n_row, n_col = lax.axis_size("row"), lax.axis_size("col")
    row_here, col_here = lax.axis_index("row"), lax.axis_index("col")

    def send(value, pairs):
        flat = [(r0 * n_col + c0, r1 * n_col + c1) for (r0, c0), (r1, c1) in pairs]
        return lax.ppermute(value, ("row", "col"), flat)

    pivot_columns = matrix[:, :NB]
    high = pivot_columns.astype(jnp.bfloat16)
    low = (pivot_columns - high.astype(jnp.float32)).astype(jnp.bfloat16)
    terms = jnp.pad(jnp.concatenate([high, low], axis=1), ((0, 0), (0, cols_dev - 2 * NB)))
    column_upper = matrix[:, NB:].astype(jnp.bfloat16)
    upper = jnp.where(col_here == 0, terms, matrix.astype(jnp.bfloat16))

    def summed(terms):
        return terms[:, :NB].astype(jnp.float32) + terms[:, NB : 2 * NB].astype(jnp.float32)

    down = strides(n_row)
    orders = [down, [down[-1]] + down[:-1]]
    held = [[0], [0]]

    def upper_step(value, step, pairs=()):
        pairs = list(pairs)
        takes = []
        for kind in range(2):
            stride = orders[kind][step]
            missing = sum(orders[kind][step + 1 :])
            takes.append((row_here & (stride | missing)) == stride)
            pairs += [
                ((h, c), (h + stride, c)) for h in held[kind] for c in range(1, n_col) if c % 2 == kind
            ]
            held[kind] = held[kind] + [h + stride for h in held[kind]]
        got = send(value, pairs)
        takes_here = jnp.where(col_here % 2 == 0, takes[0], takes[1]) & (col_here > 0)
        return jnp.where(takes_here, got, value), got

    workers = [r for r in range(n_row) if r & APART == 0]
    targets = workers[2:] + workers[1:2]
    square, partner = terms, terms
    near_upper = column_upper
    for index, target in enumerate(targets):
        served = [0, targets[-1]] if index == 0 else [targets[index - 1]]
        pairs = [((0, 0), (target, 0))] + [((r + APART, 0), (r, 0)) for r in served]
        if index == 0:
            passed, got = upper_step(upper, 0, pairs)
        else:
            got = send(upper, pairs)
        square = jnp.where(row_here == target, got, square)
        for r in served:
            partner = jnp.where(row_here == r, got, partner)
    upper, column_upper = lax.optimization_barrier((passed, column_upper))
    for target in reversed(workers[1:]):
        got = send(column_upper, [((0, 0), (target, 0))])
        near_upper = jnp.where(row_here == target, got, near_upper)
    upper, _ = upper_step(upper, 1)

    def compute(square, partner):
        columns = jnp.concatenate([pivot_columns, summed(partner)], axis=0)
        both = multipliers(summed(square), columns)
        both = both.astype(jnp.bfloat16)
        return both[:NB], both[NB:]

    def none(square, partner):
        zero = jnp.zeros((NB, NB), jnp.bfloat16)
        return zero, zero

    working = (row_here & APART == 0) & (col_here == 0)
    lower, lower_far = lax.cond(working, compute, none, square, partner)
    received = lower
    for c in range(2, n_col, 2):
        got = send(lower_far, [((r, 0), (r + APART, c)) for r in workers])
        received = jnp.where((row_here & APART != 0) & (col_here == c), got, received)
    got = send(lower_far, [((r, 0), (r + APART, 0)) for r in workers])
    received = jnp.where((row_here & APART != 0) & (col_here == 0), got, received)
    for c in range(2, n_col, 2):
        got = send(lower, [((r, 0), (r, c)) for r in targets])
        received = jnp.where((row_here & APART == 0) & (col_here == c), got, received)
    near_sent, _ = lax.optimization_barrier((near_upper, lower))
    got = send(near_sent, [((r, 0), (r + APART, 0)) for r in workers])
    near_upper = jnp.where(row_here & APART == 0, near_upper, got)
    for step in range(2, len(down)):
        upper, _ = upper_step(upper, step)
    got = send(
        received, [((r, c), (r, c + 1)) for r in range(1, n_row) for c in range(0, n_col, 2)]
    )
    received = jnp.where(col_here % 2 == 0, received, got)
    received = jnp.where(row_here == 0, jnp.zeros_like(received), received)

    column_upper = jnp.concatenate([jnp.zeros((NB, NB), jnp.bfloat16), near_upper], axis=1)
    upper = jnp.where(col_here == 0, column_upper, upper)
    return matrix - jnp.dot(received, upper, preferred_element_type=jnp.float32)


def solution(mesh):
    return jax.shard_map(
        shards,
        mesh=mesh,
        in_specs=(P("row", "col"),),
        out_specs=P("row", "col"),
        check_vma=False,
    )
```

```python
import jax
import jax.numpy as jnp
from jax import lax
from jax.sharding import PartitionSpec as P

NB = 256
HIGH = lax.Precision.HIGH
APART = 2


def strides(size):
    out, stride = [], size // 2
    while stride:
        out.append(stride)
        stride //= 2
    return out


def multipliers(square, columns):
    identity = jnp.eye(NB, dtype=jnp.float32)
    diagonal = square * identity
    across = 1.0 / jnp.sum(diagonal, axis=0, keepdims=True)
    down = 1.0 / jnp.sum(diagonal, axis=1, keepdims=True)
    approx = down * (2.0 * identity - square * across)
    product = jnp.dot(jnp.concatenate([square, columns], axis=0), approx, precision=HIGH)
    return jnp.dot(product[NB:], 2.0 * identity - product[:NB], precision=HIGH)


def shards(matrix):
    rows_dev, cols_dev = matrix.shape
    assert rows_dev == NB
    n_row, n_col = lax.axis_size("row"), lax.axis_size("col")
    row_here, col_here = lax.axis_index("row"), lax.axis_index("col")

    def send(value, pairs):
        flat = [(r0 * n_col + c0, r1 * n_col + c1) for (r0, c0), (r1, c1) in pairs]
        return lax.ppermute(value, ("row", "col"), flat)

    upper = matrix.astype(jnp.bfloat16)
    pivot_columns, column_upper = matrix[:, :NB], upper[:, NB:]

    down = strides(n_row)
    orders = [down, [down[-1]] + down[:-1]]
    held = [[0], [0]]

    def upper_step(value, step):
        pairs = []
        takes = []
        for kind in range(2):
            stride = orders[kind][step]
            missing = sum(orders[kind][step + 1 :])
            takes.append((row_here & (stride | missing)) == stride)
            pairs += [
                ((h, c), (h + stride, c)) for h in held[kind] for c in range(1, n_col) if c % 2 == kind
            ]
            held[kind] = held[kind] + [h + stride for h in held[kind]]
        got = send(value, pairs)
        return jnp.where(jnp.where(col_here % 2 == 0, takes[0], takes[1]), got, value)

    workers = [r for r in range(n_row) if r & APART == 0]
    targets = workers[2:] + workers[1:2]
    square, partner = pivot_columns, pivot_columns
    near_upper = column_upper
    upper, column_upper = lax.optimization_barrier((upper_step(upper, 0), column_upper))
    for index, target in enumerate(targets):
        served = [0, targets[-1]] if index == 0 else [targets[index - 1]]
        pairs = [((0, 0), (target, 0))] + [((r + APART, 0), (r, 0)) for r in served]
        got = send(pivot_columns, pairs)
        square = jnp.where(row_here == target, got, square)
        for r in served:
            partner = jnp.where(row_here == r, got, partner)
    for target in reversed(workers[1:]):
        got = send(column_upper, [((0, 0), (target, 0))])
        near_upper = jnp.where(row_here == target, got, near_upper)
    upper = upper_step(upper, 1)

    def compute(square, partner):
        both = multipliers(square, jnp.concatenate([pivot_columns, partner], axis=0))
        both = both.astype(jnp.bfloat16)
        return both[:NB], both[NB:]

    def none(square, partner):
        zero = jnp.zeros((NB, NB), jnp.bfloat16)
        return zero, zero

    working = (row_here & APART == 0) & (col_here == 0)
    lower, lower_far = lax.cond(working, compute, none, square, partner)
    received = lower
    for c in range(2, n_col, 2):
        got = send(lower_far, [((r, 0), (r + APART, c)) for r in workers])
        received = jnp.where((row_here & APART != 0) & (col_here == c), got, received)
    got = send(lower_far, [((r, 0), (r + APART, 0)) for r in workers])
    received = jnp.where((row_here & APART != 0) & (col_here == 0), got, received)
    for c in range(2, n_col, 2):
        got = send(lower, [((r, 0), (r, c)) for r in targets])
        received = jnp.where((row_here & APART == 0) & (col_here == c), got, received)
    near_sent, _ = lax.optimization_barrier((near_upper, lower))
    got = send(near_sent, [((r, 0), (r + APART, 0)) for r in workers])
    near_upper = jnp.where(row_here & APART == 0, near_upper, got)
    for step in range(2, len(down)):
        upper = upper_step(upper, step)
    got = send(
        received, [((r, c), (r, c + 1)) for r in range(1, n_row) for c in range(0, n_col, 2)]
    )
    received = jnp.where(col_here % 2 == 0, received, got)
    received = jnp.where(row_here == 0, jnp.zeros_like(received), received)

    column_upper = jnp.concatenate([jnp.zeros((NB, NB), jnp.bfloat16), near_upper], axis=1)
    upper = jnp.where(col_here == 0, column_upper, upper)
    return matrix - jnp.dot(received, upper, preferred_element_type=jnp.float32)


def solution(mesh):
    return jax.shard_map(
        shards,
        mesh=mesh,
        in_specs=(P("row", "col"),),
        out_specs=P("row", "col"),
        check_vma=False,
    )
```

```python
import jax
import jax.numpy as jnp
from jax import lax
from jax.sharding import PartitionSpec as P

NB = 256
HIGH = lax.Precision.HIGH
APART = 2


def strides(size):
    out, stride = [], size // 2
    while stride:
        out.append(stride)
        stride //= 2
    return out


def multipliers(square, columns):
    identity = jnp.eye(NB, dtype=jnp.float32)
    diagonal = square * identity
    across = 1.0 / jnp.sum(diagonal, axis=0, keepdims=True)
    down = 1.0 / jnp.sum(diagonal, axis=1, keepdims=True)
    approx = down * (2.0 * identity - square * across)
    product = jnp.dot(jnp.concatenate([square, columns], axis=0), approx, precision=HIGH)
    return jnp.dot(product[NB:], 2.0 * identity - product[:NB], precision=HIGH)


def shards(matrix):
    rows_dev, cols_dev = matrix.shape
    assert rows_dev == NB
    n_row, n_col = lax.axis_size("row"), lax.axis_size("col")
    row_here, col_here = lax.axis_index("row"), lax.axis_index("col")

    def send(value, pairs):
        flat = [(r0 * n_col + c0, r1 * n_col + c1) for (r0, c0), (r1, c1) in pairs]
        return lax.ppermute(value, ("row", "col"), flat)

    upper = matrix.astype(jnp.bfloat16)
    pivot_columns, column_upper = matrix[:, :NB], upper[:, NB:]

    down = strides(n_row)
    orders = [down, [down[-1]] + down[:-1]]
    held = [[0], [0]]

    def upper_step(value, step):
        pairs = []
        takes = []
        for kind in range(2):
            stride = orders[kind][step]
            missing = sum(orders[kind][step + 1 :])
            takes.append((row_here & (stride | missing)) == stride)
            pairs += [
                ((h, c), (h + stride, c)) for h in held[kind] for c in range(1, n_col) if c % 2 == kind
            ]
            held[kind] = held[kind] + [h + stride for h in held[kind]]
        got = send(value, pairs)
        return jnp.where(jnp.where(col_here % 2 == 0, takes[0], takes[1]), got, value)

    workers = [r for r in range(n_row) if r & APART == 0]
    targets = workers[2:] + workers[1:2]
    square, partner = pivot_columns, pivot_columns
    near_upper = column_upper
    upper, column_upper = lax.optimization_barrier((upper_step(upper, 0), column_upper))
    for index, target in enumerate(targets):
        served = [0, targets[-1]] if index == 0 else [targets[index - 1]]
        pairs = [((0, 0), (target, 0))] + [((r + APART, 0), (r, 0)) for r in served]
        got = send(pivot_columns, pairs)
        square = jnp.where(row_here == target, got, square)
        for r in served:
            partner = jnp.where(row_here == r, got, partner)
    beside = send(column_upper, [((0, 0), (0, 1))])
    for target in workers[1:]:
        got = send(beside, [((0, 1), (target, 0))])
        near_upper = jnp.where(row_here == target, got, near_upper)
    upper = upper_step(upper, 1)

    def compute(square, partner):
        both = multipliers(square, jnp.concatenate([pivot_columns, partner], axis=0))
        both = both.astype(jnp.bfloat16)
        return both[:NB], both[NB:]

    def none(square, partner):
        zero = jnp.zeros((NB, NB), jnp.bfloat16)
        return zero, zero

    working = (row_here & APART == 0) & (col_here == 0)
    lower, lower_far = lax.cond(working, compute, none, square, partner)
    received = lower
    for c in range(2, n_col, 2):
        got = send(lower_far, [((r, 0), (r + APART, c)) for r in workers])
        received = jnp.where((row_here & APART != 0) & (col_here == c), got, received)
    got = send(lower_far, [((r, 0), (r + APART, 0)) for r in workers])
    received = jnp.where((row_here & APART != 0) & (col_here == 0), got, received)
    for c in range(2, n_col, 2):
        got = send(lower, [((r, 0), (r, c)) for r in targets])
        received = jnp.where((row_here & APART == 0) & (col_here == c), got, received)
    near_sent, _ = lax.optimization_barrier((near_upper, lower))
    got = send(near_sent, [((r, 0), (r + APART, 0)) for r in workers])
    near_upper = jnp.where(row_here & APART == 0, near_upper, got)
    for step in range(2, len(down)):
        upper = upper_step(upper, step)
    got = send(
        received, [((r, c), (r, c + 1)) for r in range(1, n_row) for c in range(0, n_col, 2)]
    )
    received = jnp.where(col_here % 2 == 0, received, got)
    received = jnp.where(row_here == 0, jnp.zeros_like(received), received)

    column_upper = jnp.concatenate([jnp.zeros((NB, NB), jnp.bfloat16), near_upper], axis=1)
    upper = jnp.where(col_here == 0, column_upper, upper)
    return matrix - jnp.dot(received, upper, preferred_element_type=jnp.float32)


def solution(mesh):
    return jax.shard_map(
        shards,
        mesh=mesh,
        in_specs=(P("row", "col"),),
        out_specs=P("row", "col"),
        check_vma=False,
    )
```

```python
import jax
import jax.numpy as jnp
from jax import lax
from jax.sharding import PartitionSpec as P

NB = 256
HIGH = lax.Precision.HIGH
APART = 2


def strides(size):
    out, stride = [], size // 2
    while stride:
        out.append(stride)
        stride //= 2
    return out


def multipliers(square, columns):
    identity = jnp.eye(NB, dtype=jnp.float32)
    diagonal = square * identity
    across = 1.0 / jnp.sum(diagonal, axis=0, keepdims=True)
    down = 1.0 / jnp.sum(diagonal, axis=1, keepdims=True)
    approx = down * (2.0 * identity - square * across)
    product = jnp.dot(jnp.concatenate([square, columns], axis=0), approx, precision=HIGH)
    return jnp.dot(product[NB:], 2.0 * identity - product[:NB], precision=HIGH)


def shards(matrix):
    rows_dev, cols_dev = matrix.shape
    assert rows_dev == NB
    n_row, n_col = lax.axis_size("row"), lax.axis_size("col")
    row_here, col_here = lax.axis_index("row"), lax.axis_index("col")

    def send(value, pairs):
        flat = [(r0 * n_col + c0, r1 * n_col + c1) for (r0, c0), (r1, c1) in pairs]
        return lax.ppermute(value, ("row", "col"), flat)

    upper = matrix.astype(jnp.bfloat16)
    pivot_columns, column_upper = matrix[:, :NB], upper[:, NB:]

    down = strides(n_row)
    orders = [down, [down[-1]] + down[:-1]]
    held = [[0], [0]]

    def upper_step(value, step):
        pairs = []
        takes = []
        for kind in range(2):
            stride = orders[kind][step]
            missing = sum(orders[kind][step + 1 :])
            takes.append((row_here & (stride | missing)) == stride)
            pairs += [
                ((h, c), (h + stride, c)) for h in held[kind] for c in range(1, n_col) if c % 2 == kind
            ]
            held[kind] = held[kind] + [h + stride for h in held[kind]]
        got = send(value, pairs)
        return jnp.where(jnp.where(col_here % 2 == 0, takes[0], takes[1]), got, value)

    workers = [r for r in range(n_row) if r & APART == 0]
    targets = workers[2:] + workers[1:2]
    square, partner = pivot_columns, pivot_columns
    near_upper = column_upper
    upper, column_upper = lax.optimization_barrier((upper_step(upper, 0), column_upper))
    for index, target in enumerate(targets):
        served = [0, targets[-1]] if index == 0 else [targets[index - 1]]
        pairs = [((0, 0), (target, 0))] + [((r + APART, 0), (r, 0)) for r in served]
        got = send(pivot_columns, pairs)
        square = jnp.where(row_here == target, got, square)
        for r in served:
            partner = jnp.where(row_here == r, got, partner)
    for target in workers[1:]:
        got = send(column_upper, [((0, 0), (target, 0))])
        near_upper = jnp.where(row_here == target, got, near_upper)

    def compute(square, partner):
        both = multipliers(square, jnp.concatenate([pivot_columns, partner], axis=0))
        both = both.astype(jnp.bfloat16)
        return both[:NB], both[NB:]

    def none(square, partner):
        zero = jnp.zeros((NB, NB), jnp.bfloat16)
        return zero, zero

    working = (row_here & APART == 0) & (col_here == 0)
    lower, lower_far = lax.cond(working, compute, none, square, partner)
    received = lower
    for c in range(2, n_col, 2):
        got = send(lower_far, [((r, 0), (r + APART, c)) for r in workers])
        received = jnp.where((row_here & APART != 0) & (col_here == c), got, received)
    got = send(lower_far, [((r, 0), (r + APART, 0)) for r in workers])
    received = jnp.where((row_here & APART != 0) & (col_here == 0), got, received)
    for c in range(2, n_col, 2):
        got = send(lower, [((r, 0), (r, c)) for r in targets])
        received = jnp.where((row_here & APART == 0) & (col_here == c), got, received)
    near_sent, _ = lax.optimization_barrier((near_upper, lower))
    got = send(near_sent, [((r, 0), (r + APART, 0)) for r in workers])
    near_upper = jnp.where(row_here & APART == 0, near_upper, got)
    upper, _ = lax.optimization_barrier((upper, lower))
    for step in range(1, len(down)):
        upper = upper_step(upper, step)
    got = send(
        received, [((r, c), (r, c + 1)) for r in range(1, n_row) for c in range(0, n_col, 2)]
    )
    received = jnp.where(col_here % 2 == 0, received, got)
    received = jnp.where(row_here == 0, jnp.zeros_like(received), received)

    column_upper = jnp.concatenate([jnp.zeros((NB, NB), jnp.bfloat16), near_upper], axis=1)
    upper = jnp.where(col_here == 0, column_upper, upper)
    return matrix - jnp.dot(received, upper, preferred_element_type=jnp.float32)


def solution(mesh):
    return jax.shard_map(
        shards,
        mesh=mesh,
        in_specs=(P("row", "col"),),
        out_specs=P("row", "col"),
        check_vma=False,
    )
```

```python
import jax
import jax.numpy as jnp
from jax import lax
from jax.sharding import PartitionSpec as P

NB = 256
HIGH = lax.Precision.HIGH
APART = 2


def strides(size):
    out, stride = [], size // 2
    while stride:
        out.append(stride)
        stride //= 2
    return out


def multipliers(square, columns):
    identity = jnp.eye(NB, dtype=jnp.float32)
    diagonal = square * identity
    across = 1.0 / jnp.sum(diagonal, axis=0, keepdims=True)
    down = 1.0 / jnp.sum(diagonal, axis=1, keepdims=True)
    approx = down * (2.0 * identity - square * across)
    product = jnp.dot(jnp.concatenate([square, columns], axis=0), approx, precision=HIGH)
    return jnp.dot(product[NB:], 2.0 * identity - product[:NB], precision=HIGH)


def shards(matrix):
    rows_dev, cols_dev = matrix.shape
    assert rows_dev == NB
    n_row, n_col = lax.axis_size("row"), lax.axis_size("col")
    row_here, col_here = lax.axis_index("row"), lax.axis_index("col")

    def send(value, pairs):
        flat = [(r0 * n_col + c0, r1 * n_col + c1) for (r0, c0), (r1, c1) in pairs]
        return lax.ppermute(value, ("row", "col"), flat)

    def blocks(matrix):
        return matrix[:, :NB], matrix.astype(jnp.bfloat16)

    def no_blocks(matrix):
        return jnp.zeros((NB, NB), matrix.dtype), jnp.zeros(matrix.shape, jnp.bfloat16)

    sends_columns = (col_here == 0) & (row_here & APART != 0)
    pivot_columns, upper = lax.cond(
        sends_columns | (row_here == 0), blocks, no_blocks, matrix
    )
    column_upper = upper[:, NB:]

    down = strides(n_row)
    orders = [down, [down[-1]] + down[:-1]]
    held = [[0], [0]]

    def upper_step(value, step):
        pairs = []
        takes = []
        for kind in range(2):
            stride = orders[kind][step]
            missing = sum(orders[kind][step + 1 :])
            takes.append((row_here & (stride | missing)) == stride)
            pairs += [
                ((h, c), (h + stride, c)) for h in held[kind] for c in range(1, n_col) if c % 2 == kind
            ]
            held[kind] = held[kind] + [h + stride for h in held[kind]]
        got = send(value, pairs)
        return jnp.where(jnp.where(col_here % 2 == 0, takes[0], takes[1]), got, value)

    workers = [r for r in range(n_row) if r & APART == 0]
    targets = workers[1:]
    square, partner = pivot_columns, pivot_columns
    near_upper = column_upper
    upper, column_upper = lax.optimization_barrier((upper_step(upper, 0), column_upper))
    for index, target in reversed(list(enumerate(targets))):
        served = [0, targets[-1]] if index == 0 else [targets[index - 1]]
        pairs = [((0, 0), (target, 0))] + [((r + APART, 0), (r, 0)) for r in served]
        got = send(pivot_columns, pairs)
        square = jnp.where(row_here == target, got, square)
        for r in served:
            partner = jnp.where(row_here == r, got, partner)
    for target in reversed(workers[1:]):
        got = send(column_upper, [((0, 0), (target, 0))])
        near_upper = jnp.where(row_here == target, got, near_upper)
    upper = upper_step(upper, 1)

    def compute(square, partner):
        both = multipliers(square, jnp.concatenate([matrix[:, :NB], partner], axis=0))
        both = both.astype(jnp.bfloat16)
        return both[:NB], both[NB:]

    def none(square, partner):
        zero = jnp.zeros((NB, NB), jnp.bfloat16)
        return zero, zero

    working = (row_here & APART == 0) & (col_here == 0)
    lower, lower_far = lax.cond(working, compute, none, square, partner)
    received = lower
    for c in range(2, n_col, 2):
        got = send(lower_far, [((r, 0), (r + APART, c)) for r in workers])
        received = jnp.where((row_here & APART != 0) & (col_here == c), got, received)
    got = send(lower_far, [((r, 0), (r + APART, 0)) for r in workers])
    received = jnp.where((row_here & APART != 0) & (col_here == 0), got, received)
    for c in range(2, n_col, 2):
        got = send(lower, [((r, 0), (r, c)) for r in targets])
        received = jnp.where((row_here & APART == 0) & (col_here == c), got, received)
    near_sent, _ = lax.optimization_barrier((near_upper, lower))
    got = send(near_sent, [((r, 0), (r + APART, 0)) for r in workers])
    near_upper = jnp.where(row_here & APART == 0, near_upper, got)
    for step in range(2, len(down)):
        upper = upper_step(upper, step)
    got = send(
        received, [((r, c), (r, c + 1)) for r in range(1, n_row) for c in range(0, n_col, 2)]
    )
    received = jnp.where(col_here % 2 == 0, received, got)
    received = jnp.where(row_here == 0, jnp.zeros_like(received), received)

    column_upper = jnp.concatenate([jnp.zeros((NB, NB), jnp.bfloat16), near_upper], axis=1)
    upper = jnp.where(col_here == 0, column_upper, upper)
    return matrix - jnp.dot(received, upper, preferred_element_type=jnp.float32)


def solution(mesh):
    return jax.shard_map(
        shards,
        mesh=mesh,
        in_specs=(P("row", "col"),),
        out_specs=P("row", "col"),
        check_vma=False,
    )
```

```python
import jax
import jax.numpy as jnp
from jax import lax
from jax.sharding import PartitionSpec as P

NB = 256
HIGH = lax.Precision.HIGH
APART = 2


def strides(size):
    out, stride = [], size // 2
    while stride:
        out.append(stride)
        stride //= 2
    return out


def multipliers(square, columns):
    identity = jnp.eye(NB, dtype=jnp.float32)
    diagonal = square * identity
    across = 1.0 / jnp.sum(diagonal, axis=0, keepdims=True)
    down = 1.0 / jnp.sum(diagonal, axis=1, keepdims=True)
    approx = down * (2.0 * identity - square * across)
    product = jnp.dot(jnp.concatenate([square, columns], axis=0), approx, precision=HIGH)
    return jnp.dot(product[NB:], 2.0 * identity - product[:NB], precision=HIGH)


def shards(matrix):
    rows_dev, cols_dev = matrix.shape
    assert rows_dev == NB
    n_row, n_col = lax.axis_size("row"), lax.axis_size("col")
    row_here, col_here = lax.axis_index("row"), lax.axis_index("col")

    def send(value, pairs):
        flat = [(r0 * n_col + c0, r1 * n_col + c1) for (r0, c0), (r1, c1) in pairs]
        return lax.ppermute(value, ("row", "col"), flat)

    def blocks(matrix):
        return matrix[:, :NB], matrix.astype(jnp.bfloat16)

    def no_blocks(matrix):
        return jnp.zeros((NB, NB), matrix.dtype), jnp.zeros(matrix.shape, jnp.bfloat16)

    sends_columns = (col_here == 0) & (row_here & APART != 0)
    pivot_columns, first_upper = lax.cond(
        sends_columns | (row_here == 0), blocks, no_blocks, matrix
    )
    upper = matrix.astype(jnp.bfloat16)
    column_upper = upper[:, NB:]

    down = strides(n_row)
    orders = [down, [down[-1]] + down[:-1]]
    held = [[0], [0]]

    def upper_step(value, step, sent):
        pairs = []
        takes = []
        for kind in range(2):
            stride = orders[kind][step]
            missing = sum(orders[kind][step + 1 :])
            takes.append((row_here & (stride | missing)) == stride)
            pairs += [
                ((h, c), (h + stride, c)) for h in held[kind] for c in range(1, n_col) if c % 2 == kind
            ]
            held[kind] = held[kind] + [h + stride for h in held[kind]]
        got = send(sent, pairs)
        return jnp.where(jnp.where(col_here % 2 == 0, takes[0], takes[1]), got, value)

    workers = [r for r in range(n_row) if r & APART == 0]
    targets = workers[1:]
    square, partner = matrix[:, :NB], matrix[:, :NB]
    near_upper = column_upper
    upper, column_upper = lax.optimization_barrier((upper_step(upper, 0, first_upper), column_upper))
    for index, target in reversed(list(enumerate(targets))):
        served = [0, targets[-1]] if index == 0 else [targets[index - 1]]
        pairs = [((0, 0), (target, 0))] + [((r + APART, 0), (r, 0)) for r in served]
        got = send(pivot_columns, pairs)
        square = jnp.where(row_here == target, got, square)
        for r in served:
            partner = jnp.where(row_here == r, got, partner)
    for target in reversed(workers[1:]):
        got = send(column_upper, [((0, 0), (target, 0))])
        near_upper = jnp.where(row_here == target, got, near_upper)
    upper = upper_step(upper, 1, upper)

    def compute(square, partner):
        both = multipliers(square, jnp.concatenate([matrix[:, :NB], partner], axis=0))
        both = both.astype(jnp.bfloat16)
        return both[:NB], both[NB:]

    def none(square, partner):
        zero = jnp.zeros((NB, NB), jnp.bfloat16)
        return zero, zero

    working = (row_here & APART == 0) & (col_here == 0)
    lower, lower_far = lax.cond(working, compute, none, square, partner)
    received = lower
    for c in range(2, n_col, 2):
        got = send(lower_far, [((r, 0), (r + APART, c)) for r in workers])
        received = jnp.where((row_here & APART != 0) & (col_here == c), got, received)
    got = send(lower_far, [((r, 0), (r + APART, 0)) for r in workers])
    received = jnp.where((row_here & APART != 0) & (col_here == 0), got, received)
    for c in range(2, n_col, 2):
        got = send(lower, [((r, 0), (r, c)) for r in targets])
        received = jnp.where((row_here & APART == 0) & (col_here == c), got, received)
    near_sent, _ = lax.optimization_barrier((near_upper, lower))
    got = send(near_sent, [((r, 0), (r + APART, 0)) for r in workers])
    near_upper = jnp.where(row_here & APART == 0, near_upper, got)
    for step in range(2, len(down)):
        upper = upper_step(upper, step, upper)
    got = send(
        received, [((r, c), (r, c + 1)) for r in range(1, n_row) for c in range(0, n_col, 2)]
    )
    received = jnp.where(col_here % 2 == 0, received, got)
    received = jnp.where(row_here == 0, jnp.zeros_like(received), received)

    column_upper = jnp.concatenate([jnp.zeros((NB, NB), jnp.bfloat16), near_upper], axis=1)
    upper = jnp.where(col_here == 0, column_upper, upper)
    return matrix - jnp.dot(received, upper, preferred_element_type=jnp.float32)


def solution(mesh):
    return jax.shard_map(
        shards,
        mesh=mesh,
        in_specs=(P("row", "col"),),
        out_specs=P("row", "col"),
        check_vma=False,
    )
```

```python
import jax
import jax.numpy as jnp
from jax import lax
from jax.sharding import PartitionSpec as P

NB = 256
HIGH = lax.Precision.HIGH
APART = 2


def strides(size):
    out, stride = [], size // 2
    while stride:
        out.append(stride)
        stride //= 2
    return out


def multipliers(square, columns):
    identity = jnp.eye(NB, dtype=jnp.float32)
    diagonal = square * identity
    across = 1.0 / jnp.sum(diagonal, axis=0, keepdims=True)
    down = 1.0 / jnp.sum(diagonal, axis=1, keepdims=True)
    approx = down * (2.0 * identity - square * across)
    product = jnp.dot(jnp.concatenate([square, columns], axis=0), approx, precision=HIGH)
    return jnp.dot(product[NB:], 2.0 * identity - product[:NB], precision=HIGH)


def shards(matrix):
    rows_dev, cols_dev = matrix.shape
    assert rows_dev == NB
    n_row, n_col = lax.axis_size("row"), lax.axis_size("col")
    row_here, col_here = lax.axis_index("row"), lax.axis_index("col")

    def send(value, pairs):
        flat = [(r0 * n_col + c0, r1 * n_col + c1) for (r0, c0), (r1, c1) in pairs]
        return lax.ppermute(value, ("row", "col"), flat)

    def blocks(matrix):
        return matrix[:, :NB], matrix.astype(jnp.bfloat16)

    def no_blocks(matrix):
        return jnp.zeros((NB, NB), matrix.dtype), jnp.zeros(matrix.shape, jnp.bfloat16)

    sends_columns = (col_here == 0) & (row_here & APART != 0)
    pivot_columns, first_upper = lax.cond(
        sends_columns | (row_here == 0), blocks, no_blocks, matrix
    )
    upper = lax.optimization_barrier(jnp.where(row_here == 0, first_upper, 0))

    down = strides(n_row)
    orders = [down, [down[-1]] + down[:-1]]
    held = [[0], [0]]

    def upper_step(value, step, sent, pairs=()):
        pairs = list(pairs)
        takes = []
        for kind in range(2):
            stride = orders[kind][step]
            missing = sum(orders[kind][step + 1 :])
            takes.append((row_here & (stride | missing)) == stride)
            pairs += [
                ((h, c), (h + stride, c)) for h in held[kind] for c in range(1, n_col) if c % 2 == kind
            ]
            held[kind] = held[kind] + [h + stride for h in held[kind]]
        got = send(sent, pairs)
        return jnp.where(jnp.where(col_here % 2 == 0, takes[0], takes[1]), got, value), got

    workers = [r for r in range(n_row) if r & APART == 0]
    targets = workers[2:] + workers[1:2]
    square, partner = matrix[:, :NB], matrix[:, :NB]
    passed, got = upper_step(upper, 0, first_upper, [((0, 0), (1, 0))])
    near_upper = jnp.where(row_here == 1, got[:, NB:], upper[:, NB:])
    upper = passed
    for index, target in reversed(list(enumerate(targets))):
        served = [0, targets[-1]] if index == 0 else [targets[index - 1]]
        pairs = [((0, 0), (target, 0))] + [((r + APART, 0), (r, 0)) for r in served]
        got = send(pivot_columns, pairs)
        square = jnp.where(row_here == target, got, square)
        for r in served:
            partner = jnp.where(row_here == r, got, partner)
    near_sent = near_upper
    for target in reversed(targets[:-1]):
        pairs = [((1, 0), (target, 0))]
        takes = row_here == target
        if target == targets[-2]:
            pairs += [((0, 0), (APART, 0))]
            takes = takes | (row_here == APART)
        got = send(near_sent, pairs)
        near_upper = jnp.where(takes, got, near_upper)
    upper, _ = upper_step(upper, 1, upper)

    def compute(square, partner):
        both = multipliers(square, jnp.concatenate([matrix[:, :NB], partner], axis=0))
        both = both.astype(jnp.bfloat16)
        return both[:NB], both[NB:]

    def none(square, partner):
        zero = jnp.zeros((NB, NB), jnp.bfloat16)
        return zero, zero

    working = (row_here & APART == 0) & (col_here == 0)
    lower, lower_far = lax.cond(working, compute, none, square, partner)
    received = lower
    for c in range(2, n_col, 2):
        got = send(lower_far, [((r, 0), (r + APART, c)) for r in workers])
        received = jnp.where((row_here & APART != 0) & (col_here == c), got, received)
    got = send(lower_far, [((r, 0), (r + APART, 0)) for r in workers])
    received = jnp.where((row_here & APART != 0) & (col_here == 0), got, received)
    for c in range(2, n_col, 2):
        got = send(lower, [((r, 0), (r, c)) for r in targets])
        received = jnp.where((row_here & APART == 0) & (col_here == c), got, received)
    near_sent, _ = lax.optimization_barrier((near_upper, lower))
    got = send(near_sent, [((r, 0), (r + APART, 0)) for r in workers[1:]])
    near_upper = jnp.where((row_here & APART != 0) & (row_here != APART), got, near_upper)
    for step in range(2, len(down)):
        upper, _ = upper_step(upper, step, upper)
    got = send(
        received, [((r, c), (r, c + 1)) for r in range(1, n_row) for c in range(0, n_col, 2)]
    )
    received = jnp.where(col_here % 2 == 0, received, got)
    received = jnp.where(row_here == 0, jnp.zeros_like(received), received)

    column_upper = jnp.concatenate([jnp.zeros((NB, NB), jnp.bfloat16), near_upper], axis=1)
    upper = jnp.where(col_here == 0, column_upper, upper)
    return matrix - jnp.dot(received, upper, preferred_element_type=jnp.float32)


def solution(mesh):
    return jax.shard_map(
        shards,
        mesh=mesh,
        in_specs=(P("row", "col"),),
        out_specs=P("row", "col"),
        check_vma=False,
    )
```

```python
import jax
import jax.numpy as jnp
from jax import lax
from jax.sharding import PartitionSpec as P

NB = 256
HIGH = lax.Precision.HIGH
APART = 2


def strides(size):
    out, stride = [], size // 2
    while stride:
        out.append(stride)
        stride //= 2
    return out


def two_terms(values, width):
    high = lax.reduce_precision(values, exponent_bits=8, mantissa_bits=7)
    terms = [high.astype(jnp.bfloat16), (values - high).astype(jnp.bfloat16)]
    both = jnp.concatenate(terms, axis=1)
    return jnp.pad(both, ((0, 0), (0, width - both.shape[1])))


def summed(terms):
    return terms[:, :NB].astype(jnp.float32) + terms[:, NB : 2 * NB].astype(jnp.float32)


def multipliers(square, columns):
    identity = jnp.eye(NB, dtype=jnp.float32)
    diagonal = square * identity
    across = 1.0 / jnp.sum(diagonal, axis=0, keepdims=True)
    down = 1.0 / jnp.sum(diagonal, axis=1, keepdims=True)
    approx = down * (2.0 * identity - square * across)
    product = jnp.dot(jnp.concatenate([square, columns], axis=0), approx, precision=HIGH)
    return jnp.dot(product[NB:], 2.0 * identity - product[:NB], precision=HIGH)


def shards(matrix):
    rows_dev, cols_dev = matrix.shape
    assert rows_dev == NB
    n_row, n_col = lax.axis_size("row"), lax.axis_size("col")
    row_here, col_here = lax.axis_index("row"), lax.axis_index("col")

    def send(value, pairs):
        flat = [(r0 * n_col + c0, r1 * n_col + c1) for (r0, c0), (r1, c1) in pairs]
        return lax.ppermute(value, ("row", "col"), flat)

    def blocks(matrix):
        rows = matrix.astype(jnp.bfloat16)
        return jnp.where(col_here == 0, two_terms(matrix[:, :NB], cols_dev), rows), rows[:, NB:]

    def no_blocks(matrix):
        return jnp.zeros(matrix.shape, jnp.bfloat16), jnp.zeros(
            (rows_dev, cols_dev - NB), jnp.bfloat16
        )

    sends_columns = (col_here == 0) & (row_here & APART != 0)
    first_sent, column_upper = lax.cond(
        sends_columns | (row_here == 0), blocks, no_blocks, matrix
    )
    upper = lax.optimization_barrier(jnp.where(row_here == 0, first_sent, 0))

    down = strides(n_row)
    orders = [down, [down[-1]] + down[:-1]]
    held = [[0], [0]]

    def upper_step(value, step, sent, pairs=()):
        pairs = list(pairs)
        takes = []
        for kind in range(2):
            stride = orders[kind][step]
            missing = sum(orders[kind][step + 1 :])
            takes.append((row_here & (stride | missing)) == stride)
            pairs += [
                ((h, c), (h + stride, c)) for h in held[kind] for c in range(1, n_col) if c % 2 == kind
            ]
            held[kind] = held[kind] + [h + stride for h in held[kind]]
        got = send(sent, pairs)
        return jnp.where(jnp.where(col_here % 2 == 0, takes[0], takes[1]), got, value), got

    workers = [r for r in range(n_row) if r & APART == 0]
    targets = workers[2:] + workers[1:2]
    square = partner = first_sent
    for index, target in reversed(list(enumerate(targets))):
        served = [0, targets[-1]] if index == 0 else [targets[index - 1]]
        pairs = [((0, 0), (target, 0))] + [((r + APART, 0), (r, 0)) for r in served]
        if index == 0:
            upper, got = upper_step(upper, 0, first_sent, pairs)
        else:
            got = send(first_sent, pairs)
        square = jnp.where(row_here == target, got, square)
        for r in served:
            partner = jnp.where(row_here == r, got, partner)

    got = send(column_upper, [((0, 0), (1, 0))])
    near_upper = jnp.where(row_here == 1, got, column_upper)
    near_sent = near_upper
    for target in reversed(targets[1:-1]):
        pairs = [((1, 0), (target, 0))]
        takes = row_here == target
        if target == targets[1]:
            pairs += [((0, 0), (targets[0], 0))]
            takes = takes | (row_here == targets[0])
        got = send(near_sent, pairs)
        near_upper = jnp.where(takes, got, near_upper)
    upper, _ = upper_step(upper, 1, upper)

    def compute(square, partner):
        columns = jnp.concatenate([matrix[:, :NB], summed(partner)], axis=0)
        both = multipliers(summed(square), columns)
        both = both.astype(jnp.bfloat16)
        return both[:NB], both[NB:]

    def none(square, partner):
        zero = jnp.zeros((NB, NB), jnp.bfloat16)
        return zero, zero

    working = (row_here & APART == 0) & (col_here == 0)
    lower, lower_far = lax.cond(working, compute, none, square, partner)
    received = lower
    for c in range(2, n_col, 2):
        got = send(lower_far, [((r, 0), (r + APART, c)) for r in workers])
        received = jnp.where((row_here & APART != 0) & (col_here == c), got, received)
    got = send(lower_far, [((r, 0), (r + APART, 0)) for r in workers])
    received = jnp.where((row_here & APART != 0) & (col_here == 0), got, received)
    for c in range(2, n_col, 2):
        got = send(lower, [((r, 0), (r, c)) for r in targets])
        received = jnp.where((row_here & APART == 0) & (col_here == c), got, received)
    near_sent, _ = lax.optimization_barrier((near_upper, lower))
    got = send(near_sent, [((r, 0), (r + APART, 0)) for r in workers])
    near_upper = jnp.where(row_here & APART != 0, got, near_upper)
    for step in range(2, len(down)):
        upper, _ = upper_step(upper, step, upper)
    got = send(
        received, [((r, c), (r, c + 1)) for r in range(1, n_row) for c in range(0, n_col, 2)]
    )
    received = jnp.where(col_here % 2 == 0, received, got)
    received = jnp.where(row_here == 0, jnp.zeros_like(received), received)

    column_upper = jnp.concatenate([jnp.zeros((NB, NB), jnp.bfloat16), near_upper], axis=1)
    upper = jnp.where(col_here == 0, column_upper, upper)
    return matrix - jnp.dot(received, upper, preferred_element_type=jnp.float32)


def solution(mesh):
    return jax.shard_map(
        shards,
        mesh=mesh,
        in_specs=(P("row", "col"),),
        out_specs=P("row", "col"),
        check_vma=False,
    )
```

```python
import jax
import jax.numpy as jnp
from jax import lax
from jax.sharding import PartitionSpec as P

NB = 256
HIGH = lax.Precision.HIGH
APART = 2


def strides(size):
    out, stride = [], size // 2
    while stride:
        out.append(stride)
        stride //= 2
    return out


def two_terms(values, width):
    high = lax.reduce_precision(values, exponent_bits=8, mantissa_bits=7)
    terms = [high.astype(jnp.bfloat16), (values - high).astype(jnp.bfloat16)]
    both = jnp.concatenate(terms, axis=1)
    return jnp.pad(both, ((0, 0), (0, width - both.shape[1])))


def summed(terms):
    return terms[:, :NB].astype(jnp.float32) + terms[:, NB : 2 * NB].astype(jnp.float32)


def multipliers(square, columns):
    identity = jnp.eye(NB, dtype=jnp.float32)
    diagonal = square * identity
    across = 1.0 / jnp.sum(diagonal, axis=0, keepdims=True)
    down = 1.0 / jnp.sum(diagonal, axis=1, keepdims=True)
    approx = down * (2.0 * identity - square * across)
    product = jnp.dot(jnp.concatenate([square, columns], axis=0), approx, precision=HIGH)
    return jnp.dot(product[NB:], 2.0 * identity - product[:NB], precision=HIGH)


def shards(matrix):
    rows_dev, cols_dev = matrix.shape
    assert rows_dev == NB
    n_row, n_col = lax.axis_size("row"), lax.axis_size("col")
    row_here, col_here = lax.axis_index("row"), lax.axis_index("col")

    def send(value, pairs):
        flat = [(r0 * n_col + c0, r1 * n_col + c1) for (r0, c0), (r1, c1) in pairs]
        return lax.ppermute(value, ("row", "col"), flat)

    def blocks(matrix):
        rows = matrix.astype(jnp.bfloat16)
        return jnp.where(col_here == 0, two_terms(matrix[:, :NB], cols_dev), rows), rows[:, NB:]

    def no_blocks(matrix):
        return jnp.zeros(matrix.shape, jnp.bfloat16), jnp.zeros(
            (rows_dev, cols_dev - NB), jnp.bfloat16
        )

    sends_columns = (col_here == 0) & (row_here & APART != 0)
    first_sent, column_upper = lax.cond(
        sends_columns | (row_here == 0), blocks, no_blocks, matrix
    )
    upper = lax.optimization_barrier(jnp.where(row_here == 0, first_sent, 0))

    down = strides(n_row)
    orders = [down, [down[-1]] + down[:-1]]
    held = [[0], [0]]

    def upper_step(value, step, sent, pairs=()):
        pairs = list(pairs)
        takes = []
        for kind in range(2):
            stride = orders[kind][step]
            missing = sum(orders[kind][step + 1 :])
            takes.append((row_here & (stride | missing)) == stride)
            pairs += [
                ((h, c), (h + stride, c)) for h in held[kind] for c in range(1, n_col) if c % 2 == kind
            ]
            held[kind] = held[kind] + [h + stride for h in held[kind]]
        got = send(sent, pairs)
        return jnp.where(jnp.where(col_here % 2 == 0, takes[0], takes[1]), got, value), got

    workers = [r for r in range(n_row) if r & APART == 0]
    targets = workers[:1:-1]
    upper, got = upper_step(upper, 0, first_sent, [((0, 0), (1, 0)), ((APART, 0), (0, 0))])
    square = jnp.where(row_here == 1, got, first_sent)
    partner = got
    for index, target in reversed(list(enumerate(targets))):
        served = [1, targets[-1]] if index == 0 else [targets[index - 1]]
        pairs = [((0, 0), (target, 0))] + [((r + APART, 0), (r, 0)) for r in served]
        got = send(first_sent, pairs)
        square = jnp.where(row_here == target, got, square)
        for r in served:
            partner = jnp.where(row_here == r, got, partner)

    upper, column_upper = lax.optimization_barrier((upper, column_upper))
    got = send(column_upper, [((0, 0), (APART, 0))])
    near_first = jnp.where(row_here == APART, got, column_upper)
    near_upper, near_held = near_first, [0, APART]
    upper, _ = upper_step(upper, 1, upper)

    def send_both(value, pairs, hops):
        nonlocal near_upper
        hops = [hop for hop in hops if hop[1] < n_row]
        if value is not None and near_first.shape != value.shape:
            return send(value, pairs)
        if value is None:
            value = near_first
        for row, _ in hops:
            value = jnp.where((row_here == row) & (col_here == 0), near_first, value)
        got = send(value, pairs + [((a, 0), (b, 0)) for a, b in hops])
        for _, row in hops:
            near_upper = jnp.where(row_here == row, got, near_upper)
            near_held.append(row)
        return got

    def compute(square, partner):
        columns = jnp.concatenate([matrix[:, :NB], summed(partner)], axis=0)
        both = multipliers(summed(square), columns)
        both = both.astype(jnp.bfloat16)
        return both[:NB], both[NB:]

    def none(square, partner):
        zero = jnp.zeros((NB, NB), jnp.bfloat16)
        return zero, zero

    working = (row_here & APART == 0) & (col_here == 0)
    lower, lower_far = lax.cond(working, compute, none, square, partner)

    received = lower
    for c in range(2, n_col, 2):
        pairs = [((r, 0), (r + APART, c)) for r in workers]
        got = send_both(lower_far, pairs, [(APART, 4)] if c == 2 else [])
        received = jnp.where((row_here & APART != 0) & (col_here == c), got, received)
    pairs = [((r, 0), (r + APART, 0)) for r in workers]
    got = send_both(lower_far, pairs, [(APART, 5)])
    received = jnp.where((row_here & APART != 0) & (col_here == 0), got, received)
    for c in range(2, n_col, 2):
        pairs = [((r, 0), (r, c)) for r in workers[1:]]
        got = send_both(lower, pairs, [(APART, 7), (0, 1)] if c == 2 else [])
        received = jnp.where((row_here & APART == 0) & (col_here == c), got, received)
    near_first, _ = lax.optimization_barrier((near_first, lower))
    send_both(None, [], [(APART, 6), (0, 3)])
    while len(near_held) < n_row:
        missing = [r for r in range(n_row) if r not in near_held]
        hops = list(zip(near_held, missing))
        got = send(near_upper, [((a, 0), (b, 0)) for a, b in hops])
        for _, row in hops:
            near_upper = jnp.where(row_here == row, got, near_upper)
            near_held.append(row)
    for step in range(2, len(down)):
        upper, _ = upper_step(upper, step, upper)
    got = send(
        received, [((r, c), (r, c + 1)) for r in range(1, n_row) for c in range(0, n_col, 2)]
    )
    received = jnp.where(col_here % 2 == 0, received, got)
    received = jnp.where(row_here == 0, jnp.zeros_like(received), received)

    column_upper = jnp.concatenate([jnp.zeros((NB, NB), jnp.bfloat16), near_upper], axis=1)
    upper = jnp.where(col_here == 0, column_upper, upper)
    return matrix - jnp.dot(received, upper, preferred_element_type=jnp.float32)


def solution(mesh):
    return jax.shard_map(
        shards,
        mesh=mesh,
        in_specs=(P("row", "col"),),
        out_specs=P("row", "col"),
        check_vma=False,
    )
```

```python
import jax
import jax.numpy as jnp
from jax import lax
from jax.sharding import PartitionSpec as P

NB = 256
HIGH = lax.Precision.HIGH
APART = 2


def strides(size):
    out, stride = [], size // 2
    while stride:
        out.append(stride)
        stride //= 2
    return out


def multipliers(square, columns):
    identity = jnp.eye(NB, dtype=jnp.float32)
    diagonal = square * identity
    across = 1.0 / jnp.sum(diagonal, axis=0, keepdims=True)
    down = 1.0 / jnp.sum(diagonal, axis=1, keepdims=True)
    approx = down * (2.0 * identity - square * across)
    product = jnp.dot(jnp.concatenate([square, columns], axis=0), approx, precision=HIGH)
    return jnp.dot(product[NB:], 2.0 * identity - product[:NB], precision=HIGH)


def shards(matrix):
    rows_dev, cols_dev = matrix.shape
    assert rows_dev == NB
    n_row, n_col = lax.axis_size("row"), lax.axis_size("col")
    row_here, col_here = lax.axis_index("row"), lax.axis_index("col")

    def send(value, pairs):
        flat = [(r0 * n_col + c0, r1 * n_col + c1) for (r0, c0), (r1, c1) in pairs]
        return lax.ppermute(value, ("row", "col"), flat)

    def blocks(matrix):
        return matrix[:, :NB], matrix.astype(jnp.bfloat16)

    def no_blocks(matrix):
        return jnp.zeros((NB, NB), matrix.dtype), jnp.zeros(matrix.shape, jnp.bfloat16)

    sends_columns = (col_here == 0) & (row_here & APART != 0)
    pivot_columns, first_upper = lax.cond(
        sends_columns | (row_here == 0), blocks, no_blocks, matrix
    )
    upper = lax.optimization_barrier(jnp.where(row_here == 0, first_upper, 0))

    down = strides(n_row)
    orders = [[down[-1]] + down[:-1], down, down[:1] + down[-1:] + down[1:-1]]
    kinds = [2 if c == 1 else c % 2 for c in range(n_col)]
    kind_here = jnp.where(col_here == 1, 2, col_here % 2)
    held = [[0], [0], [0]]

    def upper_step(value, step, sent, pairs=()):
        pairs = list(pairs)
        takes = jnp.bool_(False)
        for kind in range(3):
            stride = orders[kind][step]
            missing = sum(orders[kind][step + 1 :])
            takes = takes | ((kind_here == kind) & ((row_here & (stride | missing)) == stride))
            pairs += [
                ((h, c), (h + stride, c))
                for h in held[kind]
                for c in range(1, n_col)
                if kinds[c] == kind
            ]
            held[kind] = held[kind] + [h + stride for h in held[kind]]
        got = send(sent, pairs)
        return jnp.where(takes, got, value), got

    workers = [r for r in range(n_row) if r & APART == 0]
    targets = workers[1:2] + workers[:1:-1]
    square, partner = matrix[:, :NB], matrix[:, :NB]
    passed, got = upper_step(upper, 0, first_upper, [((0, 0), (1, 0))])
    near_upper = jnp.where(row_here == 1, got[:, NB:], upper[:, NB:])
    upper = passed
    for index, target in reversed(list(enumerate(targets))):
        served = [targets[index - 1]] if index else [0]
        if index == 1:
            served += targets[-1:]
        pairs = [((0, 0), (target, 0))] + [((r + APART, 0), (r, 0)) for r in served]
        got = send(pivot_columns, pairs)
        square = jnp.where(row_here == target, got, square)
        for r in served:
            partner = jnp.where(row_here == r, got, partner)
    near_sent = near_upper
    for target in targets[1:]:
        got = send(near_sent, [((1, 0), (target, 0))])
        near_upper = jnp.where(row_here == target, got, near_upper)
    upper, _ = upper_step(upper, 1, upper)

    def compute(square, partner):
        both = multipliers(square, jnp.concatenate([matrix[:, :NB], partner], axis=0))
        both = both.astype(jnp.bfloat16)
        return both[:NB], both[NB:]

    def none(square, partner):
        zero = jnp.zeros((NB, NB), jnp.bfloat16)
        return zero, zero

    working = (row_here & APART == 0) & (col_here == 0)
    lower, lower_far = lax.cond(working, compute, none, square, partner)
    received = lower
    for c in range(2, n_col, 2):
        got = send(lower_far, [((r, 0), (r + APART, c)) for r in workers])
        received = jnp.where((row_here & APART != 0) & (col_here == c), got, received)
    got = send(lower_far, [((r, 0), (r + APART, 0)) for r in workers])
    received = jnp.where((row_here & APART != 0) & (col_here == 0), got, received)
    for c in range(2, n_col, 2):
        got = send(lower, [((r, 0), (r, c)) for r in targets])
        received = jnp.where((row_here & APART == 0) & (col_here == c), got, received)
    near_sent, _ = lax.optimization_barrier((near_upper, lower))
    got = send(near_sent, [((r, 0), (r + APART, 0)) for r in workers])
    near_upper = jnp.where(row_here & APART != 0, got, near_upper)
    for step in range(2, len(down)):
        upper, _ = upper_step(upper, step, upper)
    got = send(
        received, [((r, c), (r, c + 1)) for r in range(1, n_row) for c in range(0, n_col, 2)]
    )
    received = jnp.where(col_here % 2 == 0, received, got)
    received = jnp.where(row_here == 0, jnp.zeros_like(received), received)

    column_upper = jnp.concatenate([jnp.zeros((NB, NB), jnp.bfloat16), near_upper], axis=1)
    upper = jnp.where(col_here == 0, column_upper, upper)
    return matrix - jnp.dot(received, upper, preferred_element_type=jnp.float32)


def solution(mesh):
    return jax.shard_map(
        shards,
        mesh=mesh,
        in_specs=(P("row", "col"),),
        out_specs=P("row", "col"),
        check_vma=False,
    )
```

```python
import jax
import jax.numpy as jnp
from jax import lax
from jax.sharding import PartitionSpec as P

NB = 256
HIGH = lax.Precision.HIGH
APART = 2


def strides(size):
    out, stride = [], size // 2
    while stride:
        out.append(stride)
        stride //= 2
    return out


def multipliers(square, columns):
    identity = jnp.eye(NB, dtype=jnp.float32)
    diagonal = square * identity
    across = 1.0 / jnp.sum(diagonal, axis=0, keepdims=True)
    down = 1.0 / jnp.sum(diagonal, axis=1, keepdims=True)
    approx = down * (2.0 * identity - square * across)
    product = jnp.dot(jnp.concatenate([square, columns], axis=0), approx, precision=HIGH)
    return jnp.dot(product[NB:], 2.0 * identity - product[:NB], precision=HIGH)


def shards(matrix):
    rows_dev, cols_dev = matrix.shape
    assert rows_dev == NB
    n_row, n_col = lax.axis_size("row"), lax.axis_size("col")
    row_here, col_here = lax.axis_index("row"), lax.axis_index("col")

    def send(value, pairs):
        flat = [(r0 * n_col + c0, r1 * n_col + c1) for (r0, c0), (r1, c1) in pairs]
        return lax.ppermute(value, ("row", "col"), flat)

    def blocks(matrix):
        return matrix[:, :NB], matrix.astype(jnp.bfloat16)

    def no_blocks(matrix):
        return jnp.zeros((NB, NB), matrix.dtype), jnp.zeros(matrix.shape, jnp.bfloat16)

    sends_columns = (col_here == 0) & (row_here & APART != 0)
    pivot_columns, first_upper = lax.cond(
        sends_columns | (row_here == 0), blocks, no_blocks, matrix
    )
    upper = lax.optimization_barrier(jnp.where(row_here == 0, first_upper, 0))

    down = strides(n_row)
    orders = [[down[-1]] + down[:-1], down, down[:1] + down[-1:] + down[1:-1]]
    kinds = [2 if c == 1 else c % 2 for c in range(n_col)]
    kind_here = jnp.where(col_here == 1, 2, col_here % 2)
    held = [[0], [0], [0]]

    def upper_step(value, step, sent, pairs=()):
        pairs = list(pairs)
        takes = jnp.bool_(False)
        for kind in range(3):
            stride = orders[kind][step]
            missing = sum(orders[kind][step + 1 :])
            takes = takes | ((kind_here == kind) & ((row_here & (stride | missing)) == stride))
            pairs += [
                ((h, c), (h + stride, c))
                for h in held[kind]
                for c in range(1, n_col)
                if kinds[c] == kind
            ]
            held[kind] = held[kind] + [h + stride for h in held[kind]]
        got = send(sent, pairs)
        return jnp.where(takes, got, value), got

    workers = [r for r in range(n_row) if r & APART == 0]
    targets = workers[:1:-1]
    targets.insert(1, 1)
    square, partner = matrix[:, :NB], matrix[:, :NB]
    passed, got = upper_step(upper, 0, first_upper, [((0, 0), (1, 0))])
    near_upper = jnp.where(row_here == 1, got[:, NB:], upper[:, NB:])
    upper = passed
    for index, target in reversed(list(enumerate(targets))):
        served = [] if index > 1 else targets[:1] if index else [0] + targets[1:]
        pairs = [((0, 0), (target, 0))] + [((r + APART, 0), (r, 0)) for r in served]
        got = send(pivot_columns, pairs)
        square = jnp.where(row_here == target, got, square)
        for r in served:
            partner = jnp.where(row_here == r, got, partner)
    near_sent = near_upper
    for target in workers[2:]:
        got = send(near_sent, [((1, 0), (target, 0))])
        near_upper = jnp.where(row_here == target, got, near_upper)
    upper, _ = upper_step(upper, 1, upper)

    def compute(square, partner):
        both = multipliers(square, jnp.concatenate([matrix[:, :NB], partner], axis=0))
        both = both.astype(jnp.bfloat16)
        return both[:NB], both[NB:]

    def none(square, partner):
        zero = jnp.zeros((NB, NB), jnp.bfloat16)
        return zero, zero

    working = (row_here & APART == 0) & (col_here == 0)
    lower, lower_far = lax.cond(working, compute, none, square, partner)
    received = lower
    for c in range(2, n_col, 2):
        got = send(lower_far, [((r, 0), (r + APART, c)) for r in workers])
        received = jnp.where((row_here & APART != 0) & (col_here == c), got, received)
    got = send(lower_far, [((r, 0), (r + APART, 0)) for r in workers])
    received = jnp.where((row_here & APART != 0) & (col_here == 0), got, received)
    for c in range(2, n_col, 2):
        got = send(lower, [((r, 0), (r, c)) for r in targets])
        received = jnp.where((row_here & APART == 0) & (col_here == c), got, received)
    near_sent, _ = lax.optimization_barrier((near_upper, lower))
    got = send(near_sent, [((r, 0), (r + APART, 0)) for r in workers])
    near_upper = jnp.where(row_here & APART != 0, got, near_upper)
    for step in range(2, len(down)):
        upper, _ = upper_step(upper, step, upper)
    got = send(
        received, [((r, c), (r, c + 1)) for r in range(1, n_row) for c in range(0, n_col, 2)]
    )
    received = jnp.where(col_here % 2 == 0, received, got)
    received = jnp.where(row_here == 0, jnp.zeros_like(received), received)

    column_upper = jnp.concatenate([jnp.zeros((NB, NB), jnp.bfloat16), near_upper], axis=1)
    upper = jnp.where(col_here == 0, column_upper, upper)
    return matrix - jnp.dot(received, upper, preferred_element_type=jnp.float32)


def solution(mesh):
    return jax.shard_map(
        shards,
        mesh=mesh,
        in_specs=(P("row", "col"),),
        out_specs=P("row", "col"),
        check_vma=False,
    )
```

```python
import jax
import jax.numpy as jnp
from jax import lax
from jax.sharding import PartitionSpec as P

NB = 256
HIGH = lax.Precision.HIGH
APART = 2


def strides(size):
    out, stride = [], size // 2
    while stride:
        out.append(stride)
        stride //= 2
    return out


def multipliers(square, columns):
    identity = jnp.eye(NB, dtype=jnp.float32)
    diagonal = square * identity
    across = 1.0 / jnp.sum(diagonal, axis=0, keepdims=True)
    down = 1.0 / jnp.sum(diagonal, axis=1, keepdims=True)
    approx = down * (2.0 * identity - square * across)
    product = jnp.dot(jnp.concatenate([square, columns], axis=0), approx, precision=HIGH)
    return jnp.dot(product[NB:], 2.0 * identity - product[:NB], precision=HIGH)


def shards(matrix):
    rows_dev, cols_dev = matrix.shape
    assert rows_dev == NB
    n_row, n_col = lax.axis_size("row"), lax.axis_size("col")
    row_here, col_here = lax.axis_index("row"), lax.axis_index("col")

    def send(value, pairs):
        flat = [(r0 * n_col + c0, r1 * n_col + c1) for (r0, c0), (r1, c1) in pairs]
        return lax.ppermute(value, ("row", "col"), flat)

    def blocks(matrix):
        return matrix[:, :NB], matrix.astype(jnp.bfloat16)

    def no_blocks(matrix):
        return jnp.zeros((NB, NB), matrix.dtype), jnp.zeros(matrix.shape, jnp.bfloat16)

    sends_columns = (col_here == 0) & (row_here & APART != 0)
    pivot_columns, first_upper = lax.cond(
        sends_columns | (row_here == 0), blocks, no_blocks, matrix
    )
    upper = lax.optimization_barrier(jnp.where(row_here == 0, first_upper, 0))

    down = strides(n_row)
    orders = [[down[-1]] + down[:-1], down, down[:1] + down[-1:] + down[1:-1]]
    kinds = [2 if c == 1 else c % 2 for c in range(n_col)]
    kind_here = jnp.where(col_here == 1, 2, col_here % 2)
    held = [[0], [0], [0]]

    def upper_step(value, step, sent):
        pairs = []
        takes = jnp.bool_(False)
        for kind in range(3):
            stride = orders[kind][step]
            missing = sum(orders[kind][step + 1 :])
            takes = takes | ((kind_here == kind) & ((row_here & (stride | missing)) == stride))
            pairs += [
                ((h, c), (h + stride, c))
                for h in held[kind]
                for c in range(1, n_col)
                if kinds[c] == kind
            ]
            held[kind] = held[kind] + [h + stride for h in held[kind]]
        got = send(sent, pairs)
        return jnp.where(takes, got, value)

    workers = [r for r in range(n_row) if r & APART == 0]
    targets = workers[1:2] + workers[:1:-1]
    square, partner = matrix[:, :NB], matrix[:, :NB]
    near_upper = upper[:, NB:]
    upper = upper_step(upper, 0, first_upper)
    for index, target in reversed(list(enumerate(targets))):
        served = [targets[index - 1]] if index else [0]
        if index == 1:
            served += targets[-1:]
        pairs = [((0, 0), (target, 0))] + [((r + APART, 0), (r, 0)) for r in served]
        got = send(pivot_columns, pairs)
        square = jnp.where(row_here == target, got, square)
        for r in served:
            partner = jnp.where(row_here == r, got, partner)
    def near_step(near, sent, hops):
        got = send(sent, [((a, 0), (b, 0)) for a, b in hops])
        near_held.extend([b for _, b in hops])
        for _, row in hops:
            near = jnp.where(row_here == row, got, near)
        return near

    near_held = [0]
    near_sent = near_upper
    for row in (down[0], 1):
        near_upper = near_step(near_upper, near_sent, [(0, row)])
    near_held = [0, 1, down[0]]
    upper = upper_step(upper, 1, upper)

    def compute(square, partner):
        both = multipliers(square, jnp.concatenate([matrix[:, :NB], partner], axis=0))
        both = both.astype(jnp.bfloat16)
        return both[:NB], both[NB:]

    def none(square, partner):
        zero = jnp.zeros((NB, NB), jnp.bfloat16)
        return zero, zero

    working = (row_here & APART == 0) & (col_here == 0)
    lower, lower_far = lax.cond(working, compute, none, square, partner)
    received = lower
    for c in range(2, n_col, 2):
        got = send(lower_far, [((r, 0), (r + APART, c)) for r in workers])
        received = jnp.where((row_here & APART != 0) & (col_here == c), got, received)
    got = send(lower_far, [((r, 0), (r + APART, 0)) for r in workers])
    received = jnp.where((row_here & APART != 0) & (col_here == 0), got, received)
    for c in range(2, n_col, 2):
        got = send(lower, [((r, 0), (r, c)) for r in targets])
        received = jnp.where((row_here & APART == 0) & (col_here == c), got, received)
    near_sent, _ = lax.optimization_barrier((near_upper, lower))
    hops = [(0, APART), (1, n_row - 1), (down[0], down[0] + APART)]
    near_upper = near_step(near_upper, near_sent, hops)
    while len(near_held) < n_row:
        missing = [r for r in range(n_row) if r not in near_held]
        if len(missing) > 2:
            near_sent = near_upper
        near_upper = near_step(near_upper, near_sent, list(zip(near_held, missing)))
    for step in range(2, len(down)):
        upper = upper_step(upper, step, upper)
    got = send(
        received, [((r, c), (r, c + 1)) for r in range(1, n_row) for c in range(0, n_col, 2)]
    )
    received = jnp.where(col_here % 2 == 0, received, got)
    received = jnp.where(row_here == 0, jnp.zeros_like(received), received)

    column_upper = jnp.concatenate([jnp.zeros((NB, NB), jnp.bfloat16), near_upper], axis=1)
    upper = jnp.where(col_here == 0, column_upper, upper)
    return matrix - jnp.dot(received, upper, preferred_element_type=jnp.float32)


def solution(mesh):
    return jax.shard_map(
        shards,
        mesh=mesh,
        in_specs=(P("row", "col"),),
        out_specs=P("row", "col"),
        check_vma=False,
    )
```

```python
import jax
import jax.numpy as jnp
from jax import lax
from jax.sharding import PartitionSpec as P

NB = 256
HIGH = lax.Precision.HIGH
APART = 2


def strides(size):
    out, stride = [], size // 2
    while stride:
        out.append(stride)
        stride //= 2
    return out


def two_terms(values, width):
    high = lax.reduce_precision(values, exponent_bits=8, mantissa_bits=7)
    terms = [high.astype(jnp.bfloat16), (values - high).astype(jnp.bfloat16)]
    both = jnp.concatenate(terms, axis=1)
    return jnp.pad(both, ((0, 0), (0, width - both.shape[1])))


def summed(terms):
    return terms[:, :NB].astype(jnp.float32) + terms[:, NB : 2 * NB].astype(jnp.float32)


def multipliers(square, columns):
    identity = jnp.eye(NB, dtype=jnp.float32)
    diagonal = square * identity
    across = 1.0 / jnp.sum(diagonal, axis=0, keepdims=True)
    down = 1.0 / jnp.sum(diagonal, axis=1, keepdims=True)
    approx = down * (2.0 * identity - square * across)
    product = jnp.dot(jnp.concatenate([square, columns], axis=0), approx, precision=HIGH)
    return jnp.dot(product[NB:], 2.0 * identity - product[:NB], precision=HIGH)


def shards(matrix):
    rows_dev, cols_dev = matrix.shape
    assert rows_dev == NB
    n_row, n_col = lax.axis_size("row"), lax.axis_size("col")
    row_here, col_here = lax.axis_index("row"), lax.axis_index("col")

    def send(value, pairs):
        flat = [(r0 * n_col + c0, r1 * n_col + c1) for (r0, c0), (r1, c1) in pairs]
        return lax.ppermute(value, ("row", "col"), flat)

    def blocks(matrix):
        rows = matrix.astype(jnp.bfloat16)
        return jnp.where(col_here == 0, two_terms(matrix[:, :NB], cols_dev), rows), rows[:, NB:]

    def no_blocks(matrix):
        return jnp.zeros(matrix.shape, jnp.bfloat16), jnp.zeros(
            (rows_dev, cols_dev - NB), jnp.bfloat16
        )

    sends_columns = (col_here == 0) & (row_here & APART != 0)
    first_sent, column_upper = lax.cond(
        sends_columns | (row_here == 0), blocks, no_blocks, matrix
    )
    upper = lax.optimization_barrier(jnp.where(row_here == 0, first_sent, 0))

    down = strides(n_row)
    orders = [down, [down[-1]] + down[:-1]]
    held = [[0], [0]]

    def upper_step(value, step, sent, pairs=()):
        pairs = list(pairs)
        takes = []
        for kind in range(2):
            stride = orders[kind][step]
            missing = sum(orders[kind][step + 1 :])
            takes.append((row_here & (stride | missing)) == stride)
            pairs += [
                ((h, c), (h + stride, c)) for h in held[kind] for c in range(1, n_col) if c % 2 == kind
            ]
            held[kind] = held[kind] + [h + stride for h in held[kind]]
        got = send(sent, pairs)
        return jnp.where(jnp.where(col_here % 2 == 0, takes[0], takes[1]), got, value), got

    workers = [r for r in range(n_row) if r & APART == 0]
    targets = workers[:1:-1]
    targets.insert(1, 1)
    square = partner = first_sent
    for index, target in reversed(list(enumerate(targets))):
        served = [[], [0] + [r for r in workers[2:]], [1]][min(index, 2)] if index < 3 else []
        pairs = [((0, 0), (target, 0))] + [((r + APART, 0), (r, 0)) for r in served]
        if index == 0:
            upper, got = upper_step(upper, 0, first_sent, pairs)
        else:
            got = send(first_sent, pairs)
        square = jnp.where(row_here == target, got, square)
        for r in served:
            partner = jnp.where(row_here == r, got, partner)

    upper, column_upper = lax.optimization_barrier((upper, column_upper))
    near_upper = column_upper
    for target in targets:
        got = send(column_upper, [((0, 0), (target, 0))])
        near_upper = jnp.where(row_here == target, got, near_upper)
    upper, _ = upper_step(upper, 1, upper)

    def compute(square, partner):
        columns = jnp.concatenate([matrix[:, :NB], summed(partner)], axis=0)
        both = multipliers(summed(square), columns)
        both = both.astype(jnp.bfloat16)
        return both[:NB], both[NB:]

    def none(square, partner):
        zero = jnp.zeros((NB, NB), jnp.bfloat16)
        return zero, zero

    working = (row_here & APART == 0) & (col_here == 0)
    lower, lower_far = lax.cond(working, compute, none, square, partner)
    received = lower
    for c in range(2, n_col, 2):
        got = send(lower_far, [((r, 0), (r + APART, c)) for r in workers])
        received = jnp.where((row_here & APART != 0) & (col_here == c), got, received)
    got = send(lower_far, [((r, 0), (r + APART, 0)) for r in workers])
    received = jnp.where((row_here & APART != 0) & (col_here == 0), got, received)
    for c in range(2, n_col, 2):
        got = send(lower, [((r, 0), (r, c)) for r in targets])
        received = jnp.where((row_here & APART == 0) & (col_here == c), got, received)
    near_sent, _ = lax.optimization_barrier((near_upper, lower))
    got = send(near_sent, [((r, 0), (r + APART, 0)) for r in workers])
    near_upper = jnp.where(row_here & APART != 0, got, near_upper)
    for step in range(2, len(down)):
        upper, _ = upper_step(upper, step, upper)
    got = send(
        received, [((r, c), (r, c + 1)) for r in range(1, n_row) for c in range(0, n_col, 2)]
    )
    received = jnp.where(col_here % 2 == 0, received, got)
    received = jnp.where(row_here == 0, jnp.zeros_like(received), received)

    column_upper = jnp.concatenate([jnp.zeros((NB, NB), jnp.bfloat16), near_upper], axis=1)
    upper = jnp.where(col_here == 0, column_upper, upper)
    return matrix - jnp.dot(received, upper, preferred_element_type=jnp.float32)


def solution(mesh):
    return jax.shard_map(
        shards,
        mesh=mesh,
        in_specs=(P("row", "col"),),
        out_specs=P("row", "col"),
        check_vma=False,
    )
```

```python
import jax
import jax.numpy as jnp
from jax import lax
from jax.sharding import PartitionSpec as P

NB = 256
HIGH = lax.Precision.HIGH
APART = 2


def strides(size):
    out, stride = [], size // 2
    while stride:
        out.append(stride)
        stride //= 2
    return out


def multipliers(square, columns):
    identity = jnp.eye(NB, dtype=jnp.float32)
    diagonal = square * identity
    across = 1.0 / jnp.sum(diagonal, axis=0, keepdims=True)
    down = 1.0 / jnp.sum(diagonal, axis=1, keepdims=True)
    approx = down * (2.0 * identity - square * across)
    product = jnp.dot(jnp.concatenate([square, columns], axis=0), approx, precision=HIGH)
    return jnp.dot(product[NB:], 2.0 * identity - product[:NB], precision=HIGH)


def shards(matrix):
    rows_dev, cols_dev = matrix.shape
    assert rows_dev == NB
    n_row, n_col = lax.axis_size("row"), lax.axis_size("col")
    row_here, col_here = lax.axis_index("row"), lax.axis_index("col")

    def send(value, pairs):
        flat = [(r0 * n_col + c0, r1 * n_col + c1) for (r0, c0), (r1, c1) in pairs]
        return lax.ppermute(value, ("row", "col"), flat)

    def blocks(matrix):
        return matrix[:, :NB], matrix.astype(jnp.bfloat16)

    def no_blocks(matrix):
        return jnp.zeros((NB, NB), matrix.dtype), jnp.zeros(matrix.shape, jnp.bfloat16)

    sends_columns = (col_here == 0) & (row_here & APART != 0)
    pivot_columns, first_upper = lax.cond(
        sends_columns | (row_here == 0), blocks, no_blocks, matrix
    )
    upper = lax.optimization_barrier(jnp.where(row_here == 0, first_upper, 0))

    down = strides(n_row)
    orders = [[down[-1]] + down[:-1], down, down[:1] + down[-1:] + down[1:-1]]
    kinds = [2 if c == 1 else c % 2 for c in range(n_col)]
    kind_here = jnp.where(col_here == 1, 2, col_here % 2)
    held = [[0], [0], [0]]

    def upper_step(value, step, sent, pairs=()):
        pairs = list(pairs)
        takes = jnp.bool_(False)
        for kind in range(3):
            stride = orders[kind][step]
            missing = sum(orders[kind][step + 1 :])
            takes = takes | ((kind_here == kind) & ((row_here & (stride | missing)) == stride))
            pairs += [
                ((h, c), (h + stride, c))
                for h in held[kind]
                for c in range(1, n_col)
                if kinds[c] == kind
            ]
            held[kind] = held[kind] + [h + stride for h in held[kind]]
        got = send(sent, pairs)
        return jnp.where(takes, got, value), got

    workers = [r for r in range(n_row) if r & APART == 0]
    targets = workers[:1:-1]
    targets.insert(1, 1)
    square, partner = matrix[:, :NB], matrix[:, :NB]
    passed, got = upper_step(upper, 0, first_upper, [((0, 0), (1, 0))])
    near_upper = jnp.where(row_here == 1, got[:, NB:], upper[:, NB:])
    upper = passed
    for index, target in reversed(list(enumerate(targets))):
        served = [] if index > 1 else targets[:1] if index else [0] + targets[1:]
        pairs = [((0, 0), (target, 0))] + [((r + APART, 0), (r, 0)) for r in served]
        got = send(pivot_columns, pairs)
        square = jnp.where(row_here == target, got, square)
        for r in served:
            partner = jnp.where(row_here == r, got, partner)
    near_sent = near_upper
    for target in workers[2:]:
        got = send(near_sent, [((1, 0), (target, 0))])
        near_upper = jnp.where(row_here == target, got, near_upper)
    upper, _ = upper_step(upper, 1, upper)

    def compute(square, partner):
        both = multipliers(square, jnp.concatenate([matrix[:, :NB], partner], axis=0))
        both = both.astype(jnp.bfloat16)
        return both[:NB], both[NB:]

    def none(square, partner):
        zero = jnp.zeros((NB, NB), jnp.bfloat16)
        return zero, zero

    working = (row_here & APART == 0) & (col_here == 0)
    lower, lower_far = lax.cond(working, compute, none, square, partner)
    received = lower
    for c in range(0, n_col, 2):
        got = send(lower_far, [((r, 0), (r + APART, c)) for r in workers])
        received = jnp.where((row_here & APART != 0) & (col_here == c), got, received)
    for c in range(2, n_col, 2):
        got = send(lower, [((r, 0), (r, c)) for r in targets])
        received = jnp.where((row_here & APART == 0) & (col_here == c), got, received)
    near_sent, _ = lax.optimization_barrier((near_upper, lower))
    got = send(near_sent, [((r, 0), (r + APART, 0)) for r in workers])
    near_upper = jnp.where(row_here & APART != 0, got, near_upper)
    for step in range(2, len(down)):
        upper, _ = upper_step(upper, step, upper)
    got = send(
        received, [((r, c), (r, c + 1)) for r in range(1, n_row) for c in range(0, n_col, 2)]
    )
    received = jnp.where(col_here % 2 == 0, received, got)
    received = jnp.where(row_here == 0, jnp.zeros_like(received), received)

    column_upper = jnp.concatenate([jnp.zeros((NB, NB), jnp.bfloat16), near_upper], axis=1)
    upper = jnp.where(col_here == 0, column_upper, upper)
    return matrix - jnp.dot(received, upper, preferred_element_type=jnp.float32)


def solution(mesh):
    return jax.shard_map(
        shards,
        mesh=mesh,
        in_specs=(P("row", "col"),),
        out_specs=P("row", "col"),
        check_vma=False,
    )
```

```python
import jax
import jax.numpy as jnp
from jax import lax
from jax.sharding import PartitionSpec as P

NB = 256
HIGH = lax.Precision.HIGH
APART = 2


def strides(size):
    out, stride = [], size // 2
    while stride:
        out.append(stride)
        stride //= 2
    return out


def multipliers(square, columns):
    identity = jnp.eye(NB, dtype=jnp.float32)
    diagonal = square * identity
    across = 1.0 / jnp.sum(diagonal, axis=0, keepdims=True)
    down = 1.0 / jnp.sum(diagonal, axis=1, keepdims=True)
    approx = down * (2.0 * identity - square * across)
    product = jnp.dot(jnp.concatenate([square, columns], axis=0), approx, precision=HIGH)
    return jnp.dot(product[NB:], 2.0 * identity - product[:NB], precision=HIGH)


def shards(matrix):
    rows_dev, cols_dev = matrix.shape
    assert rows_dev == NB
    n_row, n_col = lax.axis_size("row"), lax.axis_size("col")
    row_here, col_here = lax.axis_index("row"), lax.axis_index("col")

    def send(value, pairs):
        flat = [(r0 * n_col + c0, r1 * n_col + c1) for (r0, c0), (r1, c1) in pairs]
        return lax.ppermute(value, ("row", "col"), flat)

    def blocks(matrix):
        return matrix[:, :NB], matrix.astype(jnp.bfloat16)

    def no_blocks(matrix):
        return jnp.zeros((NB, NB), matrix.dtype), jnp.zeros(matrix.shape, jnp.bfloat16)

    sends_columns = (col_here == 0) & (row_here & APART != 0)
    pivot_columns, first_upper = lax.cond(
        sends_columns | (row_here == 0), blocks, no_blocks, matrix
    )
    upper = lax.optimization_barrier(jnp.where(row_here == 0, first_upper, 0))

    down = strides(n_row)
    orders = [[down[-1]] + down[:-1], down, down[:1] + down[-1:] + down[1:-1]]
    kinds = [2 if c == 1 else c % 2 for c in range(n_col)]
    kind_here = jnp.where(col_here == 1, 2, col_here % 2)
    held = [[0], [0], [0]]

    def upper_step(value, step, sent, pairs=()):
        pairs = list(pairs)
        takes = jnp.bool_(False)
        for kind in range(3):
            stride = orders[kind][step]
            missing = sum(orders[kind][step + 1 :])
            takes = takes | ((kind_here == kind) & ((row_here & (stride | missing)) == stride))
            pairs += [
                ((h, c), (h + stride, c))
                for h in held[kind]
                for c in range(1, n_col)
                if kinds[c] == kind
            ]
            held[kind] = held[kind] + [h + stride for h in held[kind]]
        got = send(sent, pairs)
        return jnp.where(takes, got, value), got

    workers = [r for r in range(n_row) if r & APART == 0]
    targets = workers[:1:-1]
    targets.insert(1, 1)
    square, partner = matrix[:, :NB], matrix[:, :NB]
    passed, got = upper_step(upper, 0, first_upper, [((0, 0), (1, 0))])
    near_upper = jnp.where(row_here == 1, got[:, NB:], upper[:, NB:])
    upper = passed
    for index, target in reversed(list(enumerate(targets))):
        served = [] if index > 1 else targets[:1] if index else [0] + targets[1:]
        pairs = [((0, 0), (target, 0))] + [((r + APART, 0), (r, 0)) for r in served]
        got = send(pivot_columns, pairs)
        square = jnp.where(row_here == target, got, square)
        for r in served:
            partner = jnp.where(row_here == r, got, partner)
    near_sent = near_upper
    for target in workers[2:]:
        got = send(near_sent, [((1, 0), (target, 0))])
        near_upper = jnp.where(row_here == target, got, near_upper)
    near_first = send(near_sent, [((r, 0), (r + APART, 0)) for r in workers[:2]])
    upper, _ = upper_step(upper, 1, upper)

    def compute(square, partner):
        both = multipliers(square, jnp.concatenate([matrix[:, :NB], partner], axis=0))
        both = both.astype(jnp.bfloat16)
        return both[:NB], both[NB:]

    def none(square, partner):
        zero = jnp.zeros((NB, NB), jnp.bfloat16)
        return zero, zero

    working = (row_here & APART == 0) & (col_here == 0)
    lower, lower_far = lax.cond(working, compute, none, square, partner)
    received = lower
    for c in range(0, n_col, 2):
        got = send(lower_far, [((r, 0), (r + APART, c)) for r in workers])
        received = jnp.where((row_here & APART != 0) & (col_here == c), got, received)
    for c in range(2, n_col, 2):
        got = send(lower, [((r, 0), (r, c)) for r in targets])
        received = jnp.where((row_here & APART == 0) & (col_here == c), got, received)
    near_sent, _ = lax.optimization_barrier((near_upper, lower))
    got = send(near_sent, [((r, 0), (r + APART, 0)) for r in workers[2:]])
    near_upper = jnp.where(row_here & APART != 0, got, near_upper)
    near_upper = jnp.where((row_here | 1) == APART + 1, near_first, near_upper)
    for step in range(2, len(down)):
        upper, _ = upper_step(upper, step, upper)
    got = send(
        received, [((r, c), (r, c + 1)) for r in range(1, n_row) for c in range(0, n_col, 2)]
    )
    received = jnp.where(col_here % 2 == 0, received, got)
    received = jnp.where(row_here == 0, jnp.zeros_like(received), received)

    column_upper = jnp.concatenate([jnp.zeros((NB, NB), jnp.bfloat16), near_upper], axis=1)
    upper = jnp.where(col_here == 0, column_upper, upper)
    return matrix - jnp.dot(received, upper, preferred_element_type=jnp.float32)


def solution(mesh):
    return jax.shard_map(
        shards,
        mesh=mesh,
        in_specs=(P("row", "col"),),
        out_specs=P("row", "col"),
        check_vma=False,
    )
```

```python
import jax
import jax.numpy as jnp
from jax import lax
from jax.sharding import PartitionSpec as P

NB = 256
HIGH = lax.Precision.HIGH
APART = 2


def strides(size):
    out, stride = [], size // 2
    while stride:
        out.append(stride)
        stride //= 2
    return out


def multipliers(square, columns):
    identity = jnp.eye(NB, dtype=jnp.float32)
    diagonal = square * identity
    across = 1.0 / jnp.sum(diagonal, axis=0, keepdims=True)
    down = 1.0 / jnp.sum(diagonal, axis=1, keepdims=True)
    approx = down * (2.0 * identity - square * across)
    product = jnp.dot(jnp.concatenate([square, columns], axis=0), approx, precision=HIGH)
    return jnp.dot(product[NB:], 2.0 * identity - product[:NB], precision=HIGH)


def shards(matrix):
    rows_dev, cols_dev = matrix.shape
    assert rows_dev == NB
    n_row, n_col = lax.axis_size("row"), lax.axis_size("col")
    row_here, col_here = lax.axis_index("row"), lax.axis_index("col")

    def send(value, pairs):
        flat = [(r0 * n_col + c0, r1 * n_col + c1) for (r0, c0), (r1, c1) in pairs]
        return lax.ppermute(value, ("row", "col"), flat)

    def blocks(matrix):
        return matrix[:, :NB], matrix.astype(jnp.bfloat16)

    def no_blocks(matrix):
        return jnp.zeros((NB, NB), matrix.dtype), jnp.zeros(matrix.shape, jnp.bfloat16)

    sends_columns = (col_here == 0) & (row_here & APART != 0)
    pivot_columns, first_upper = lax.cond(
        sends_columns | (row_here == 0), blocks, no_blocks, matrix
    )
    upper = lax.optimization_barrier(jnp.where(row_here == 0, first_upper, 0))

    down = strides(n_row)
    orders = [[down[-1]] + down[:-1], down, down[:1] + down[-1:] + down[1:-1]]
    kinds = [2 if c == 1 else c % 2 for c in range(n_col)]
    kind_here = jnp.where(col_here == 1, 2, col_here % 2)
    held = [[0], [0], [0]]

    def upper_step(value, step, sent, pairs=()):
        pairs = list(pairs)
        takes = jnp.bool_(False)
        for kind in range(3):
            stride = orders[kind][step]
            missing = sum(orders[kind][step + 1 :])
            takes = takes | ((kind_here == kind) & ((row_here & (stride | missing)) == stride))
            pairs += [
                ((h, c), (h + stride, c))
                for h in held[kind]
                for c in range(1, n_col)
                if kinds[c] == kind
            ]
            held[kind] = held[kind] + [h + stride for h in held[kind]]
        got = send(sent, pairs)
        return jnp.where(takes, got, value), got

    workers = [r for r in range(n_row) if r & APART == 0]
    targets = workers[:1:-1]
    targets.insert(1, 1)
    square, partner = matrix[:, :NB], matrix[:, :NB]
    passed, got = upper_step(upper, 0, first_upper, [((0, 0), (1, 0))])
    near_upper = jnp.where(row_here == 1, got[:, NB:], upper[:, NB:])
    upper = passed
    for index, target in reversed(list(enumerate(targets))):
        served = [] if index > 1 else targets[:1] if index else [0] + targets[1:]
        pairs = [((0, 0), (target, 0))] + [((r + APART, 0), (r, 0)) for r in served]
        got = send(pivot_columns, pairs)
        square = jnp.where(row_here == target, got, square)
        for r in served:
            partner = jnp.where(row_here == r, got, partner)
    near_sent = near_upper
    for target in workers[2:]:
        got = send(near_sent, [((1, 0), (target, 0))])
        near_upper = jnp.where(row_here == target, got, near_upper)
    upper, _ = upper_step(upper, 1, upper)

    def compute(square, partner):
        both = multipliers(square, jnp.concatenate([matrix[:, :NB], partner], axis=0))
        both = both.astype(jnp.bfloat16)
        return both[:NB], both[NB:]

    def none(square, partner):
        zero = jnp.zeros((NB, NB), jnp.bfloat16)
        return zero, zero

    working = (row_here & APART == 0) & (col_here == 0)
    lower, lower_far = lax.cond(working, compute, none, square, partner)
    received = lower
    both = jnp.concatenate([lower_far, near_upper], axis=1)
    for c in range(0, n_col, 2):
        got = send(lower_far if c else both, [((r, 0), (r + APART, c)) for r in workers])
        if c == 0:
            near_upper = jnp.where(row_here & APART != 0, got[:, NB:], near_upper)
        takes = (row_here & APART != 0) & (col_here == c)
        received = jnp.where(takes, got[:, :NB], received)
    for c in range(2, n_col, 2):
        got = send(lower, [((r, 0), (r, c)) for r in targets])
        received = jnp.where((row_here & APART == 0) & (col_here == c), got, received)
    for step in range(2, len(down)):
        upper, _ = upper_step(upper, step, upper)
    got = send(
        received, [((r, c), (r, c + 1)) for r in range(1, n_row) for c in range(0, n_col, 2)]
    )
    received = jnp.where(col_here % 2 == 0, received, got)
    received = jnp.where(row_here == 0, jnp.zeros_like(received), received)

    column_upper = jnp.concatenate([jnp.zeros((NB, NB), jnp.bfloat16), near_upper], axis=1)
    upper = jnp.where(col_here == 0, column_upper, upper)
    return matrix - jnp.dot(received, upper, preferred_element_type=jnp.float32)


def solution(mesh):
    return jax.shard_map(
        shards,
        mesh=mesh,
        in_specs=(P("row", "col"),),
        out_specs=P("row", "col"),
        check_vma=False,
    )
```

```python
import jax
import jax.numpy as jnp
from jax import lax
from jax.sharding import PartitionSpec as P

NB = 256
HIGH = lax.Precision.HIGH
APART = 2


def strides(size):
    out, stride = [], size // 2
    while stride:
        out.append(stride)
        stride //= 2
    return out


def multipliers(square, columns):
    identity = jnp.eye(NB, dtype=jnp.float32)
    diagonal = square * identity
    across = 1.0 / jnp.sum(diagonal, axis=0, keepdims=True)
    down = 1.0 / jnp.sum(diagonal, axis=1, keepdims=True)
    approx = down * (2.0 * identity - square * across)
    product = jnp.dot(jnp.concatenate([square, columns], axis=0), approx, precision=HIGH)
    return jnp.dot(product[NB:], 2.0 * identity - product[:NB], precision=HIGH)


def shards(matrix):
    rows_dev, cols_dev = matrix.shape
    assert rows_dev == NB
    n_row, n_col = lax.axis_size("row"), lax.axis_size("col")
    row_here, col_here = lax.axis_index("row"), lax.axis_index("col")

    def send(value, pairs):
        flat = [(r0 * n_col + c0, r1 * n_col + c1) for (r0, c0), (r1, c1) in pairs]
        return lax.ppermute(value, ("row", "col"), flat)

    def blocks(matrix):
        return matrix[:, :NB], matrix.astype(jnp.bfloat16)

    def no_blocks(matrix):
        return jnp.zeros((NB, NB), matrix.dtype), jnp.zeros(matrix.shape, jnp.bfloat16)

    sends_columns = (col_here == 0) & (row_here & APART != 0)
    pivot_columns, first_upper = lax.cond(
        sends_columns | (row_here == 0), blocks, no_blocks, matrix
    )
    upper = lax.optimization_barrier(jnp.where(row_here == 0, first_upper, 0))

    down = strides(n_row)
    orders = [[down[-1]] + down[:-1], down, down[:1] + down[-1:] + down[1:-1]]
    kinds = [2 if c == 1 else c % 2 for c in range(n_col)]
    kind_here = jnp.where(col_here == 1, 2, col_here % 2)
    held = [[0], [0], [0]]

    def upper_step(value, step, sent, pairs=()):
        pairs = list(pairs)
        takes = jnp.bool_(False)
        for kind in range(3):
            stride = orders[kind][step]
            missing = sum(orders[kind][step + 1 :])
            takes = takes | ((kind_here == kind) & ((row_here & (stride | missing)) == stride))
            pairs += [
                ((h, c), (h + stride, c))
                for h in held[kind]
                for c in range(1, n_col)
                if kinds[c] == kind
            ]
            held[kind] = held[kind] + [h + stride for h in held[kind]]
        got = send(sent, pairs)
        return jnp.where(takes, got, value), got

    workers = [r for r in range(n_row) if r & APART == 0]
    targets = workers[:1:-1]
    targets.insert(1, 1)
    square, partner = matrix[:, :NB], matrix[:, :NB]
    passed, got = upper_step(upper, 0, first_upper, [((0, 0), (1, 0))])
    near_upper = jnp.where(row_here == 1, got[:, NB:], upper[:, NB:])
    upper = passed
    for index, target in reversed(list(enumerate(targets))):
        served = [] if index > 1 else targets[:1] if index else [0] + targets[1:]
        pairs = [((0, 0), (target, 0))] + [((r + APART, 0), (r, 0)) for r in served]
        got = send(pivot_columns, pairs)
        square = jnp.where(row_here == target, got, square)
        for r in served:
            partner = jnp.where(row_here == r, got, partner)
    near_sent = near_upper
    for even, odd in zip(workers[2::2], workers[3::2]):
        got = send(near_sent, [((0, 0), (even, 0)), ((1, 0), (odd, 0))])
        near_upper = jnp.where((row_here | 1) == odd, got, near_upper)
    upper, _ = upper_step(upper, 1, upper)

    def compute(square, partner):
        both = multipliers(square, jnp.concatenate([matrix[:, :NB], partner], axis=0))
        both = both.astype(jnp.bfloat16)
        return both[:NB], both[NB:]

    def none(square, partner):
        zero = jnp.zeros((NB, NB), jnp.bfloat16)
        return zero, zero

    working = (row_here & APART == 0) & (col_here == 0)
    lower, lower_far = lax.cond(working, compute, none, square, partner)
    received = lower
    for c in range(0, n_col, 2):
        got = send(lower_far, [((r, 0), (r + APART, c)) for r in workers])
        received = jnp.where((row_here & APART != 0) & (col_here == c), got, received)
    for c in range(2, n_col, 2):
        got = send(lower, [((r, 0), (r, c)) for r in targets])
        received = jnp.where((row_here & APART == 0) & (col_here == c), got, received)
    near_sent, _ = lax.optimization_barrier((near_upper, lower))
    got = send(near_sent, [((r, 0), (r + APART, 0)) for r in workers])
    near_upper = jnp.where(row_here & APART != 0, got, near_upper)
    for step in range(2, len(down)):
        upper, _ = upper_step(upper, step, upper)
    got = send(
        received, [((r, c), (r, c + 1)) for r in range(1, n_row) for c in range(0, n_col, 2)]
    )
    received = jnp.where(col_here % 2 == 0, received, got)
    received = jnp.where(row_here == 0, jnp.zeros_like(received), received)

    column_upper = jnp.concatenate([jnp.zeros((NB, NB), jnp.bfloat16), near_upper], axis=1)
    upper = jnp.where(col_here == 0, column_upper, upper)
    return matrix - jnp.dot(received, upper, preferred_element_type=jnp.float32)


def solution(mesh):
    return jax.shard_map(
        shards,
        mesh=mesh,
        in_specs=(P("row", "col"),),
        out_specs=P("row", "col"),
        check_vma=False,
    )
```

```python
import jax
import jax.numpy as jnp
from jax import lax
from jax.sharding import PartitionSpec as P

NB = 256
HIGH = lax.Precision.HIGH
APART = 2


def strides(size):
    out, stride = [], size // 2
    while stride:
        out.append(stride)
        stride //= 2
    return out


def multipliers(square, columns):
    identity = jnp.eye(NB, dtype=jnp.float32)
    diagonal = square * identity
    across = 1.0 / jnp.sum(diagonal, axis=0, keepdims=True)
    down = 1.0 / jnp.sum(diagonal, axis=1, keepdims=True)
    approx = down * (2.0 * identity - square * across)
    product = jnp.dot(jnp.concatenate([square, columns], axis=0), approx, precision=HIGH)
    return jnp.dot(product[NB:], 2.0 * identity - product[:NB], precision=HIGH)


def shards(matrix):
    rows_dev, cols_dev = matrix.shape
    assert rows_dev == NB
    n_row, n_col = lax.axis_size("row"), lax.axis_size("col")
    row_here, col_here = lax.axis_index("row"), lax.axis_index("col")

    def send(value, pairs):
        flat = [(r0 * n_col + c0, r1 * n_col + c1) for (r0, c0), (r1, c1) in pairs]
        return lax.ppermute(value, ("row", "col"), flat)

    def blocks(matrix):
        return matrix[:, :NB], matrix.astype(jnp.bfloat16)

    def no_blocks(matrix):
        return jnp.zeros((NB, NB), matrix.dtype), jnp.zeros(matrix.shape, jnp.bfloat16)

    sends_columns = (col_here == 0) & (row_here & APART != 0)
    pivot_columns, first_upper = lax.cond(
        sends_columns | (row_here == 0), blocks, no_blocks, matrix
    )
    upper = lax.optimization_barrier(jnp.where(row_here == 0, first_upper, 0))

    down = strides(n_row)
    middle = n_row // 2
    orders = [[down[-1]] + down[:-1], down]
    held = [[0], [0]]
    beside_steps = [[(0, middle)], [(middle, middle + 1)]]
    for stride in down[1:-1]:
        far = [b for step in beside_steps for _, b in step]
        beside_steps.append([(h, h + stride) for h in far])
    beside_steps[-1].append((0, 1))
    beside_back = [(middle + r - 2, r) for r in range(2, middle)]

    def among(rows):
        found = jnp.bool_(False)
        for row in rows:
            found = found | (row_here == row)
        return found

    def upper_step(value, step, sent):
        pairs = [((a, 1), (b, 1)) for a, b in beside_steps[step]]
        takes = (col_here == 1) & among([b for _, b in beside_steps[step]])
        for kind in range(2):
            stride = orders[kind][step]
            missing = sum(orders[kind][step + 1 :])
            takes = takes | (
                (col_here != 1)
                & (col_here % 2 == kind)
                & ((row_here & (stride | missing)) == stride)
            )
            pairs += [
                ((h, c), (h + stride, c))
                for h in held[kind]
                for c in range(3 * kind, n_col, 2)
            ]
            held[kind] = held[kind] + [h + stride for h in held[kind]]
        got = send(sent, pairs)
        return jnp.where(takes, got, value)

    workers = [r for r in range(n_row) if r & APART == 0]
    targets = workers[:1:-1]
    targets.insert(1, 1)
    square, partner = matrix[:, :NB], matrix[:, :NB]
    upper = upper_step(upper, 0, first_upper)
    for index, target in reversed(list(enumerate(targets))):
        served = [] if index > 1 else targets[:1] if index else [0] + targets[1:]
        pairs = [((0, 0), (target, 0))] + [((r + APART, 0), (r, 0)) for r in served]
        got = send(pivot_columns, pairs)
        square = jnp.where(row_here == target, got, square)
        for r in served:
            partner = jnp.where(row_here == r, got, partner)
    upper = upper_step(upper, 1, upper)

    def compute(square, partner):
        both = multipliers(square, jnp.concatenate([matrix[:, :NB], partner], axis=0))
        both = both.astype(jnp.bfloat16)
        return both[:NB], both[NB:]

    def none(square, partner):
        zero = jnp.zeros((NB, NB), jnp.bfloat16)
        return zero, zero

    working = (row_here & APART == 0) & (col_here == 0)
    lower, lower_far = lax.cond(working, compute, none, square, partner)
    received = lower
    for c in range(0, n_col, 2):
        got = send(lower_far, [((r, 0), (r + APART, c)) for r in workers])
        received = jnp.where((row_here & APART != 0) & (col_here == c), got, received)
    for c in range(2, n_col, 2):
        got = send(lower, [((r, 0), (r, c)) for r in targets])
        received = jnp.where((row_here & APART == 0) & (col_here == c), got, received)
    sent = upper
    for step in range(2, len(down)):
        upper = upper_step(upper, step, upper)
    if len(beside_back) > 2:
        sent = upper
    got = send(sent, [((a, 1), (b, 1)) for a, b in beside_back])
    upper = jnp.where((col_here == 1) & (row_here > 1) & (row_here < middle), got, upper)
    got = send(
        received, [((r, c), (r, c + 1)) for r in range(1, n_row) for c in range(0, n_col, 2)]
    )
    received = jnp.where(col_here % 2 == 0, received, got)
    received = jnp.where(row_here == 0, jnp.zeros_like(received), received)

    col_done = col_here * cols_dev + jnp.arange(cols_dev, dtype=jnp.int32) < NB
    upper = jnp.where(col_done[None, :], jnp.zeros_like(upper), upper)
    return matrix - jnp.dot(received, upper, preferred_element_type=jnp.float32)


def solution(mesh):
    return jax.shard_map(
        shards,
        mesh=mesh,
        in_specs=(P("row", "col"),),
        out_specs=P("row", "col"),
        check_vma=False,
    )
```

```python
import jax
import jax.numpy as jnp
from jax import lax
from jax.sharding import PartitionSpec as P

NB = 256
HIGH = lax.Precision.HIGH
APART = 2


def strides(size):
    out, stride = [], size // 2
    while stride:
        out.append(stride)
        stride //= 2
    return out


def multipliers(square, columns):
    identity = jnp.eye(NB, dtype=jnp.float32)
    diagonal = square * identity
    across = 1.0 / jnp.sum(diagonal, axis=0, keepdims=True)
    down = 1.0 / jnp.sum(diagonal, axis=1, keepdims=True)
    approx = down * (2.0 * identity - square * across)
    product = jnp.dot(jnp.concatenate([square, columns], axis=0), approx, precision=HIGH)
    return jnp.dot(product[NB:], 2.0 * identity - product[:NB], precision=HIGH)


def shards(matrix):
    rows_dev, cols_dev = matrix.shape
    assert rows_dev == NB
    n_row, n_col = lax.axis_size("row"), lax.axis_size("col")
    row_here, col_here = lax.axis_index("row"), lax.axis_index("col")

    def send(value, pairs):
        flat = [(r0 * n_col + c0, r1 * n_col + c1) for (r0, c0), (r1, c1) in pairs]
        return lax.ppermute(value, ("row", "col"), flat)

    def blocks(matrix):
        return matrix[:, :NB], matrix.astype(jnp.bfloat16)

    def no_blocks(matrix):
        return jnp.zeros((NB, NB), matrix.dtype), jnp.zeros(matrix.shape, jnp.bfloat16)

    sends_columns = (col_here == 0) & (row_here & APART != 0)
    pivot_columns, first_upper = lax.cond(
        sends_columns | (row_here == 0), blocks, no_blocks, matrix
    )
    upper = lax.optimization_barrier(jnp.where(row_here == 0, first_upper, 0))

    down = strides(n_row)
    middle = n_row // 2
    orders = [[down[-1]] + down[:-1], down]
    held = [[0], [0]]
    beside_steps = [[(0, middle)], [(middle, middle + 1)]]
    for stride in down[1:-1]:
        far = [b for step in beside_steps for _, b in step]
        beside_steps.append([(h, h + stride) for h in far])
    beside_steps[-1].append((0, 1))
    beside_back = [(middle + r - 2, r) for r in range(2, middle)]
    relieved = middle + APART

    def among(rows):
        found = jnp.bool_(False)
        for row in rows:
            found = found | (row_here == row)
        return found

    def upper_step(value, step, sent):
        pairs = [((a, 1), (b, 1)) for a, b in beside_steps[step]]
        takes = (col_here == 1) & among([b for _, b in beside_steps[step]])
        for kind in range(2):
            stride = orders[kind][step]
            missing = sum(orders[kind][step + 1 :])
            takes = takes | (
                (col_here != 1)
                & (col_here % 2 == kind)
                & ((row_here & (stride | missing)) == stride)
            )
            pairs += [
                ((h, c), (h + stride, c))
                for h in held[kind]
                for c in range(3 * kind, n_col, 2)
                if c or h + stride != relieved
            ]
            held[kind] = held[kind] + [h + stride for h in held[kind]]
        got = send(sent, pairs)
        return jnp.where(takes, got, value)

    workers = [r for r in range(n_row) if r & APART == 0]
    targets = workers[:1:-1]
    targets.insert(1, 1)
    square, partner = matrix[:, :NB], matrix[:, :NB]
    upper = upper_step(upper, 0, first_upper)
    for index, target in reversed(list(enumerate(targets))):
        served = [] if index > 1 else targets[:1] if index else [0] + targets[1:]
        pairs = [((0, 0), (target, 0))] + [((r + APART, 0), (r, 0)) for r in served]
        got = send(pivot_columns, pairs)
        square = jnp.where(row_here == target, got, square)
        for r in served:
            partner = jnp.where(row_here == r, got, partner)
    upper = upper_step(upper, 1, upper)

    def compute(square, partner):
        both = multipliers(square, jnp.concatenate([matrix[:, :NB], partner], axis=0))
        both = both.astype(jnp.bfloat16)
        return both[:NB], both[NB:]

    def none(square, partner):
        zero = jnp.zeros((NB, NB), jnp.bfloat16)
        return zero, zero

    working = (row_here & APART == 0) & (col_here == 0)
    lower, lower_far = lax.cond(working, compute, none, square, partner)
    received = lower
    for c in range(0, n_col, 2):
        got = send(lower_far, [((r, 0), (r + APART, c)) for r in workers])
        received = jnp.where((row_here & APART != 0) & (col_here == c), got, received)
    for c in range(2, n_col, 2):
        got = send(lower, [((r, 0), (r, c)) for r in targets])
        received = jnp.where((row_here & APART == 0) & (col_here == c), got, received)
    got = send(lower, [((middle, 0), (middle, 3))])
    direct = (row_here == middle) & (col_here == 3)
    received = jnp.where(direct, got, received)
    sent = upper
    for step in range(2, len(down)):
        upper = upper_step(upper, step, upper)
    if len(beside_back) > 2:
        sent = upper
    pairs = [((a, 1), (b, 1)) for a, b in beside_back] + [((middle + 1, 0), (relieved, 0))]
    got = send(sent, pairs)
    takes = (col_here == 1) & (row_here > 1) & (row_here < middle)
    takes = takes | ((col_here == 0) & (row_here == relieved))
    upper = jnp.where(takes, got, upper)
    got = send(
        received,
        [
            ((r, c), (r, c + 1))
            for r in range(1, n_row)
            for c in range(0, n_col, 2)
            if (r, c) != (middle, 2)
        ],
    )
    received = jnp.where((col_here % 2 == 0) | direct, received, got)
    received = jnp.where(row_here == 0, jnp.zeros_like(received), received)

    col_done = col_here * cols_dev + jnp.arange(cols_dev, dtype=jnp.int32) < NB
    upper = jnp.where(col_done[None, :], jnp.zeros_like(upper), upper)
    return matrix - jnp.dot(received, upper, preferred_element_type=jnp.float32)


def solution(mesh):
    return jax.shard_map(
        shards,
        mesh=mesh,
        in_specs=(P("row", "col"),),
        out_specs=P("row", "col"),
        check_vma=False,
    )
```

```python
import jax
import jax.numpy as jnp
from jax import lax
from jax.sharding import PartitionSpec as P

NB = 256
HIGH = lax.Precision.HIGH
APART = 2


def strides(size):
    out, stride = [], size // 2
    while stride:
        out.append(stride)
        stride //= 2
    return out


def two_terms(values, width):
    high = lax.reduce_precision(values, exponent_bits=8, mantissa_bits=7)
    terms = [high.astype(jnp.bfloat16), (values - high).astype(jnp.bfloat16)]
    both = jnp.concatenate(terms, axis=1)
    return jnp.pad(both, ((0, 0), (0, width - both.shape[1])))


def summed(terms):
    return terms[:, :NB].astype(jnp.float32) + terms[:, NB : 2 * NB].astype(jnp.float32)


def multipliers(square, columns):
    identity = jnp.eye(NB, dtype=jnp.float32)
    diagonal = square * identity
    across = 1.0 / jnp.sum(diagonal, axis=0, keepdims=True)
    down = 1.0 / jnp.sum(diagonal, axis=1, keepdims=True)
    approx = down * (2.0 * identity - square * across)
    product = jnp.dot(jnp.concatenate([square, columns], axis=0), approx, precision=HIGH)
    return jnp.dot(product[NB:], 2.0 * identity - product[:NB], precision=HIGH)


def shards(matrix):
    rows_dev, cols_dev = matrix.shape
    assert rows_dev == NB
    n_row, n_col = lax.axis_size("row"), lax.axis_size("col")
    row_here, col_here = lax.axis_index("row"), lax.axis_index("col")

    def send(value, pairs):
        flat = [(r0 * n_col + c0, r1 * n_col + c1) for (r0, c0), (r1, c1) in pairs]
        return lax.ppermute(value, ("row", "col"), flat)

    middle = n_row // 2
    shared = middle + APART

    def blocks(matrix):
        columns, rows = matrix[:, :NB], matrix.astype(jnp.bfloat16)
        return columns, jnp.where(row_here == shared, two_terms(columns, cols_dev), rows)

    def no_blocks(matrix):
        return jnp.zeros((NB, NB), matrix.dtype), jnp.zeros(matrix.shape, jnp.bfloat16)

    sends_columns = (col_here == 0) & (row_here & APART != 0)
    pivot_columns, first_upper = lax.cond(
        sends_columns | (row_here == 0), blocks, no_blocks, matrix
    )
    upper = lax.optimization_barrier(jnp.where(row_here == 0, first_upper, 0))

    down = strides(n_row)
    orders = [[down[-1]] + down[:-1], down]
    held = [[0], [0]]
    beside_steps = [[(0, middle)], [(middle, middle + 1)]]
    for stride in down[1:-1]:
        far = [b for step in beside_steps for _, b in step]
        beside_steps.append([(h, h + stride) for h in far])
    beside_steps[-1].append((0, 1))
    beside_back = [(middle + r - 2, r) for r in range(2, middle)]

    def among(rows):
        found = jnp.bool_(False)
        for row in rows:
            found = found | (row_here == row)
        return found

    def upper_step(value, step, sent, pairs=()):
        pairs = list(pairs) + [((a, 1), (b, 1)) for a, b in beside_steps[step]]
        takes = (col_here == 1) & among([b for _, b in beside_steps[step]])
        for kind in range(2):
            stride = orders[kind][step]
            missing = sum(orders[kind][step + 1 :])
            takes = takes | (
                (col_here != 1)
                & (col_here % 2 == kind)
                & ((row_here & (stride | missing)) == stride)
            )
            pairs += [
                ((h, c), (h + stride, c))
                for h in held[kind]
                for c in range(3 * kind, n_col, 2)
            ]
            held[kind] = held[kind] + [h + stride for h in held[kind]]
        got = send(sent, pairs)
        return jnp.where(takes, got, value), got

    workers = [r for r in range(n_row) if r & APART == 0]
    targets = workers[:1:-1]
    targets.insert(1, 1)
    square, partner = matrix[:, :NB], matrix[:, :NB]
    upper, got = upper_step(upper, 0, first_upper, [((shared, 0), (0, 0))])
    own = jnp.where(row_here == 0, summed(got), matrix[:, :NB])
    for index, target in enumerate(targets):
        served = [] if index > 1 else targets[:1] if index else [0] + targets[1:]
        pairs = [((0, 0), (target, 0))] + [((r + APART, 0), (r, 0)) for r in served]
        got = send(pivot_columns, pairs)
        square = jnp.where(row_here == target, got, square)
        for r in served:
            partner = jnp.where(row_here == r, got, partner)
    upper, _ = upper_step(upper, 1, upper)

    def compute(square, own, partner):
        both = multipliers(square, jnp.concatenate([own, partner], axis=0))
        both = both.astype(jnp.bfloat16)
        return both[:NB], both[NB:]

    def none(square, own, partner):
        zero = jnp.zeros((NB, NB), jnp.bfloat16)
        return zero, zero

    working = (row_here & APART == 0) & (col_here == 0)
    lower, lower_far = lax.cond(working, compute, none, square, own, partner)
    others = [r for r in workers if r not in (0, middle)]
    far = row_here & APART != 0
    received = lower

    def send_near(c):
        pairs = [((r, 0), (r + APART, 0)) for r in workers]
        return send(lower_far, pairs), far & (col_here == 0)

    def send_cross(c):
        sent = jnp.where((row_here == 0) | (row_here == middle), lower, lower_far)
        pairs = [((0, 0), (shared, c)), ((middle, 0), (middle, c))]
        pairs += [((r, 0), (r + APART, c)) for r in others]
        takes = (far & (row_here != APART)) | (row_here == middle)
        return send(sent, pairs), takes & (col_here == c)

    def send_own(c):
        pairs = [((0, 0), (APART, c))] + [((r, 0), (r, c)) for r in others]
        takes = (~far & (row_here != middle)) | (row_here == APART)
        sent = jnp.where(row_here == 0, lower_far, lower)
        return send(sent, pairs), takes & (col_here == c)

    even = range(2, n_col, 2)
    for step, columns in ((send_near, [0]), (send_own, even), (send_cross, even)):
        for c in columns:
            got, takes = step(c)
            received = jnp.where(takes, got, received)
    sent = upper
    for step in range(2, len(down)):
        upper, _ = upper_step(upper, step, upper)
    if len(beside_back) > 2:
        sent = upper
    got = send(sent, [((a, 1), (b, 1)) for a, b in beside_back])
    upper = jnp.where((col_here == 1) & (row_here > 1) & (row_here < middle), got, upper)
    got = send(
        received, [((r, c), (r, c + 1)) for r in range(1, n_row) for c in range(0, n_col, 2)]
    )
    received = jnp.where(col_here % 2 == 0, received, got)
    received = jnp.where(row_here == 0, jnp.zeros_like(received), received)

    col_done = col_here * cols_dev + jnp.arange(cols_dev, dtype=jnp.int32) < NB
    upper = jnp.where(col_done[None, :], jnp.zeros_like(upper), upper)
    return matrix - jnp.dot(received, upper, preferred_element_type=jnp.float32)


def solution(mesh):
    return jax.shard_map(
        shards,
        mesh=mesh,
        in_specs=(P("row", "col"),),
        out_specs=P("row", "col"),
        check_vma=False,
    )
```

```python
import jax
import jax.numpy as jnp
from jax import lax
from jax.sharding import PartitionSpec as P

NB = 256
HIGH = lax.Precision.HIGH
APART = 2


def strides(size):
    out, stride = [], size // 2
    while stride:
        out.append(stride)
        stride //= 2
    return out


def two_terms(values, width):
    high = lax.reduce_precision(values, exponent_bits=8, mantissa_bits=7)
    terms = [high.astype(jnp.bfloat16), (values - high).astype(jnp.bfloat16)]
    both = jnp.concatenate(terms, axis=1)
    return jnp.pad(both, ((0, 0), (0, width - both.shape[1])))


def summed(terms):
    return terms[:, :NB].astype(jnp.float32) + terms[:, NB : 2 * NB].astype(jnp.float32)


def multipliers(square, columns):
    identity = jnp.eye(NB, dtype=jnp.float32)
    diagonal = square * identity
    across = 1.0 / jnp.sum(diagonal, axis=0, keepdims=True)
    down = 1.0 / jnp.sum(diagonal, axis=1, keepdims=True)
    approx = down * (2.0 * identity - square * across)
    product = jnp.dot(jnp.concatenate([square, columns], axis=0), approx, precision=HIGH)
    return jnp.dot(product[NB:], 2.0 * identity - product[:NB], precision=HIGH)


def shards(matrix):
    rows_dev, cols_dev = matrix.shape
    assert rows_dev == NB
    n_row, n_col = lax.axis_size("row"), lax.axis_size("col")
    row_here, col_here = lax.axis_index("row"), lax.axis_index("col")

    def send(value, pairs):
        flat = [(r0 * n_col + c0, r1 * n_col + c1) for (r0, c0), (r1, c1) in pairs]
        return lax.ppermute(value, ("row", "col"), flat)

    middle = n_row // 2
    shared = middle + APART

    def blocks(matrix):
        terms, rows = two_terms(matrix[:, :NB], cols_dev), matrix.astype(jnp.bfloat16)
        return terms, jnp.where(row_here == shared, terms, rows)

    def no_blocks(matrix):
        return jnp.zeros(matrix.shape, jnp.bfloat16), jnp.zeros(matrix.shape, jnp.bfloat16)

    sends_columns = (col_here == 0) & (row_here & APART != 0)
    pivot_columns, first_upper = lax.cond(
        sends_columns | (row_here == 0), blocks, no_blocks, matrix
    )
    upper = lax.optimization_barrier(jnp.where(row_here == 0, first_upper, 0))

    down = strides(n_row)
    orders = [[down[-1]] + down[:-1], down]
    held = [[0], [0]]
    beside_steps = [[(0, middle)], [(middle, middle + 1)]]
    for stride in down[1:-1]:
        far = [b for step in beside_steps for _, b in step]
        beside_steps.append([(h, h + stride) for h in far])
    beside_steps[-1].append((0, 1))
    beside_back = [(middle + r - 2, r) for r in range(2, middle)]

    def among(rows):
        found = jnp.bool_(False)
        for row in rows:
            found = found | (row_here == row)
        return found

    def upper_step(value, step, sent, pairs=()):
        pairs = list(pairs) + [((a, 1), (b, 1)) for a, b in beside_steps[step]]
        takes = (col_here == 1) & among([b for _, b in beside_steps[step]])
        for kind in range(2):
            stride = orders[kind][step]
            missing = sum(orders[kind][step + 1 :])
            takes = takes | (
                (col_here != 1)
                & (col_here % 2 == kind)
                & ((row_here & (stride | missing)) == stride)
            )
            pairs += [
                ((h, c), (h + stride, c))
                for h in held[kind]
                for c in range(3 * kind, n_col, 2)
            ]
            held[kind] = held[kind] + [h + stride for h in held[kind]]
        got = send(sent, pairs)
        return jnp.where(takes, got, value), got

    workers = [r for r in range(n_row) if r & APART == 0]
    targets = workers[:1:-1]
    targets.insert(1, 1)
    square = partner = pivot_columns
    upper, got = upper_step(upper, 0, first_upper, [((shared, 0), (0, 0))])
    own = jnp.where(row_here == 0, summed(got), matrix[:, :NB])
    for index, target in enumerate(targets):
        served = [] if index > 1 else targets[:1] if index else [0] + targets[1:]
        pairs = [((0, 0), (target, 0))] + [((r + APART, 0), (r, 0)) for r in served]
        got = send(pivot_columns, pairs)
        square = jnp.where(row_here == target, got, square)
        for r in served:
            partner = jnp.where(row_here == r, got, partner)
    upper, _ = upper_step(upper, 1, upper)

    def compute(square, own, partner):
        columns = jnp.concatenate([own, summed(partner)], axis=0)
        both = multipliers(summed(square), columns)
        both = both.astype(jnp.bfloat16)
        return both[:NB], both[NB:]

    def none(square, own, partner):
        zero = jnp.zeros((NB, NB), jnp.bfloat16)
        return zero, zero

    working = (row_here & APART == 0) & (col_here == 0)
    lower, lower_far = lax.cond(working, compute, none, square, own, partner)
    others = [r for r in workers if r not in (0, middle)]
    far = row_here & APART != 0
    received = lower

    def send_near(c):
        pairs = [((r, 0), (r + APART, 0)) for r in workers]
        return send(lower_far, pairs), far & (col_here == 0)

    def send_cross(c):
        sent = jnp.where((row_here == 0) | (row_here == middle), lower, lower_far)
        pairs = [((0, 0), (shared, c)), ((middle, 0), (middle, c))]
        pairs += [((r, 0), (r + APART, c)) for r in others]
        takes = (far & (row_here != APART)) | (row_here == middle)
        return send(sent, pairs), takes & (col_here == c)

    def send_own(c):
        pairs = [((0, 0), (APART, c))] + [((r, 0), (r, c)) for r in others]
        takes = (~far & (row_here != middle)) | (row_here == APART)
        sent = jnp.where(row_here == 0, lower_far, lower)
        return send(sent, pairs), takes & (col_here == c)

    even = range(2, n_col, 2)
    for step, columns in ((send_near, [0]), (send_own, even), (send_cross, even)):
        for c in columns:
            got, takes = step(c)
            received = jnp.where(takes, got, received)
    sent = upper
    for step in range(2, len(down)):
        upper, _ = upper_step(upper, step, upper)
    if len(beside_back) > 2:
        sent = upper
    got = send(sent, [((a, 1), (b, 1)) for a, b in beside_back])
    upper = jnp.where((col_here == 1) & (row_here > 1) & (row_here < middle), got, upper)
    got = send(
        received, [((r, c), (r, c + 1)) for r in range(1, n_row) for c in range(0, n_col, 2)]
    )
    received = jnp.where(col_here % 2 == 0, received, got)
    received = jnp.where(row_here == 0, jnp.zeros_like(received), received)

    col_done = col_here * cols_dev + jnp.arange(cols_dev, dtype=jnp.int32) < NB
    upper = jnp.where(col_done[None, :], jnp.zeros_like(upper), upper)
    return matrix - jnp.dot(received, upper, preferred_element_type=jnp.float32)


def solution(mesh):
    return jax.shard_map(
        shards,
        mesh=mesh,
        in_specs=(P("row", "col"),),
        out_specs=P("row", "col"),
        check_vma=False,
    )
```

```python
import jax
import jax.numpy as jnp
from jax import lax
from jax.sharding import PartitionSpec as P

NB = 256
HIGH = lax.Precision.HIGH
APART = 2


def strides(size):
    out, stride = [], size // 2
    while stride:
        out.append(stride)
        stride //= 2
    return out


def two_terms(values, width):
    high = lax.reduce_precision(values, exponent_bits=8, mantissa_bits=7)
    terms = [high.astype(jnp.bfloat16), (values - high).astype(jnp.bfloat16)]
    both = jnp.concatenate(terms, axis=1)
    return jnp.pad(both, ((0, 0), (0, width - both.shape[1])))


def summed(terms):
    return terms[:, :NB].astype(jnp.float32) + terms[:, NB : 2 * NB].astype(jnp.float32)


def multipliers(square, columns):
    identity = jnp.eye(NB, dtype=jnp.float32)
    diagonal = square * identity
    across = 1.0 / jnp.sum(diagonal, axis=0, keepdims=True)
    down = 1.0 / jnp.sum(diagonal, axis=1, keepdims=True)
    approx = down * (2.0 * identity - square * across)
    product = jnp.dot(jnp.concatenate([square, columns], axis=0), approx, precision=HIGH)
    return jnp.dot(product[NB:], 2.0 * identity - product[:NB], precision=HIGH)


def shards(matrix):
    rows_dev, cols_dev = matrix.shape
    assert rows_dev == NB
    n_row, n_col = lax.axis_size("row"), lax.axis_size("col")
    row_here, col_here = lax.axis_index("row"), lax.axis_index("col")

    def send(value, pairs):
        flat = [(r0 * n_col + c0, r1 * n_col + c1) for (r0, c0), (r1, c1) in pairs]
        return lax.ppermute(value, ("row", "col"), flat)

    middle = n_row // 2
    shared = middle + APART

    def blocks(matrix):
        terms, rows = two_terms(matrix[:, :NB], cols_dev), matrix.astype(jnp.bfloat16)
        return terms, jnp.where(row_here == shared, terms, rows)

    def no_blocks(matrix):
        return jnp.zeros(matrix.shape, jnp.bfloat16), jnp.zeros(matrix.shape, jnp.bfloat16)

    sends_columns = (col_here == 0) & (row_here & APART != 0)
    pivot_columns, first_upper = lax.cond(
        sends_columns | (row_here == 0), blocks, no_blocks, matrix
    )
    upper = lax.optimization_barrier(jnp.where(row_here == 0, first_upper, 0))

    down = strides(n_row)
    orders = [[down[-1]] + down[:-1], down]
    held = [[0], [0]]
    beside_steps = [[(0, middle)], [(middle, middle + 1)]]
    for stride in down[1:-1]:
        far = [b for step in beside_steps for _, b in step]
        beside_steps.append([(h, h + stride) for h in far])
    beside_steps[-1].append((0, 1))
    beside_back = [(middle + r - 2, r) for r in range(2, middle)]
    first_steps = [[(0, 1)], [(0, APART), (1, middle + 1)]]
    first_held = [0, 1, APART, middle + 1]
    for step in range(2, len(down)):
        hops = []
        for source in first_held[step == len(down) - 1 :]:
            missing = [r for r in range(n_row) if r not in first_held + [b for _, b in hops]]
            near = [r for r in missing if r == source + APART]
            hops += [(source, r) for r in (near or missing)[:1]]
        first_steps.append(hops)
        first_held = first_held + [b for _, b in hops]
    first_back = [(APART, r) for r in range(n_row) if r not in first_held]
    assert len(first_back) == 1

    def among(rows):
        found = jnp.bool_(False)
        for row in rows:
            found = found | (row_here == row)
        return found

    def upper_step(value, step, sent, pairs=()):
        pairs = list(pairs) + [((a, 1), (b, 1)) for a, b in beside_steps[step]]
        pairs += [((a, 0), (b, 0)) for a, b in first_steps[step]]
        takes = (col_here == 1) & among([b for _, b in beside_steps[step]])
        takes = takes | ((col_here == 0) & among([b for _, b in first_steps[step]]))
        for kind in range(2):
            stride = orders[kind][step]
            missing = sum(orders[kind][step + 1 :])
            takes = takes | (
                (col_here > 1)
                & (col_here % 2 == kind)
                & ((row_here & (stride | missing)) == stride)
            )
            pairs += [
                ((h, c), (h + stride, c))
                for h in held[kind]
                for c in range(2 + kind, n_col, 2)
            ]
            held[kind] = held[kind] + [h + stride for h in held[kind]]
        got = send(sent, pairs)
        return jnp.where(takes, got, value), got

    workers = [r for r in range(n_row) if r & APART == 0]
    targets = workers[:1:-1]
    targets.insert(1, 1)
    square = partner = pivot_columns
    upper, got = upper_step(upper, 0, first_upper, [((shared, 0), (0, 0))])
    own = jnp.where(row_here == 0, summed(got), matrix[:, :NB])
    for index, target in enumerate(targets):
        served = [] if index > 1 else targets[:1] if index else [0] + targets[1:]
        pairs = [((0, 0), (target, 0))] + [((r + APART, 0), (r, 0)) for r in served]
        got = send(pivot_columns, pairs)
        square = jnp.where(row_here == target, got, square)
        for r in served:
            partner = jnp.where(row_here == r, got, partner)
    upper, _ = upper_step(upper, 1, upper)

    def compute(square, own, partner):
        columns = jnp.concatenate([own, summed(partner)], axis=0)
        both = multipliers(summed(square), columns)
        both = both.astype(jnp.bfloat16)
        return both[:NB], both[NB:]

    def none(square, own, partner):
        zero = jnp.zeros((NB, NB), jnp.bfloat16)
        return zero, zero

    working = (row_here & APART == 0) & (col_here == 0)
    lower, lower_far = lax.cond(working, compute, none, square, own, partner)
    others = [r for r in workers if r not in (0, middle)]
    far = row_here & APART != 0
    received = lower

    def send_near(c):
        pairs = [((r, 0), (r + APART, 0)) for r in workers]
        return send(lower_far, pairs), far & (col_here == 0)

    def send_cross(c):
        sent = jnp.where((row_here == 0) | (row_here == middle), lower, lower_far)
        pairs = [((0, 0), (shared, c)), ((middle, 0), (middle, c))]
        pairs += [((r, 0), (r + APART, c)) for r in others]
        takes = (far & (row_here != APART)) | (row_here == middle)
        return send(sent, pairs), takes & (col_here == c)

    def send_own(c):
        pairs = [((0, 0), (APART, c))] + [((r, 0), (r, c)) for r in others]
        takes = (~far & (row_here != middle)) | (row_here == APART)
        sent = jnp.where(row_here == 0, lower_far, lower)
        return send(sent, pairs), takes & (col_here == c)

    even = range(2, n_col, 2)
    for step, columns in ((send_near, [0]), (send_own, even), (send_cross, even)):
        for c in columns:
            got, takes = step(c)
            received = jnp.where(takes, got, received)
    sent = upper
    for step in range(2, len(down)):
        upper, _ = upper_step(upper, step, upper)
    if len(beside_back) > 2:
        sent = upper
    pairs = [((a, 1), (b, 1)) for a, b in beside_back] + [((a, 0), (b, 0)) for a, b in first_back]
    got = send(sent, pairs)
    takes = (col_here == 1) & (row_here > 1) & (row_here < middle)
    takes = takes | ((col_here == 0) & among([b for _, b in first_back]))
    upper = jnp.where(takes, got, upper)
    got = send(
        received, [((r, c), (r, c + 1)) for r in range(1, n_row) for c in range(0, n_col, 2)]
    )
    received = jnp.where(col_here % 2 == 0, received, got)
    received = jnp.where(row_here == 0, jnp.zeros_like(received), received)

    col_done = col_here * cols_dev + jnp.arange(cols_dev, dtype=jnp.int32) < NB
    upper = jnp.where(col_done[None, :], jnp.zeros_like(upper), upper)
    return matrix - jnp.dot(received, upper, preferred_element_type=jnp.float32)


def solution(mesh):
    return jax.shard_map(
        shards,
        mesh=mesh,
        in_specs=(P("row", "col"),),
        out_specs=P("row", "col"),
        check_vma=False,
    )
```

```python
import jax
import jax.numpy as jnp
from jax import lax
from jax.sharding import PartitionSpec as P

NB = 256
HIGH = lax.Precision.HIGH
APART = 2


def strides(size):
    out, stride = [], size // 2
    while stride:
        out.append(stride)
        stride //= 2
    return out


def two_terms(values, width):
    high = lax.reduce_precision(values, exponent_bits=8, mantissa_bits=7)
    terms = [high.astype(jnp.bfloat16), (values - high).astype(jnp.bfloat16)]
    both = jnp.concatenate(terms, axis=1)
    return jnp.pad(both, ((0, 0), (0, width - both.shape[1])))


def summed(terms):
    return terms[:, :NB].astype(jnp.float32) + terms[:, NB : 2 * NB].astype(jnp.float32)


def multipliers(square, columns):
    identity = jnp.eye(NB, dtype=jnp.float32)
    diagonal = square * identity
    across = 1.0 / jnp.sum(diagonal, axis=0, keepdims=True)
    down = 1.0 / jnp.sum(diagonal, axis=1, keepdims=True)
    approx = down * (2.0 * identity - square * across)
    product = jnp.dot(jnp.concatenate([square, columns], axis=0), approx, precision=HIGH)
    return jnp.dot(product[NB:], 2.0 * identity - product[:NB], precision=HIGH)


def shards(matrix):
    rows_dev, cols_dev = matrix.shape
    assert rows_dev == NB
    n_row, n_col = lax.axis_size("row"), lax.axis_size("col")
    row_here, col_here = lax.axis_index("row"), lax.axis_index("col")

    def send(value, pairs):
        flat = [(r0 * n_col + c0, r1 * n_col + c1) for (r0, c0), (r1, c1) in pairs]
        return lax.ppermute(value, ("row", "col"), flat)

    middle = n_row // 2
    shared = middle + APART

    def blocks(matrix):
        terms, rows = two_terms(matrix[:, :NB], cols_dev), matrix.astype(jnp.bfloat16)
        return terms, jnp.where(row_here == APART, terms, rows)

    def no_blocks(matrix):
        return jnp.zeros(matrix.shape, jnp.bfloat16), jnp.zeros(matrix.shape, jnp.bfloat16)

    sends_columns = (col_here == 0) & (row_here & APART != 0)
    pivot_columns, first_upper = lax.cond(
        sends_columns | (row_here == 0), blocks, no_blocks, matrix
    )
    upper = lax.optimization_barrier(jnp.where(row_here == 0, first_upper, 0))

    down = strides(n_row)
    orders = [[down[-1]] + down[:-1], down]
    held = [[0], [0]]
    beside_steps = [[(0, middle)], [(middle, middle + 1)]]
    for stride in down[1:-1]:
        far = [b for step in beside_steps for _, b in step]
        beside_steps.append([(h, h + stride) for h in far])
    beside_steps[-1].append((0, 1))
    beside_back = [(middle + r - 2, r) for r in range(2, middle)]
    first_steps = [[(0, 1)], [(0, APART), (1, middle)]]
    first_held = [0, 1, APART, middle]
    first_wish = {1: middle + 1, APART: APART + 1, middle: middle + APART}
    for step in range(2, len(down)):
        hops = []
        for source in first_held[step == len(down) - 1 :]:
            missing = [r for r in range(n_row) if r not in first_held + [b for _, b in hops]]
            near = [r for r in missing if r == first_wish.get(source)]
            hops += [(source, r) for r in (near or missing)[:1]]
        first_steps.append(hops)
        first_held = first_held + [b for _, b in hops]
    first_back = [(APART, r) for r in range(n_row) if r not in first_held]
    assert len(first_back) == 1

    def among(rows):
        found = jnp.bool_(False)
        for row in rows:
            found = found | (row_here == row)
        return found

    def upper_step(value, step, sent, pairs=()):
        pairs = list(pairs) + [((a, 1), (b, 1)) for a, b in beside_steps[step]]
        pairs += [((a, 0), (b, 0)) for a, b in first_steps[step]]
        takes = (col_here == 1) & among([b for _, b in beside_steps[step]])
        takes = takes | ((col_here == 0) & among([b for _, b in first_steps[step]]))
        for kind in range(2):
            stride = orders[kind][step]
            missing = sum(orders[kind][step + 1 :])
            takes = takes | (
                (col_here > 1)
                & (col_here % 2 == kind)
                & ((row_here & (stride | missing)) == stride)
            )
            pairs += [
                ((h, c), (h + stride, c))
                for h in held[kind]
                for c in range(2 + kind, n_col, 2)
            ]
            held[kind] = held[kind] + [h + stride for h in held[kind]]
        got = send(sent, pairs)
        return jnp.where(takes, got, value), got

    workers = [r for r in range(n_row) if r & APART == 0]
    targets = workers[:1:-1]
    targets.insert(1, 1)
    square = pivot_columns
    upper, partner = upper_step(upper, 0, first_upper, [((APART, 0), (0, 0))])
    for index, target in enumerate(targets):
        served = [] if index > 1 else targets[:1] + [middle] if index else targets[1:]
        served = [r for r in served if index or r != middle]
        pairs = [((0, 0), (target, 0))] + [((r + APART, 0), (r, 0)) for r in served]
        if index == 0:
            pairs += [((shared, 0), (0, 0))]
        got = send(pivot_columns, pairs)
        square = jnp.where(row_here == target, got, square)
        if index == 0:
            own = jnp.where(row_here == 0, summed(got), matrix[:, :NB])
        for r in served:
            partner = jnp.where(row_here == r, got, partner)
    upper, _ = upper_step(upper, 1, upper)

    def compute(square, own, partner):
        columns = jnp.concatenate([own, summed(partner)], axis=0)
        both = multipliers(summed(square), columns)
        both = both.astype(jnp.bfloat16)
        return both[:NB], both[NB:]

    def none(square, own, partner):
        zero = jnp.zeros((NB, NB), jnp.bfloat16)
        return zero, zero

    working = (row_here & APART == 0) & (col_here == 0)
    lower, lower_far = lax.cond(working, compute, none, square, own, partner)
    others = [r for r in workers if r not in (0, middle)]
    far = row_here & APART != 0
    received = lower

    def send_near(c):
        pairs = [((r, 0), (r + APART, 0)) for r in workers]
        return send(lower_far, pairs), far & (col_here == 0)

    def send_cross(c):
        sent = jnp.where((row_here == 0) | (row_here == middle), lower, lower_far)
        pairs = [((0, 0), (shared, c)), ((middle, 0), (middle, c))]
        pairs += [((r, 0), (r + APART, c)) for r in others]
        takes = (far & (row_here != APART)) | (row_here == middle)
        return send(sent, pairs), takes & (col_here == c)

    def send_own(c):
        pairs = [((0, 0), (APART, c))] + [((r, 0), (r, c)) for r in others]
        takes = (~far & (row_here != middle)) | (row_here == APART)
        sent = jnp.where(row_here == 0, lower_far, lower)
        return send(sent, pairs), takes & (col_here == c)

    even = range(2, n_col, 2)
    for step, columns in ((send_near, [0]), (send_own, even), (send_cross, even)):
        for c in columns:
            got, takes = step(c)
            received = jnp.where(takes, got, received)
    sent = upper
    for step in range(2, len(down)):
        upper, _ = upper_step(upper, step, upper)
    if len(beside_back) > 2:
        sent = upper
    pairs = [((a, 1), (b, 1)) for a, b in beside_back] + [((a, 0), (b, 0)) for a, b in first_back]
    got = send(sent, pairs)
    takes = (col_here == 1) & (row_here > 1) & (row_here < middle)
    takes = takes | ((col_here == 0) & among([b for _, b in first_back]))
    upper = jnp.where(takes, got, upper)
    got = send(
        received, [((r, c), (r, c + 1)) for r in range(1, n_row) for c in range(0, n_col, 2)]
    )
    received = jnp.where(col_here % 2 == 0, received, got)
    received = jnp.where(row_here == 0, jnp.zeros_like(received), received)

    col_done = col_here * cols_dev + jnp.arange(cols_dev, dtype=jnp.int32) < NB
    upper = jnp.where(col_done[None, :], jnp.zeros_like(upper), upper)
    return matrix - jnp.dot(received, upper, preferred_element_type=jnp.float32)


def solution(mesh):
    return jax.shard_map(
        shards,
        mesh=mesh,
        in_specs=(P("row", "col"),),
        out_specs=P("row", "col"),
        check_vma=False,
    )
```

```python
import jax
import jax.numpy as jnp
from jax import lax
from jax.sharding import PartitionSpec as P

NB = 256
HIGH = lax.Precision.HIGH
APART = 2


def strides(size):
    out, stride = [], size // 2
    while stride:
        out.append(stride)
        stride //= 2
    return out


def multipliers(square, columns):
    identity = jnp.eye(NB, dtype=jnp.float32)
    diagonal = square * identity
    across = 1.0 / jnp.sum(diagonal, axis=0, keepdims=True)
    down = 1.0 / jnp.sum(diagonal, axis=1, keepdims=True)
    approx = down * (2.0 * identity - square * across)
    product = jnp.dot(jnp.concatenate([square, columns], axis=0), approx, precision=HIGH)
    return jnp.dot(product[NB:], 2.0 * identity - product[:NB], precision=HIGH)


def shards(matrix):
    rows_dev, cols_dev = matrix.shape
    assert rows_dev == NB
    n_row, n_col = lax.axis_size("row"), lax.axis_size("col")
    row_here, col_here = lax.axis_index("row"), lax.axis_index("col")

    def send(value, pairs):
        flat = [(r0 * n_col + c0, r1 * n_col + c1) for (r0, c0), (r1, c1) in pairs]
        return lax.ppermute(value, ("row", "col"), flat)

    def blocks(matrix):
        return matrix[:, :NB], matrix.astype(jnp.bfloat16)

    def no_blocks(matrix):
        return jnp.zeros((NB, NB), matrix.dtype), jnp.zeros(matrix.shape, jnp.bfloat16)

    sends_columns = (col_here == 0) & (row_here & APART != 0)
    pivot_columns, first_upper = lax.cond(
        sends_columns | (row_here == 0), blocks, no_blocks, matrix
    )
    upper = lax.optimization_barrier(jnp.where(row_here == 0, first_upper, 0))

    down = strides(n_row)
    middle = n_row // 2
    orders = [[down[-1]] + down[:-1], down]
    held = [[0], [0]]
    beside_steps = [[(0, middle)], [(middle, middle + 1)]]
    for stride in down[1:-1]:
        far = [b for step in beside_steps for _, b in step]
        beside_steps.append([(h, h + stride) for h in far])
    beside_steps[-1].append((0, 1))
    beside_back = [(middle + r - 2, r) for r in range(2, middle)]
    relieved = middle + APART

    def among(rows):
        found = jnp.bool_(False)
        for row in rows:
            found = found | (row_here == row)
        return found

    def upper_step(value, step, sent):
        pairs = [((a, 1), (b, 1)) for a, b in beside_steps[step]]
        takes = (col_here == 1) & among([b for _, b in beside_steps[step]])
        for kind in range(2):
            stride = orders[kind][step]
            missing = sum(orders[kind][step + 1 :])
            takes = takes | (
                (col_here != 1)
                & (col_here % 2 == kind)
                & ((row_here & (stride | missing)) == stride)
            )
            pairs += [
                ((h, c), (h + stride, c))
                for h in held[kind]
                for c in range(3 * kind, n_col, 2)
                if c or h + stride != relieved
            ]
            held[kind] = held[kind] + [h + stride for h in held[kind]]
        got = send(sent, pairs)
        return jnp.where(takes, got, value)

    workers = [r for r in range(n_row) if r & APART == 0]
    targets = workers[:1:-1]
    targets.insert(1, 1)
    square, partner = matrix[:, :NB], matrix[:, :NB]
    upper = upper_step(upper, 0, first_upper)
    for index, target in reversed(list(enumerate(targets))):
        served = [] if index > 1 else targets[:1] if index else [0] + targets[1:]
        pairs = [((0, 0), (target, 0))] + [((r + APART, 0), (r, 0)) for r in served]
        got = send(pivot_columns, pairs)
        square = jnp.where(row_here == target, got, square)
        for r in served:
            partner = jnp.where(row_here == r, got, partner)
    upper = upper_step(upper, 1, upper)

    def compute(square, partner):
        both = multipliers(square, jnp.concatenate([matrix[:, :NB], partner], axis=0))
        both = both.astype(jnp.bfloat16)
        return both[:NB], both[NB:]

    def none(square, partner):
        zero = jnp.zeros((NB, NB), jnp.bfloat16)
        return zero, zero

    working = (row_here & APART == 0) & (col_here == 0)
    lower, lower_far = lax.cond(working, compute, none, square, partner)
    received = lower
    far = row_here & APART != 0
    swapped = (row_here == middle) | (row_here == relieved)

    def route(rows, c, own):
        return [((r, 0), (r if own != (r == middle) else r + APART, c)) for r in rows]

    def send_far(c):
        sent = jnp.where(row_here == middle, lower, lower_far)
        return send(sent, route(workers, c, False)), (far != swapped) & (col_here == c)

    def send_own(c):
        sent = jnp.where(row_here == middle, lower_far, lower)
        return send(sent, route(targets, c, True)), (~far != swapped) & (col_here == c)

    def send_near(c):
        pairs = [((r, 0), (r + APART, 0)) for r in workers]
        return send(lower_far, pairs), far & (col_here == 0)

    even = range(2, n_col, 2)
    for step, columns in ((send_near, [0]), (send_own, even), (send_far, even)):
        for c in columns:
            got, takes = step(c)
            received = jnp.where(takes, got, received)
    sent = upper
    for step in range(2, len(down)):
        upper = upper_step(upper, step, upper)
    if len(beside_back) > 2:
        sent = upper
    pairs = [((a, 1), (b, 1)) for a, b in beside_back] + [((middle + 1, 0), (relieved, 0))]
    got = send(sent, pairs)
    takes = (col_here == 1) & (row_here > 1) & (row_here < middle)
    takes = takes | ((col_here == 0) & (row_here == relieved))
    upper = jnp.where(takes, got, upper)
    got = send(
        received, [((r, c), (r, c + 1)) for r in range(1, n_row) for c in range(0, n_col, 2)]
    )
    received = jnp.where(col_here % 2 == 0, received, got)
    received = jnp.where(row_here == 0, jnp.zeros_like(received), received)

    col_done = col_here * cols_dev + jnp.arange(cols_dev, dtype=jnp.int32) < NB
    upper = jnp.where(col_done[None, :], jnp.zeros_like(upper), upper)
    return matrix - jnp.dot(received, upper, preferred_element_type=jnp.float32)


def solution(mesh):
    return jax.shard_map(
        shards,
        mesh=mesh,
        in_specs=(P("row", "col"),),
        out_specs=P("row", "col"),
        check_vma=False,
    )
```

```python
import jax
import jax.numpy as jnp
from jax import lax
from jax.sharding import PartitionSpec as P

NB = 256
HIGH = lax.Precision.HIGH
APART = 2


def strides(size):
    out, stride = [], size // 2
    while stride:
        out.append(stride)
        stride //= 2
    return out


def multipliers(square, columns):
    identity = jnp.eye(NB, dtype=jnp.float32)
    diagonal = square * identity
    across = 1.0 / jnp.sum(diagonal, axis=0, keepdims=True)
    down = 1.0 / jnp.sum(diagonal, axis=1, keepdims=True)
    approx = down * (2.0 * identity - square * across)
    product = jnp.dot(jnp.concatenate([square, columns], axis=0), approx, precision=HIGH)
    return jnp.dot(product[NB:], 2.0 * identity - product[:NB], precision=HIGH)


def shards(matrix):
    rows_dev, cols_dev = matrix.shape
    assert rows_dev == NB
    n_row, n_col = lax.axis_size("row"), lax.axis_size("col")
    row_here, col_here = lax.axis_index("row"), lax.axis_index("col")

    def send(value, pairs):
        flat = [(r0 * n_col + c0, r1 * n_col + c1) for (r0, c0), (r1, c1) in pairs]
        return lax.ppermute(value, ("row", "col"), flat)

    def blocks(matrix):
        return matrix[:, :NB], matrix.astype(jnp.bfloat16)

    def no_blocks(matrix):
        return jnp.zeros((NB, NB), matrix.dtype), jnp.zeros(matrix.shape, jnp.bfloat16)

    sends_columns = (col_here == 0) & (row_here & APART != 0)
    pivot_columns, first_upper = lax.cond(
        sends_columns | (row_here == 0), blocks, no_blocks, matrix
    )
    upper = lax.optimization_barrier(jnp.where(row_here == 0, first_upper, 0))

    down = strides(n_row)
    middle = n_row // 2
    orders = [[down[-1]] + down[:-1], down]
    held = [[0], [0]]
    beside_steps = [[(0, middle)], [(middle, middle + 1)]]
    for stride in down[1:-1]:
        far = [b for step in beside_steps for _, b in step]
        beside_steps.append([(h, h + stride) for h in far])
    beside_steps[-1].append((0, 1))
    beside_back = [(middle + r - 2, r) for r in range(2, middle)]

    def among(rows):
        found = jnp.bool_(False)
        for row in rows:
            found = found | (row_here == row)
        return found

    def upper_step(value, step, sent):
        pairs = [((a, 1), (b, 1)) for a, b in beside_steps[step]]
        takes = (col_here == 1) & among([b for _, b in beside_steps[step]])
        for kind in range(2):
            stride = orders[kind][step]
            missing = sum(orders[kind][step + 1 :])
            takes = takes | (
                (col_here != 1)
                & (col_here % 2 == kind)
                & ((row_here & (stride | missing)) == stride)
            )
            pairs += [
                ((h, c), (h + stride, c))
                for h in held[kind]
                for c in range(3 * kind, n_col, 2)
            ]
            held[kind] = held[kind] + [h + stride for h in held[kind]]
        got = send(sent, pairs)
        return jnp.where(takes, got, value)

    workers = [r for r in range(n_row) if r & APART == 0]
    targets = workers[:1:-1]
    targets.insert(1, 1)
    square, partner = matrix[:, :NB], matrix[:, :NB]
    upper = upper_step(upper, 0, first_upper)
    for index, target in reversed(list(enumerate(targets))):
        served = [] if index > 1 else targets[:1] if index else [0] + targets[1:]
        pairs = [((0, 0), (target, 0))] + [((r + APART, 0), (r, 0)) for r in served]
        got = send(pivot_columns, pairs)
        square = jnp.where(row_here == target, got, square)
        for r in served:
            partner = jnp.where(row_here == r, got, partner)
    upper = upper_step(upper, 1, upper)

    def compute(square, partner):
        both = multipliers(square, jnp.concatenate([matrix[:, :NB], partner], axis=0))
        both = both.astype(jnp.bfloat16)
        return both[:NB], both[NB:]

    def none(square, partner):
        zero = jnp.zeros((NB, NB), jnp.bfloat16)
        return zero, zero

    working = (row_here & APART == 0) & (col_here == 0)
    lower, lower_far = lax.cond(working, compute, none, square, partner)
    received = lower
    far = row_here & APART != 0
    swapped = (row_here == middle) | (row_here == middle + APART)

    def route(rows, c, own):
        return [((r, 0), (r if own != (r == middle) else r + APART, c)) for r in rows]

    def send_far(c):
        sent = jnp.where(row_here == middle, lower, lower_far)
        return send(sent, route(workers, c, False)), (far != swapped) & (col_here == c)

    def send_own(c):
        sent = jnp.where(row_here == middle, lower_far, lower)
        return send(sent, route(targets, c, True)), (~far != swapped) & (col_here == c)

    def send_near(c):
        pairs = [((r, 0), (r + APART, 0)) for r in workers]
        return send(lower_far, pairs), far & (col_here == 0)

    even = range(2, n_col, 2)
    for step, columns in ((send_near, [0]), (send_own, even), (send_far, even)):
        for c in columns:
            got, takes = step(c)
            received = jnp.where(takes, got, received)
    sent = upper
    for step in range(2, len(down)):
        upper = upper_step(upper, step, upper)
    if len(beside_back) > 2:
        sent = upper
    got = send(sent, [((a, 1), (b, 1)) for a, b in beside_back])
    upper = jnp.where((col_here == 1) & (row_here > 1) & (row_here < middle), got, upper)
    got = send(
        received, [((r, c), (r, c + 1)) for r in range(1, n_row) for c in range(0, n_col, 2)]
    )
    received = jnp.where(col_here % 2 == 0, received, got)
    received = jnp.where(row_here == 0, jnp.zeros_like(received), received)

    col_done = col_here * cols_dev + jnp.arange(cols_dev, dtype=jnp.int32) < NB
    upper = jnp.where(col_done[None, :], jnp.zeros_like(upper), upper)
    return matrix - jnp.dot(received, upper, preferred_element_type=jnp.float32)


def solution(mesh):
    return jax.shard_map(
        shards,
        mesh=mesh,
        in_specs=(P("row", "col"),),
        out_specs=P("row", "col"),
        check_vma=False,
    )
```

```python
import jax
import jax.numpy as jnp
from jax import lax
from jax.sharding import PartitionSpec as P

NB = 256
HIGH = lax.Precision.HIGH
APART = 2


def strides(size):
    out, stride = [], size // 2
    while stride:
        out.append(stride)
        stride //= 2
    return out


def multipliers(square, columns):
    identity = jnp.eye(NB, dtype=jnp.float32)
    diagonal = square * identity
    across = 1.0 / jnp.sum(diagonal, axis=0, keepdims=True)
    down = 1.0 / jnp.sum(diagonal, axis=1, keepdims=True)
    approx = down * (2.0 * identity - square * across)
    product = jnp.dot(jnp.concatenate([square, columns], axis=0), approx, precision=HIGH)
    return jnp.dot(product[NB:], 2.0 * identity - product[:NB], precision=HIGH)


def shards(matrix):
    rows_dev, cols_dev = matrix.shape
    assert rows_dev == NB
    n_row, n_col = lax.axis_size("row"), lax.axis_size("col")
    row_here, col_here = lax.axis_index("row"), lax.axis_index("col")

    def send(value, pairs):
        flat = [(r0 * n_col + c0, r1 * n_col + c1) for (r0, c0), (r1, c1) in pairs]
        return lax.ppermute(value, ("row", "col"), flat)

    def blocks(matrix):
        return matrix[:, :NB], matrix.astype(jnp.bfloat16)

    def no_blocks(matrix):
        return jnp.zeros((NB, NB), matrix.dtype), jnp.zeros(matrix.shape, jnp.bfloat16)

    sends_columns = (col_here == 0) & (row_here & APART != 0)
    pivot_columns, first_upper = lax.cond(
        sends_columns | (row_here == 0), blocks, no_blocks, matrix
    )
    upper = lax.optimization_barrier(jnp.where(row_here == 0, first_upper, 0))

    down = strides(n_row)
    middle = n_row // 2
    orders = [[down[-1]] + down[:-1], down]
    held = [[0], [0]]
    beside_steps = [[(0, middle)], [(middle, middle + 1)]]
    for stride in down[1:-1]:
        far = [b for step in beside_steps for _, b in step]
        beside_steps.append([(h, h + stride) for h in far])
    beside_steps[-1].append((0, 1))
    beside_back = [(middle + r - 2, r) for r in range(2, middle)]

    def among(rows):
        found = jnp.bool_(False)
        for row in rows:
            found = found | (row_here == row)
        return found

    def upper_step(value, step, sent):
        pairs = [((a, 1), (b, 1)) for a, b in beside_steps[step]]
        takes = (col_here == 1) & among([b for _, b in beside_steps[step]])
        for kind in range(2):
            stride = orders[kind][step]
            missing = sum(orders[kind][step + 1 :])
            takes = takes | (
                (col_here != 1)
                & (col_here % 2 == kind)
                & ((row_here & (stride | missing)) == stride)
            )
            pairs += [
                ((h, c), (h + stride, c))
                for h in held[kind]
                for c in range(3 * kind, n_col, 2)
            ]
            held[kind] = held[kind] + [h + stride for h in held[kind]]
        got = send(sent, pairs)
        return jnp.where(takes, got, value)

    workers = [r for r in range(n_row) if r & APART == 0]
    targets = workers[2:]
    targets.insert(1, 1)
    square, partner = matrix[:, :NB], matrix[:, :NB]
    upper = upper_step(upper, 0, first_upper)
    for index, target in reversed(list(enumerate(targets))):
        served = [] if index > 1 else targets[:1] if index else [0] + targets[1:]
        pairs = [((0, 0), (target, 0))] + [((r + APART, 0), (r, 0)) for r in served]
        got = send(pivot_columns, pairs)
        square = jnp.where(row_here == target, got, square)
        for r in served:
            partner = jnp.where(row_here == r, got, partner)
    upper = upper_step(upper, 1, upper)

    def compute(square, partner):
        both = multipliers(square, jnp.concatenate([matrix[:, :NB], partner], axis=0))
        both = both.astype(jnp.bfloat16)
        return both[:NB], both[NB:]

    def none(square, partner):
        zero = jnp.zeros((NB, NB), jnp.bfloat16)
        return zero, zero

    working = (row_here & APART == 0) & (col_here == 0)
    lower, lower_far = lax.cond(working, compute, none, square, partner)
    received = lower
    far = row_here & APART != 0
    late = middle + 1
    swapped = (row_here == late) | (row_here == late + APART)

    def route(rows, c, own):
        return [((r, 0), (r if own != (r == late) else r + APART, c)) for r in rows]

    def send_far(c):
        sent = jnp.where(row_here == late, lower, lower_far)
        return send(sent, route(workers, c, False)), (far != swapped) & (col_here == c)

    def send_own(c):
        sent = jnp.where(row_here == late, lower_far, lower)
        return send(sent, route(targets, c, True)), (~far != swapped) & (col_here == c)

    def send_near(c):
        pairs = [((r, 0), (r + APART, 0)) for r in workers]
        return send(lower_far, pairs), far & (col_here == 0)

    even = range(2, n_col, 2)
    for step, columns in ((send_near, [0]), (send_own, even), (send_far, even)):
        for c in columns:
            got, takes = step(c)
            received = jnp.where(takes, got, received)
    sent = upper
    for step in range(2, len(down)):
        upper = upper_step(upper, step, upper)
    if len(beside_back) > 2:
        sent = upper
    got = send(sent, [((a, 1), (b, 1)) for a, b in beside_back])
    upper = jnp.where((col_here == 1) & (row_here > 1) & (row_here < middle), got, upper)
    got = send(
        received, [((r, c), (r, c + 1)) for r in range(1, n_row) for c in range(0, n_col, 2)]
    )
    received = jnp.where(col_here % 2 == 0, received, got)
    received = jnp.where(row_here == 0, jnp.zeros_like(received), received)

    col_done = col_here * cols_dev + jnp.arange(cols_dev, dtype=jnp.int32) < NB
    upper = jnp.where(col_done[None, :], jnp.zeros_like(upper), upper)
    return matrix - jnp.dot(received, upper, preferred_element_type=jnp.float32)


def solution(mesh):
    return jax.shard_map(
        shards,
        mesh=mesh,
        in_specs=(P("row", "col"),),
        out_specs=P("row", "col"),
        check_vma=False,
    )
```

```python
import jax
import jax.numpy as jnp
from jax import lax
from jax.sharding import PartitionSpec as P

NB = 256
HIGH = lax.Precision.HIGH
APART = 2


def strides(size):
    out, stride = [], size // 2
    while stride:
        out.append(stride)
        stride //= 2
    return out


def multipliers(square, columns):
    identity = jnp.eye(NB, dtype=jnp.float32)
    diagonal = square * identity
    across = 1.0 / jnp.sum(diagonal, axis=0, keepdims=True)
    down = 1.0 / jnp.sum(diagonal, axis=1, keepdims=True)
    approx = down * (2.0 * identity - square * across)
    product = jnp.dot(jnp.concatenate([square, columns], axis=0), approx, precision=HIGH)
    return jnp.dot(product[NB:], 2.0 * identity - product[:NB], precision=HIGH)


def shards(matrix):
    rows_dev, cols_dev = matrix.shape
    assert rows_dev == NB
    n_row, n_col = lax.axis_size("row"), lax.axis_size("col")
    row_here, col_here = lax.axis_index("row"), lax.axis_index("col")

    def send(value, pairs):
        flat = [(r0 * n_col + c0, r1 * n_col + c1) for (r0, c0), (r1, c1) in pairs]
        return lax.ppermute(value, ("row", "col"), flat)

    def blocks(matrix):
        return matrix[:, :NB], matrix.astype(jnp.bfloat16)

    def no_blocks(matrix):
        return jnp.zeros((NB, NB), matrix.dtype), jnp.zeros(matrix.shape, jnp.bfloat16)

    sends_columns = (col_here == 0) & (row_here & APART != 0)
    pivot_columns, first_upper = lax.cond(
        sends_columns | (row_here == 0), blocks, no_blocks, matrix
    )
    upper = lax.optimization_barrier(jnp.where(row_here == 0, first_upper, 0))

    down = strides(n_row)
    middle = n_row // 2
    orders = [[down[-1]] + down[:-1], down]
    held = [[0], [0]]
    beside_steps = [[(0, middle + 1)], [(middle + 1, middle)]]
    for stride in down[1:-1]:
        far = [b for step in beside_steps for _, b in step]
        beside_steps.append([(h, h + stride) for h in far])
    beside_steps[-1].append((0, 1))
    beside_back = [(middle + r - 2, r) for r in range(2, middle)]

    def among(rows):
        found = jnp.bool_(False)
        for row in rows:
            found = found | (row_here == row)
        return found

    def upper_step(value, step, sent):
        pairs = [((a, 1), (b, 1)) for a, b in beside_steps[step]]
        takes = (col_here == 1) & among([b for _, b in beside_steps[step]])
        for kind in range(2):
            stride = orders[kind][step]
            missing = sum(orders[kind][step + 1 :])
            takes = takes | (
                (col_here != 1)
                & (col_here % 2 == kind)
                & ((row_here & (stride | missing)) == stride)
            )
            pairs += [
                ((h, c), (h + stride, c))
                for h in held[kind]
                for c in range(3 * kind, n_col, 2)
            ]
            held[kind] = held[kind] + [h + stride for h in held[kind]]
        got = send(sent, pairs)
        return jnp.where(takes, got, value)

    workers = [r for r in range(n_row) if r & APART == 0]
    targets = workers[2:]
    targets.insert(1, 1)
    square, partner = matrix[:, :NB], matrix[:, :NB]
    upper = upper_step(upper, 0, first_upper)
    for index, target in reversed(list(enumerate(targets))):
        served = [] if index > 1 else targets[:1] if index else [0] + targets[1:]
        pairs = [((0, 0), (target, 0))] + [((r + APART, 0), (r, 0)) for r in served]
        got = send(pivot_columns, pairs)
        square = jnp.where(row_here == target, got, square)
        for r in served:
            partner = jnp.where(row_here == r, got, partner)
    upper = upper_step(upper, 1, upper)

    def compute(square, partner):
        both = multipliers(square, jnp.concatenate([matrix[:, :NB], partner], axis=0))
        both = both.astype(jnp.bfloat16)
        return both[:NB], both[NB:]

    def none(square, partner):
        zero = jnp.zeros((NB, NB), jnp.bfloat16)
        return zero, zero

    working = (row_here & APART == 0) & (col_here == 0)
    lower, lower_far = lax.cond(working, compute, none, square, partner)
    received = lower
    far = row_here & APART != 0
    late = middle + 1
    swapped = (row_here == late) | (row_here == late + APART)

    def route(rows, c, own):
        return [((r, 0), (r if own != (r == late) else r + APART, c)) for r in rows]

    def send_far(c):
        sent = jnp.where(row_here == late, lower, lower_far)
        return send(sent, route(workers, c, False)), (far != swapped) & (col_here == c)

    def send_own(c):
        sent = jnp.where(row_here == late, lower_far, lower)
        return send(sent, route(targets, c, True)), (~far != swapped) & (col_here == c)

    def send_near(c):
        pairs = [((r, 0), (r + APART, 0)) for r in workers]
        return send(lower_far, pairs), far & (col_here == 0)

    even = range(2, n_col, 2)
    for step, columns in ((send_near, [0]), (send_own, even), (send_far, even)):
        for c in columns:
            got, takes = step(c)
            received = jnp.where(takes, got, received)
    sent = upper
    for step in range(2, len(down)):
        upper = upper_step(upper, step, upper)
    if len(beside_back) > 2:
        sent = upper
    got = send(sent, [((a, 1), (b, 1)) for a, b in beside_back])
    upper = jnp.where((col_here == 1) & (row_here > 1) & (row_here < middle), got, upper)
    got = send(
        received, [((r, c), (r, c + 1)) for r in range(1, n_row) for c in range(0, n_col, 2)]
    )
    received = jnp.where(col_here % 2 == 0, received, got)
    received = jnp.where(row_here == 0, jnp.zeros_like(received), received)

    col_done = col_here * cols_dev + jnp.arange(cols_dev, dtype=jnp.int32) < NB
    upper = jnp.where(col_done[None, :], jnp.zeros_like(upper), upper)
    return matrix - jnp.dot(received, upper, preferred_element_type=jnp.float32)


def solution(mesh):
    return jax.shard_map(
        shards,
        mesh=mesh,
        in_specs=(P("row", "col"),),
        out_specs=P("row", "col"),
        check_vma=False,
    )
```

```python
import jax
import jax.numpy as jnp
from jax import lax
from jax.sharding import PartitionSpec as P

NB = 256
HIGH = lax.Precision.HIGH
APART = 2


def strides(size):
    out, stride = [], size // 2
    while stride:
        out.append(stride)
        stride //= 2
    return out


def multipliers(square, columns):
    identity = jnp.eye(NB, dtype=jnp.float32)
    diagonal = square * identity
    across = 1.0 / jnp.sum(diagonal, axis=0, keepdims=True)
    down = 1.0 / jnp.sum(diagonal, axis=1, keepdims=True)
    approx = down * (2.0 * identity - square * across)
    product = jnp.dot(jnp.concatenate([square, columns], axis=0), approx, precision=HIGH)
    return jnp.dot(product[NB:], 2.0 * identity - product[:NB], precision=HIGH)


def shards(matrix):
    rows_dev, cols_dev = matrix.shape
    assert rows_dev == NB
    n_row, n_col = lax.axis_size("row"), lax.axis_size("col")
    row_here, col_here = lax.axis_index("row"), lax.axis_index("col")

    def send(value, pairs):
        flat = [(r0 * n_col + c0, r1 * n_col + c1) for (r0, c0), (r1, c1) in pairs]
        return lax.ppermute(value, ("row", "col"), flat)

    def blocks(matrix):
        return matrix[:, :NB], matrix.astype(jnp.bfloat16)

    def no_blocks(matrix):
        return jnp.zeros((NB, NB), matrix.dtype), jnp.zeros(matrix.shape, jnp.bfloat16)

    sends_columns = (col_here == 0) & (row_here & APART != 0)
    pivot_columns, first_upper = lax.cond(
        sends_columns | (row_here == 0), blocks, no_blocks, matrix
    )
    upper = lax.optimization_barrier(jnp.where(row_here == 0, first_upper, 0))

    down = strides(n_row)
    middle = n_row // 2
    orders = [[down[-1]] + down[:-1], down]
    held = [[0], [0]]
    beside_steps = [[(0, middle)], [(middle, middle + 1)]]
    for stride in down[1:-1]:
        far = [b for step in beside_steps for _, b in step]
        beside_steps.append([(h, h + stride) for h in far])
    beside_steps[-1].append((0, 1))
    beside_back = [(middle + r - 2, r) for r in range(2, middle)]

    def among(rows):
        found = jnp.bool_(False)
        for row in rows:
            found = found | (row_here == row)
        return found

    def upper_step(value, step, sent):
        pairs = [((a, 1), (b, 1)) for a, b in beside_steps[step]]
        takes = (col_here == 1) & among([b for _, b in beside_steps[step]])
        for kind in range(2):
            stride = orders[kind][step]
            missing = sum(orders[kind][step + 1 :])
            takes = takes | (
                (col_here != 1)
                & (col_here % 2 == kind)
                & ((row_here & (stride | missing)) == stride)
            )
            pairs += [
                ((h, c), (h + stride, c))
                for h in held[kind]
                for c in range(3 * kind, n_col, 2)
            ]
            held[kind] = held[kind] + [h + stride for h in held[kind]]
        got = send(sent, pairs)
        return jnp.where(takes, got, value), got

    workers = [r for r in range(n_row) if r & APART == 0]
    targets = workers[:1:-1]
    targets.insert(1, 1)
    square, partner = matrix[:, :NB], matrix[:, :NB]
    upper, _ = upper_step(upper, 0, first_upper)
    for index, target in reversed(list(enumerate(targets))):
        served = [] if index > 1 else targets[:1] if index else [0] + targets[1:]
        pairs = [((0, 0), (target, 0))] + [((r + APART, 0), (r, 0)) for r in served]
        got = send(pivot_columns, pairs)
        square = jnp.where(row_here == target, got, square)
        for r in served:
            partner = jnp.where(row_here == r, got, partner)
    upper, _ = upper_step(upper, 1, upper)

    def compute(square, partner):
        both = multipliers(square, jnp.concatenate([matrix[:, :NB], partner], axis=0))
        both = both.astype(jnp.bfloat16)
        return both[:NB], both[NB:]

    def none(square, partner):
        zero = jnp.zeros((NB, NB), jnp.bfloat16)
        return zero, zero

    working = (row_here & APART == 0) & (col_here == 0)
    lower, lower_far = lax.cond(working, compute, none, square, partner)
    received = lower
    far = row_here & APART != 0
    swapped = (row_here == middle) | (row_here == middle + APART)

    def route(rows, c, own):
        return [((r, 0), (r if own != (r == middle) else r + APART, c)) for r in rows]

    def send_far(c):
        sent = jnp.where(row_here == middle, lower, lower_far)
        return send(sent, route(workers, c, False)), (far != swapped) & (col_here == c)

    def send_own(c):
        sent = jnp.where(row_here == middle, lower_far, lower)
        return send(sent, route(targets, c, True)), (~far != swapped) & (col_here == c)

    even = range(2, n_col, 2)
    for step, columns in ((send_own, even), (send_far, even)):
        for c in columns:
            got, takes = step(c)
            received = jnp.where(takes, got, received)
    sent = upper
    for step in range(2, len(down) - 1):
        upper, _ = upper_step(upper, step, upper)
    both = jnp.concatenate([lower_far, upper[:, NB:]], axis=1)
    last_sent = jnp.where(col_here == 0, both, upper)
    upper, got = upper_step(upper, len(down) - 1, last_sent)
    received = jnp.where(far & (col_here == 0), got[:, :NB], received)
    if len(beside_back) > 2:
        sent = upper
    got = send(sent, [((a, 1), (b, 1)) for a, b in beside_back])
    upper = jnp.where((col_here == 1) & (row_here > 1) & (row_here < middle), got, upper)
    got = send(
        received, [((r, c), (r, c + 1)) for r in range(1, n_row) for c in range(0, n_col, 2)]
    )
    received = jnp.where(col_here % 2 == 0, received, got)
    received = jnp.where(row_here == 0, jnp.zeros_like(received), received)

    col_done = col_here * cols_dev + jnp.arange(cols_dev, dtype=jnp.int32) < NB
    upper = jnp.where(col_done[None, :], jnp.zeros_like(upper), upper)
    return matrix - jnp.dot(received, upper, preferred_element_type=jnp.float32)


def solution(mesh):
    return jax.shard_map(
        shards,
        mesh=mesh,
        in_specs=(P("row", "col"),),
        out_specs=P("row", "col"),
        check_vma=False,
    )
```

```python
import jax
import jax.numpy as jnp
from jax import lax
from jax.sharding import PartitionSpec as P

NB = 256
HIGH = lax.Precision.HIGH
APART = 2


def strides(size):
    out, stride = [], size // 2
    while stride:
        out.append(stride)
        stride //= 2
    return out


def multipliers(square, columns):
    identity = jnp.eye(NB, dtype=jnp.float32)
    diagonal = square * identity
    across = 1.0 / jnp.sum(diagonal, axis=0, keepdims=True)
    down = 1.0 / jnp.sum(diagonal, axis=1, keepdims=True)
    approx = down * (2.0 * identity - square * across)
    product = jnp.dot(jnp.concatenate([square, columns], axis=0), approx, precision=HIGH)
    return jnp.dot(product[NB:], 2.0 * identity - product[:NB], precision=HIGH)


def shards(matrix):
    rows_dev, cols_dev = matrix.shape
    assert rows_dev == NB
    n_row, n_col = lax.axis_size("row"), lax.axis_size("col")
    row_here, col_here = lax.axis_index("row"), lax.axis_index("col")

    def send(value, pairs):
        flat = [(r0 * n_col + c0, r1 * n_col + c1) for (r0, c0), (r1, c1) in pairs]
        return lax.ppermute(value, ("row", "col"), flat)

    def blocks(matrix):
        return matrix[:, :NB], matrix.astype(jnp.bfloat16)

    def no_blocks(matrix):
        return jnp.zeros((NB, NB), matrix.dtype), jnp.zeros(matrix.shape, jnp.bfloat16)

    sends_columns = (col_here == 0) & (row_here & APART != 0)
    pivot_columns, first_upper = lax.cond(
        sends_columns | (row_here == 0), blocks, no_blocks, matrix
    )
    upper = lax.optimization_barrier(jnp.where(row_here == 0, first_upper, 0))

    down = strides(n_row)
    middle = n_row // 2
    orders = [[down[-1]] + down[:-1], down]
    held = [[0], [0]]
    beside_steps = [[(0, middle)], [(middle, middle + 1)]]
    for stride in down[1:-1]:
        far = [b for step in beside_steps for _, b in step]
        beside_steps.append([(h, h + stride) for h in far])
    beside_steps[-1].append((0, 1))
    beside_back = [(middle + r - 2, r) for r in range(2, middle)]

    def among(rows):
        found = jnp.bool_(False)
        for row in rows:
            found = found | (row_here == row)
        return found

    def upper_step(value, step, sent):
        pairs = [((a, 1), (b, 1)) for a, b in beside_steps[step]]
        takes = (col_here == 1) & among([b for _, b in beside_steps[step]])
        for kind in range(2):
            stride = orders[kind][step]
            missing = sum(orders[kind][step + 1 :])
            takes = takes | (
                (col_here != 1)
                & (col_here % 2 == kind)
                & ((row_here & (stride | missing)) == stride)
            )
            pairs += [
                ((h, c), (h + stride, c))
                for h in held[kind]
                for c in range(3 * kind, n_col, 2)
            ]
            held[kind] = held[kind] + [h + stride for h in held[kind]]
        got = send(sent, pairs)
        return jnp.where(takes, got, value)

    workers = [r for r in range(n_row) if r & APART == 0]
    targets = workers[:1:-1]
    targets.insert(1, 1)
    square, partner = matrix[:, :NB], matrix[:, :NB]
    upper = upper_step(upper, 0, first_upper)
    for index, target in reversed(list(enumerate(targets))):
        served = [] if index > 1 else targets[:1] if index else [0] + targets[1:]
        pairs = [((0, 0), (target, 0))] + [((r + APART, 0), (r, 0)) for r in served]
        got = send(pivot_columns, pairs)
        square = jnp.where(row_here == target, got, square)
        for r in served:
            partner = jnp.where(row_here == r, got, partner)
    upper = upper_step(upper, 1, upper)

    def compute(square, partner):
        both = multipliers(square, jnp.concatenate([matrix[:, :NB], partner], axis=0))
        both = both.astype(jnp.bfloat16)
        return both[:NB], both[NB:]

    def none(square, partner):
        zero = jnp.zeros((NB, NB), jnp.bfloat16)
        return zero, zero

    working = (row_here & APART == 0) & (col_here == 0)
    lower, lower_far = lax.cond(working, compute, none, square, partner)
    received = lower
    far = row_here & APART != 0
    swapped = (row_here == middle) | (row_here == middle + APART)

    def route(rows, c, own):
        return [((r, 0), (r if own != (r == middle) else r + APART, c)) for r in rows]

    def send_far(c):
        sent = jnp.where(row_here == middle, lower, lower_far)
        return send(sent, route(workers, c, False)), (far != swapped) & (col_here == c)

    def send_own(c):
        sent = jnp.where(row_here == middle, lower_far, lower)
        return send(sent, route(targets, c, True)), (~far != swapped) & (col_here == c)

    def send_near(c):
        pairs = [((r, 0), (r + APART, 0)) for r in workers]
        return send(lower_far, pairs), far & (col_here == 0)

    odd = range(3, n_col, 2)
    for step, columns in ((send_near, [0]), (send_own, odd), (send_far, odd)):
        for c in columns:
            got, takes = step(c)
            received = jnp.where(takes, got, received)
    sent = upper
    for step in range(2, len(down)):
        upper = upper_step(upper, step, upper)
    if len(beside_back) > 2:
        sent = upper
    got = send(sent, [((a, 1), (b, 1)) for a, b in beside_back])
    upper = jnp.where((col_here == 1) & (row_here > 1) & (row_here < middle), got, upper)
    got = send(
        received,
        [((r, 0), (r, 1)) for r in range(1, n_row)]
        + [((r, c), (r, c - 1)) for r in range(1, n_row) for c in odd],
    )
    received = jnp.where((col_here == 0) | (col_here > 1) & (col_here % 2 == 1), received, got)
    received = jnp.where(row_here == 0, jnp.zeros_like(received), received)

    col_done = col_here * cols_dev + jnp.arange(cols_dev, dtype=jnp.int32) < NB
    upper = jnp.where(col_done[None, :], jnp.zeros_like(upper), upper)
    return matrix - jnp.dot(received, upper, preferred_element_type=jnp.float32)


def solution(mesh):
    return jax.shard_map(
        shards,
        mesh=mesh,
        in_specs=(P("row", "col"),),
        out_specs=P("row", "col"),
        check_vma=False,
    )
```

```python
import jax
import jax.numpy as jnp
from jax import lax
from jax.sharding import PartitionSpec as P

NB = 256
HIGH = lax.Precision.HIGH
APART = 2


def strides(size):
    out, stride = [], size // 2
    while stride:
        out.append(stride)
        stride //= 2
    return out


def multipliers(square, columns):
    identity = jnp.eye(NB, dtype=jnp.float32)
    diagonal = square * identity
    across = 1.0 / jnp.sum(diagonal, axis=0, keepdims=True)
    down = 1.0 / jnp.sum(diagonal, axis=1, keepdims=True)
    approx = down * (2.0 * identity - square * across)
    product = jnp.dot(jnp.concatenate([square, columns], axis=0), approx, precision=HIGH)
    return jnp.dot(product[NB:], 2.0 * identity - product[:NB], precision=HIGH)


def shards(matrix):
    rows_dev, cols_dev = matrix.shape
    assert rows_dev == NB
    n_row, n_col = lax.axis_size("row"), lax.axis_size("col")
    row_here, col_here = lax.axis_index("row"), lax.axis_index("col")

    def send(value, pairs):
        flat = [(r0 * n_col + c0, r1 * n_col + c1) for (r0, c0), (r1, c1) in pairs]
        return lax.ppermute(value, ("row", "col"), flat)

    def blocks(matrix):
        return matrix[:, :NB], matrix.astype(jnp.bfloat16)

    def no_blocks(matrix):
        return jnp.zeros((NB, NB), matrix.dtype), jnp.zeros(matrix.shape, jnp.bfloat16)

    sends_columns = (col_here == 0) & (row_here & APART != 0)
    pivot_columns, first_upper = lax.cond(
        sends_columns | (row_here == 0), blocks, no_blocks, matrix
    )
    upper = lax.optimization_barrier(jnp.where(row_here == 0, first_upper, 0))

    down = strides(n_row)
    middle = n_row // 2
    orders = [[down[-1]] + down[:-1], down]
    held = [[0], [0]]
    fits = cols_dev == 2 * NB
    row_upper = upper[:, NB:]
    beside_steps = [[(0, middle)], [(middle, middle + 1)]]
    for stride in down[1:-1]:
        far = [b for step in beside_steps for _, b in step]
        beside_steps.append([(h, h + stride) for h in far])
    beside_steps[-1].append((0, 1))
    beside_back = [(middle + r - 2, r) for r in range(2, middle)]

    def among(rows):
        found = jnp.bool_(False)
        for row in rows:
            found = found | (row_here == row)
        return found

    def upper_step(value, step, sent):
        pairs = [((a, 1), (b, 1)) for a, b in beside_steps[step]]
        takes = (col_here == 1) & among([b for _, b in beside_steps[step]])
        for kind in range(2):
            stride = orders[kind][step]
            missing = sum(orders[kind][step + 1 :])
            takes = takes | (
                (col_here != 1)
                & (col_here % 2 == kind)
                & ((row_here & (stride | missing)) == stride)
            )
            hops = [(h, h + stride) for h in held[kind]]
            pairs += [((a, c), (b, c)) for a, b in hops for c in range(2 + kind, n_col, 2)]
            if kind == 0:
                if step == len(down) - 1:
                    crossed = {middle: middle + APART + 1, middle + 1: middle + APART}
                    hops = [(a, crossed.get(a, b)) for a, b in hops if a or not fits]
                pairs += [((a, 0), (b, 0)) for a, b in hops]
            held[kind] = held[kind] + [h + stride for h in held[kind]]
        got = send(sent, pairs)
        return jnp.where(takes, got, value)

    workers = [r for r in range(n_row) if r & APART == 0]
    targets = workers[:1:-1]
    targets.insert(1, 1)
    square, partner = matrix[:, :NB], matrix[:, :NB]
    upper = upper_step(upper, 0, first_upper)
    for index, target in reversed(list(enumerate(targets))):
        served = [] if index > 1 else targets[:1] if index else [0] + targets[1:]
        pairs = [((0, 0), (target, 0))] + [((r + APART, 0), (r, 0)) for r in served]
        got = send(pivot_columns, pairs)
        square = jnp.where(row_here == target, got, square)
        for r in served:
            partner = jnp.where(row_here == r, got, partner)
    upper = upper_step(upper, 1, upper)

    def compute(square, partner):
        both = multipliers(square, jnp.concatenate([matrix[:, :NB], partner], axis=0))
        both = both.astype(jnp.bfloat16)
        return both[:NB], both[NB:]

    def none(square, partner):
        zero = jnp.zeros((NB, NB), jnp.bfloat16)
        return zero, zero

    working = (row_here & APART == 0) & (col_here == 0)
    lower, lower_far = lax.cond(working, compute, none, square, partner)
    received = lower
    far = row_here & APART != 0
    swapped = (row_here == middle) | (row_here == middle + APART)

    def route(rows, c, own):
        return [((r, 0), (r if own != (r == middle) else r + APART, c)) for r in rows]

    def send_far(c):
        sent = jnp.where(row_here == middle, lower, lower_far)
        return send(sent, route(workers, c, False)), (far != swapped) & (col_here == c)

    def send_own(c):
        sent = jnp.where(row_here == middle, lower_far, lower)
        pairs = route(targets, c, True)
        if fits and c == 3:
            sent = jnp.where(row_here == 0, row_upper, sent)
            pairs += [((0, 0), (APART, 0))]
        return send(sent, pairs), (~far != swapped) & (col_here == c)

    def send_near(c):
        pairs = [((r, 0), (r + APART, 0)) for r in workers]
        return send(lower_far, pairs), far & (col_here == 0)

    odd = range(3, n_col, 2)
    for step, columns in ((send_near, [0]), (send_own, odd), (send_far, odd)):
        for c in columns:
            got, takes = step(c)
            received = jnp.where(takes, got, received)
            if step is send_own and c == 3:
                third_got = got
    sent = upper
    for step in range(2, len(down)):
        upper = upper_step(upper, step, upper)
    if len(beside_back) > 2:
        sent = upper
    got = send(sent, [((a, 1), (b, 1)) for a, b in beside_back])
    upper = jnp.where((col_here == 1) & (row_here > 1) & (row_here < middle), got, upper)
    got = send(
        received,
        [((r, 0), (r, 1)) for r in range(1, n_row)]
        + [((r, c), (r, c - 1)) for r in range(1, n_row) for c in odd],
    )
    received = jnp.where((col_here == 0) | (col_here > 1) & (col_here % 2 == 1), received, got)
    received = jnp.where(row_here == 0, jnp.zeros_like(received), received)

    if fits:
        relayed = jnp.pad(third_got, ((0, 0), (NB, 0)))
        upper = jnp.where((row_here == APART) & (col_here == 0), relayed, upper)
    col_done = col_here * cols_dev + jnp.arange(cols_dev, dtype=jnp.int32) < NB
    upper = jnp.where(col_done[None, :], jnp.zeros_like(upper), upper)
    return matrix - jnp.dot(received, upper, preferred_element_type=jnp.float32)


def solution(mesh):
    return jax.shard_map(
        shards,
        mesh=mesh,
        in_specs=(P("row", "col"),),
        out_specs=P("row", "col"),
        check_vma=False,
    )
```

```python
import jax
import jax.numpy as jnp
from jax import lax
from jax.sharding import PartitionSpec as P

NB = 256
HIGH = lax.Precision.HIGH
APART = 2


def strides(size):
    out, stride = [], size // 2
    while stride:
        out.append(stride)
        stride //= 2
    return out


def multipliers(square, columns):
    identity = jnp.eye(NB, dtype=jnp.float32)
    diagonal = square * identity
    across = 1.0 / jnp.sum(diagonal, axis=0, keepdims=True)
    down = 1.0 / jnp.sum(diagonal, axis=1, keepdims=True)
    approx = down * (2.0 * identity - square * across)
    product = jnp.dot(jnp.concatenate([square, columns], axis=0), approx, precision=HIGH)
    return jnp.dot(product[NB:], 2.0 * identity - product[:NB], precision=HIGH)


def shards(matrix):
    rows_dev, cols_dev = matrix.shape
    assert rows_dev == NB
    n_row, n_col = lax.axis_size("row"), lax.axis_size("col")
    row_here, col_here = lax.axis_index("row"), lax.axis_index("col")

    def send(value, pairs):
        flat = [(r0 * n_col + c0, r1 * n_col + c1) for (r0, c0), (r1, c1) in pairs]
        return lax.ppermute(value, ("row", "col"), flat)

    def blocks(matrix):
        return matrix[:, :NB], matrix.astype(jnp.bfloat16)

    def no_blocks(matrix):
        return jnp.zeros((NB, NB), matrix.dtype), jnp.zeros(matrix.shape, jnp.bfloat16)

    sends_columns = (col_here == 0) & (row_here & APART != 0)
    pivot_columns, first_upper = lax.cond(
        sends_columns | (row_here == 0), blocks, no_blocks, matrix
    )
    upper = lax.optimization_barrier(jnp.where(row_here == 0, first_upper, 0))

    down = strides(n_row)
    middle = n_row // 2
    orders = [[down[-1]] + down[:-1], down]
    held = [[0], [0]]
    fits = cols_dev == 2 * NB
    row_upper = upper[:, NB:]
    beside_steps = [[(0, middle)], [(middle, middle + 1)]]
    for stride in down[1:-1]:
        far = [b for step in beside_steps for _, b in step]
        beside_steps.append([(h, h + stride) for h in far])
    beside_steps[-1].append((0, 1))
    beside_back = [(middle + r - 2, r) for r in range(2, middle)]

    def among(rows):
        found = jnp.bool_(False)
        for row in rows:
            found = found | (row_here == row)
        return found

    def upper_step(value, step, sent):
        pairs = [((a, 1), (b, 1)) for a, b in beside_steps[step]]
        takes = (col_here == 1) & among([b for _, b in beside_steps[step]])
        for kind in range(2):
            stride = orders[kind][step]
            missing = sum(orders[kind][step + 1 :])
            takes = takes | (
                (col_here != 1)
                & (col_here % 2 == kind)
                & ((row_here & (stride | missing)) == stride)
            )
            hops = [(h, h + stride) for h in held[kind]]
            pairs += [((a, c), (b, c)) for a, b in hops for c in range(2 + kind, n_col, 2)]
            if kind == 0:
                if step == len(down) - 1 and fits:
                    hops = [(a, b if a else middle + APART) for a, b in hops if a != middle]
                pairs += [((a, 0), (b, 0)) for a, b in hops]
            held[kind] = held[kind] + [h + stride for h in held[kind]]
        got = send(sent, pairs)
        return jnp.where(takes, got, value)

    workers = [r for r in range(n_row) if r & APART == 0]
    targets = workers[:1:-1]
    targets.insert(1, 1)
    square, partner = matrix[:, :NB], matrix[:, :NB]
    upper = upper_step(upper, 0, first_upper)
    for index, target in reversed(list(enumerate(targets))):
        served = [] if index > 1 else targets[:1] if index else [0] + targets[1:]
        pairs = [((0, 0), (target, 0))] + [((r + APART, 0), (r, 0)) for r in served]
        got = send(pivot_columns, pairs)
        square = jnp.where(row_here == target, got, square)
        for r in served:
            partner = jnp.where(row_here == r, got, partner)
    upper = upper_step(upper, 1, upper)

    def compute(square, partner):
        both = multipliers(square, jnp.concatenate([matrix[:, :NB], partner], axis=0))
        both = both.astype(jnp.bfloat16)
        return both[:NB], both[NB:]

    def none(square, partner):
        zero = jnp.zeros((NB, NB), jnp.bfloat16)
        return zero, zero

    working = (row_here & APART == 0) & (col_here == 0)
    lower, lower_far = lax.cond(working, compute, none, square, partner)
    received = lower
    far = row_here & APART != 0
    swapped = (row_here == middle) | (row_here == middle + APART)

    def route(rows, c, own):
        return [((r, 0), (r if own != (r == middle) else r + APART, c)) for r in rows]

    def send_far(c):
        sent = jnp.where(row_here == middle, lower, lower_far)
        return send(sent, route(workers, c, False)), (far != swapped) & (col_here == c)

    def send_own(c):
        sent = jnp.where(row_here == middle, lower_far, lower)
        pairs = route(targets, c, True)
        if fits and c == 3:
            sent = jnp.where(row_here == 0, row_upper, sent)
            pairs += [((0, 0), (APART, 0))]
        return send(sent, pairs), (~far != swapped) & (col_here == c)

    def send_near(c):
        pairs = [((r, 0), (r + APART, 0)) for r in workers]
        return send(lower_far, pairs), far & (col_here == 0)

    odd = range(3, n_col, 2)
    for step, columns in ((send_near, [0]), (send_own, odd), (send_far, odd)):
        for c in columns:
            got, takes = step(c)
            received = jnp.where(takes, got, received)
            if step is send_own and c == 3:
                third_got = got
    sent = upper
    for step in range(2, len(down)):
        upper = upper_step(upper, step, upper)
    if len(beside_back) > 2:
        sent = upper
    got = send(sent, [((a, 1), (b, 1)) for a, b in beside_back])
    upper = jnp.where((col_here == 1) & (row_here > 1) & (row_here < middle), got, upper)
    got = send(
        received,
        [((r, 0), (r, 1)) for r in range(1, n_row)]
        + [((r, c), (r, c - 1)) for r in range(1, n_row) for c in odd],
    )
    received = jnp.where((col_here == 0) | (col_here > 1) & (col_here % 2 == 1), received, got)
    received = jnp.where(row_here == 0, jnp.zeros_like(received), received)

    if fits:
        relayed = jnp.pad(third_got, ((0, 0), (NB, 0)))
        upper = jnp.where((row_here == APART) & (col_here == 0), relayed, upper)
    col_done = col_here * cols_dev + jnp.arange(cols_dev, dtype=jnp.int32) < NB
    upper = jnp.where(col_done[None, :], jnp.zeros_like(upper), upper)
    return matrix - jnp.dot(received, upper, preferred_element_type=jnp.float32)


def solution(mesh):
    return jax.shard_map(
        shards,
        mesh=mesh,
        in_specs=(P("row", "col"),),
        out_specs=P("row", "col"),
        check_vma=False,
    )
```

```python
import jax
import jax.numpy as jnp
from jax import lax
from jax.sharding import PartitionSpec as P

NB = 256
HIGH = lax.Precision.HIGH
APART = 2


def strides(size):
    out, stride = [], size // 2
    while stride:
        out.append(stride)
        stride //= 2
    return out


def multipliers(square, columns):
    identity = jnp.eye(NB, dtype=jnp.float32)
    diagonal = square * identity
    across = 1.0 / jnp.sum(diagonal, axis=0, keepdims=True)
    down = 1.0 / jnp.sum(diagonal, axis=1, keepdims=True)
    approx = down * (2.0 * identity - square * across)
    product = jnp.dot(jnp.concatenate([square, columns], axis=0), approx, precision=HIGH)
    return jnp.dot(product[NB:], 2.0 * identity - product[:NB], precision=HIGH)


def shards(matrix):
    rows_dev, cols_dev = matrix.shape
    assert rows_dev == NB
    n_row, n_col = lax.axis_size("row"), lax.axis_size("col")
    row_here, col_here = lax.axis_index("row"), lax.axis_index("col")

    def send(value, pairs):
        flat = [(r0 * n_col + c0, r1 * n_col + c1) for (r0, c0), (r1, c1) in pairs]
        return lax.ppermute(value, ("row", "col"), flat)

    def blocks(matrix):
        return matrix[:, :NB], matrix.astype(jnp.bfloat16)

    def no_blocks(matrix):
        return jnp.zeros((NB, NB), matrix.dtype), jnp.zeros(matrix.shape, jnp.bfloat16)

    sends_columns = (col_here == 0) & (row_here & APART != 0)
    pivot_columns, first_upper = lax.cond(
        sends_columns | (row_here == 0), blocks, no_blocks, matrix
    )
    upper = lax.optimization_barrier(jnp.where(row_here == 0, first_upper, 0))

    down = strides(n_row)
    middle = n_row // 2
    orders = [[down[-1]] + down[:-1], down]
    held = [[0], [0]]
    fits = cols_dev == 2 * NB
    row_upper = upper[:, NB:]
    beside_steps = [[(0, middle)], [(middle, middle + 1)]]
    for stride in down[1:-1]:
        far = [b for step in beside_steps for _, b in step]
        beside_steps.append([(h, h + stride) for h in far])
    beside_steps[-1].append((0, 1))
    beside_back = [(middle + r - 2, r) for r in range(2, middle)]

    def among(rows):
        found = jnp.bool_(False)
        for row in rows:
            found = found | (row_here == row)
        return found

    def upper_step(value, step, sent):
        pairs = [((a, 1), (b, 1)) for a, b in beside_steps[step]]
        takes = (col_here == 1) & among([b for _, b in beside_steps[step]])
        for kind in range(2):
            stride = orders[kind][step]
            missing = sum(orders[kind][step + 1 :])
            takes = takes | (
                (col_here != 1)
                & (col_here % 2 == kind)
                & ((row_here & (stride | missing)) == stride)
            )
            hops = [(h, h + stride) for h in held[kind]]
            pairs += [((a, c), (b, c)) for a, b in hops for c in range(2 + kind, n_col, 2)]
            if kind == 0:
                if step == len(down) - 1:
                    crossed = {middle: middle + APART + 1, middle + 1: middle + APART}
                    hops = [(a, crossed.get(a, b)) for a, b in hops if a or not fits]
                pairs += [((a, 0), (b, 0)) for a, b in hops]
            held[kind] = held[kind] + [h + stride for h in held[kind]]
        got = send(sent, pairs)
        return jnp.where(takes, got, value)

    workers = [r for r in range(n_row) if r & APART == 0]
    targets = workers[:1:-1]
    targets.insert(1, 1)
    square, partner = matrix[:, :NB], matrix[:, :NB]
    upper = upper_step(upper, 0, first_upper)
    for index, target in reversed(list(enumerate(targets))):
        served = [] if index > 1 else targets[:1] if index else [0] + targets[1:]
        pairs = [((0, 0), (target, 0))] + [((r + APART, 0), (r, 0)) for r in served]
        got = send(pivot_columns, pairs)
        square = jnp.where(row_here == target, got, square)
        for r in served:
            partner = jnp.where(row_here == r, got, partner)
    upper = upper_step(upper, 1, upper)

    def compute(square, partner):
        both = multipliers(square, jnp.concatenate([matrix[:, :NB], partner], axis=0))
        both = both.astype(jnp.bfloat16)
        return both[:NB], both[NB:]

    def none(square, partner):
        zero = jnp.zeros((NB, NB), jnp.bfloat16)
        return zero, zero

    working = (row_here & APART == 0) & (col_here == 0)
    lower, lower_far = lax.cond(working, compute, none, square, partner)
    received = lower
    far = row_here & APART != 0
    swapped = (row_here == middle) | (row_here == middle + APART)

    def route(rows, c, own):
        return [((r, 0), (r if own != (r == middle) else r + APART, c)) for r in rows]

    def send_far(c):
        sent = jnp.where(row_here == middle, lower, lower_far)
        return send(sent, route(workers, c, False)), (far != swapped) & (col_here == c)

    def send_own(c):
        sent = jnp.where(row_here == middle, lower_far, lower)
        pairs = route(targets, c, True)
        if fits and c == 3:
            sent = jnp.where(row_here == 0, row_upper, sent)
            pairs += [((0, 0), (APART, 0))]
        return send(sent, pairs), (~far != swapped) & (col_here == c)

    def send_near(c):
        pairs = [((r, 0), (r + APART, 0)) for r in workers]
        return send(lower_far, pairs), far & (col_here == 0)

    odd = range(3, n_col, 2)
    for step, columns in ((send_near, [0]), (send_own, odd), (send_far, odd)):
        for c in columns:
            got, takes = step(c)
            received = jnp.where(takes, got, received)
            if step is send_own and c == 3:
                third_got = got
    sent = upper
    for step in range(2, len(down)):
        upper = upper_step(upper, step, upper)
    if len(beside_back) > 2:
        sent = upper
    got = send(sent, [((a, 1), (b, 1)) for a, b in beside_back])
    upper = jnp.where((col_here == 1) & (row_here > 1) & (row_here < middle), got, upper)
    got = send(
        received,
        [((r, 0), (r, 1)) for r in range(1, n_row)]
        + [((r, c), (r, c - 1)) for r in range(1, n_row) for c in odd],
    )
    received = jnp.where((col_here == 0) | (col_here > 1) & (col_here % 2 == 1), received, got)
    received = jnp.where(row_here == 0, jnp.zeros_like(received), received)

    done, kept = upper[:, :NB], upper[:, NB:]
    if fits:
        kept = jnp.where((row_here == APART) & (col_here == 0), third_got, kept)
    upper = jnp.concatenate([jnp.where(col_here == 0, jnp.zeros_like(done), done), kept], axis=1)
    return matrix - jnp.dot(received, upper, preferred_element_type=jnp.float32)


def solution(mesh):
    return jax.shard_map(
        shards,
        mesh=mesh,
        in_specs=(P("row", "col"),),
        out_specs=P("row", "col"),
        check_vma=False,
    )
```

```python
import jax
import jax.numpy as jnp
from jax import lax
from jax.sharding import PartitionSpec as P

NB = 256
HIGH = lax.Precision.HIGH
APART = 2


def strides(size):
    out, stride = [], size // 2
    while stride:
        out.append(stride)
        stride //= 2
    return out


def multipliers(square, columns):
    identity = jnp.eye(NB, dtype=jnp.float32)
    diagonal = square * identity
    across = 1.0 / jnp.sum(diagonal, axis=0, keepdims=True)
    down = 1.0 / jnp.sum(diagonal, axis=1, keepdims=True)
    approx = down * (2.0 * identity - square * across)
    product = jnp.dot(jnp.concatenate([square, columns], axis=0), approx, precision=HIGH)
    return jnp.dot(product[NB:], 2.0 * identity - product[:NB], precision=HIGH)


def shards(matrix):
    rows_dev, cols_dev = matrix.shape
    assert rows_dev == NB
    n_row, n_col = lax.axis_size("row"), lax.axis_size("col")
    row_here, col_here = lax.axis_index("row"), lax.axis_index("col")

    def send(value, pairs):
        flat = [(r0 * n_col + c0, r1 * n_col + c1) for (r0, c0), (r1, c1) in pairs]
        return lax.ppermute(value, ("row", "col"), flat)

    def blocks(matrix):
        return matrix[:, :NB], matrix.astype(jnp.bfloat16)

    def no_blocks(matrix):
        return jnp.zeros((NB, NB), matrix.dtype), jnp.zeros(matrix.shape, jnp.bfloat16)

    sends_columns = (col_here == 0) & (row_here & APART != 0)
    pivot_columns, first_upper = lax.cond(
        sends_columns | (row_here == 0), blocks, no_blocks, matrix
    )
    upper = lax.optimization_barrier(jnp.where(row_here == 0, first_upper, 0))

    down = strides(n_row)
    middle = n_row // 2
    orders = [[down[-1]] + down[:-1], down]
    held = [[0], [0]]
    fits = cols_dev == 2 * NB
    row_upper = upper[:, NB:]
    beside_steps = [[(0, middle)], [(middle, middle + 1)]]
    for stride in down[1:-1]:
        far = [b for step in beside_steps for _, b in step]
        beside_steps.append([(h, h + stride) for h in far])
    beside_steps[-1].append((0, 1))
    beside_back = [(middle + r - 2, r) for r in range(2, middle)]

    def among(rows):
        found = jnp.bool_(False)
        for row in rows:
            found = found | (row_here == row)
        return found

    def upper_step(value, step, sent):
        pairs = [((a, 1), (b, 1)) for a, b in beside_steps[step]]
        takes = (col_here == 1) & among([b for _, b in beside_steps[step]])
        for kind in range(2):
            stride = orders[kind][step]
            missing = sum(orders[kind][step + 1 :])
            takes = takes | (
                (col_here != 1)
                & (col_here % 2 == kind)
                & ((row_here & (stride | missing)) == stride)
            )
            hops = [(h, h + stride) for h in held[kind]]
            pairs += [((a, c), (b, c)) for a, b in hops for c in range(2 + kind, n_col, 2)]
            if kind == 0:
                if step == len(down) - 1:
                    crossed = {middle: middle + APART + 1, middle + 1: middle + APART}
                    hops = [(a, crossed.get(a, b)) for a, b in hops if a or not fits]
                pairs += [((a, 0), (b, 0)) for a, b in hops]
            held[kind] = held[kind] + [h + stride for h in held[kind]]
        got = send(sent, pairs)
        return jnp.where(takes, got, value)

    workers = [r for r in range(n_row) if r & APART == 0]
    targets = workers[:1:-1]
    targets.insert(1, 1)
    square, partner = matrix[:, :NB], matrix[:, :NB]
    upper = upper_step(upper, 0, first_upper)
    for index, target in reversed(list(enumerate(targets))):
        served = [] if index > 1 else targets[:1] if index else [0] + targets[1:]
        pairs = [((0, 0), (target, 0))] + [((r + APART, 0), (r, 0)) for r in served]
        got = send(pivot_columns, pairs)
        square = jnp.where(row_here == target, got, square)
        for r in served:
            partner = jnp.where(row_here == r, got, partner)
    upper = upper_step(upper, 1, upper)

    def compute(square, partner):
        both = multipliers(square, jnp.concatenate([matrix[:, :NB], partner], axis=0))
        both = both.astype(jnp.bfloat16)
        return jnp.where(row_here == 0, jnp.zeros_like(both[:NB]), both[:NB]), both[NB:]

    def none(square, partner):
        zero = jnp.zeros((NB, NB), jnp.bfloat16)
        return zero, zero

    working = (row_here & APART == 0) & (col_here == 0)
    lower, lower_far = lax.cond(working, compute, none, square, partner)
    received = lower
    far = row_here & APART != 0
    swapped = (row_here == middle) | (row_here == middle + APART)

    def route(rows, c, own):
        return [((r, 0), (r if own != (r == middle) else r + APART, c)) for r in rows]

    def send_far(c):
        sent = jnp.where(row_here == middle, lower, lower_far)
        return send(sent, route(workers, c, False)), (far != swapped) & (col_here == c)

    def send_own(c):
        sent = jnp.where(row_here == middle, lower_far, lower)
        pairs = route(targets, c, True)
        if fits and c == 3:
            sent = jnp.where(row_here == 0, row_upper, sent)
            pairs += [((0, 0), (APART, 0))]
        return send(sent, pairs), (~far != swapped) & (col_here == c)

    def send_near(c):
        pairs = [((r, 0), (r + APART, 0)) for r in workers]
        return send(lower_far, pairs), far & (col_here == 0)

    odd = range(3, n_col, 2)
    for step, columns in ((send_near, [0]), (send_own, odd), (send_far, odd)):
        for c in columns:
            got, takes = step(c)
            received = jnp.where(takes, got, received)
            if step is send_own and c == 3:
                third_got = got
    sent = upper
    for step in range(2, len(down)):
        upper = upper_step(upper, step, upper)
    if len(beside_back) > 2:
        sent = upper
    got = send(sent, [((a, 1), (b, 1)) for a, b in beside_back])
    upper = jnp.where((col_here == 1) & (row_here > 1) & (row_here < middle), got, upper)
    got = send(
        received,
        [((r, 0), (r, 1)) for r in range(1, n_row)]
        + [((r, c), (r, c - 1)) for r in range(1, n_row) for c in odd],
    )
    received = jnp.where((col_here == 0) | (col_here > 1) & (col_here % 2 == 1), received, got)

    if fits:
        relayed = jnp.pad(third_got, ((0, 0), (NB, 0)))
        upper = jnp.where((row_here == APART) & (col_here == 0), relayed, upper)
    col_done = col_here * cols_dev + jnp.arange(cols_dev, dtype=jnp.int32) < NB
    upper = jnp.where(col_done[None, :], jnp.zeros_like(upper), upper)
    return matrix - jnp.dot(received, upper, preferred_element_type=jnp.float32)


def solution(mesh):
    return jax.shard_map(
        shards,
        mesh=mesh,
        in_specs=(P("row", "col"),),
        out_specs=P("row", "col"),
        check_vma=False,
    )
```

```python
import jax
import jax.numpy as jnp
from jax import lax
from jax.sharding import PartitionSpec as P

NB = 256
HIGH = lax.Precision.HIGH
APART = 2


def strides(size):
    out, stride = [], size // 2
    while stride:
        out.append(stride)
        stride //= 2
    return out


def multipliers(square, columns):
    identity = jnp.eye(NB, dtype=jnp.float32)
    diagonal = square * identity
    across = 1.0 / jnp.sum(diagonal, axis=0, keepdims=True)
    down = 1.0 / jnp.sum(diagonal, axis=1, keepdims=True)
    approx = down * (2.0 * identity - square * across)
    product = jnp.dot(jnp.concatenate([square, columns], axis=0), approx, precision=HIGH)
    return jnp.dot(product[NB:], 2.0 * identity - product[:NB], precision=HIGH)


def shards(matrix):
    rows_dev, cols_dev = matrix.shape
    assert rows_dev == NB
    n_row, n_col = lax.axis_size("row"), lax.axis_size("col")
    row_here, col_here = lax.axis_index("row"), lax.axis_index("col")

    def send(value, pairs):
        flat = [(r0 * n_col + c0, r1 * n_col + c1) for (r0, c0), (r1, c1) in pairs]
        return lax.ppermute(value, ("row", "col"), flat)

    def blocks(matrix):
        return matrix[:, :NB], matrix.astype(jnp.bfloat16)

    def no_blocks(matrix):
        return jnp.zeros((NB, NB), matrix.dtype), jnp.zeros(matrix.shape, jnp.bfloat16)

    sends_columns = (col_here == 0) & (row_here & APART != 0)
    pivot_columns, first_upper = lax.cond(
        sends_columns | (row_here == 0), blocks, no_blocks, matrix
    )
    upper = lax.optimization_barrier(jnp.where(row_here == 0, first_upper, 0))

    down = strides(n_row)
    middle = n_row // 2
    orders = [[down[-1]] + down[:-1], down]
    held = [[0], [0]]
    beside_steps = [[(0, middle)], [(middle, middle + 1)]]
    for stride in down[1:-1]:
        far = [b for step in beside_steps for _, b in step]
        beside_steps.append([(h, h + stride) for h in far])
    beside_steps[-1].append((0, 1))
    beside_back = [(middle + r - 2, r) for r in range(2, middle)]

    def among(rows):
        found = jnp.bool_(False)
        for row in rows:
            found = found | (row_here == row)
        return found

    def upper_step(value, step, sent):
        pairs = [((a, 1), (b, 1)) for a, b in beside_steps[step]]
        takes = (col_here == 1) & among([b for _, b in beside_steps[step]])
        for kind in range(2):
            stride = orders[kind][step]
            missing = sum(orders[kind][step + 1 :])
            takes = takes | (
                (col_here != 1)
                & (col_here % 2 == kind)
                & ((row_here & (stride | missing)) == stride)
            )
            hops = [(h, h + stride) for h in held[kind]]
            pairs += [((a, c), (b, c)) for a, b in hops for c in range(2 + kind, n_col, 2)]
            if kind == 0:
                if step == len(down) - 1:
                    crossed = {middle: middle + APART + 1, middle + 1: middle + APART}
                    hops = [(a, crossed.get(a, b)) for a, b in hops]
                pairs += [((a, 0), (b, 0)) for a, b in hops]
            held[kind] = held[kind] + [h + stride for h in held[kind]]
        got = send(sent, pairs)
        return jnp.where(takes, got, value)

    workers = [r for r in range(n_row) if r & APART == 0]
    targets = workers[:1:-1]
    targets.insert(1, 1)
    square, partner = matrix[:, :NB], matrix[:, :NB]
    upper = upper_step(upper, 0, first_upper)
    for index, target in reversed(list(enumerate(targets))):
        served = [] if index > 1 else targets[:1] if index else [0] + targets[1:]
        pairs = [((0, 0), (target, 0))] + [((r + APART, 0), (r, 0)) for r in served]
        got = send(pivot_columns, pairs)
        square = jnp.where(row_here == target, got, square)
        for r in served:
            partner = jnp.where(row_here == r, got, partner)
    upper = upper_step(upper, 1, upper)

    def compute(square, partner):
        both = multipliers(square, jnp.concatenate([matrix[:, :NB], partner], axis=0))
        both = both.astype(jnp.bfloat16)
        return jnp.where(row_here == 0, jnp.zeros_like(both[:NB]), both[:NB]), both[NB:]

    def none(square, partner):
        zero = jnp.zeros((NB, NB), jnp.bfloat16)
        return zero, zero

    working = (row_here & APART == 0) & (col_here == 0)
    lower, lower_far = lax.cond(working, compute, none, square, partner)
    received = lower
    far = row_here & APART != 0
    swapped = (row_here == middle) | (row_here == middle + APART)

    def route(rows, c, own):
        return [((r, 0), (r if own != (r == middle) else r + APART, c)) for r in rows]

    def send_far(c):
        sent = jnp.where(row_here == middle, lower, lower_far)
        return send(sent, route(workers, c, False)), (far != swapped) & (col_here == c)

    def send_own(c):
        sent = jnp.where(row_here == middle, lower_far, lower)
        return send(sent, route(targets, c, True)), (~far != swapped) & (col_here == c)

    def send_near(c):
        pairs = [((r, 0), (r + APART, 0)) for r in workers]
        return send(lower_far, pairs), far & (col_here == 0)

    odd = range(3, n_col, 2)
    for step, columns in ((send_near, [0]), (send_own, odd), (send_far, odd)):
        for c in columns:
            got, takes = step(c)
            received = jnp.where(takes, got, received)
    sent = upper
    for step in range(2, len(down)):
        upper = upper_step(upper, step, upper)
    if len(beside_back) > 2:
        sent = upper
    got = send(sent, [((a, 1), (b, 1)) for a, b in beside_back])
    upper = jnp.where((col_here == 1) & (row_here > 1) & (row_here < middle), got, upper)
    got = send(
        received,
        [((r, 0), (r, 1)) for r in range(1, n_row)]
        + [((r, c), (r, c - 1)) for r in range(1, n_row) for c in odd],
    )
    received = jnp.where((col_here == 0) | (col_here > 1) & (col_here % 2 == 1), received, got)

    col_done = col_here * cols_dev + jnp.arange(cols_dev, dtype=jnp.int32) < NB
    upper = jnp.where(col_done[None, :], jnp.zeros_like(upper), upper)
    return matrix - jnp.dot(received, upper, preferred_element_type=jnp.float32)


def solution(mesh):
    return jax.shard_map(
        shards,
        mesh=mesh,
        in_specs=(P("row", "col"),),
        out_specs=P("row", "col"),
        check_vma=False,
    )
```

```python
import jax
import jax.numpy as jnp
from jax import lax
from jax.sharding import PartitionSpec as P

NB = 256
HIGH = lax.Precision.HIGH
APART = 2


def strides(size):
    out, stride = [], size // 2
    while stride:
        out.append(stride)
        stride //= 2
    return out


def multipliers(square, columns):
    identity = jnp.eye(NB, dtype=jnp.float32)
    diagonal = square * identity
    across = 1.0 / jnp.sum(diagonal, axis=0, keepdims=True)
    down = 1.0 / jnp.sum(diagonal, axis=1, keepdims=True)
    approx = down * (2.0 * identity - square * across)
    product = jnp.dot(jnp.concatenate([square, columns], axis=0), approx, precision=HIGH)
    return jnp.dot(product[NB:], 2.0 * identity - product[:NB], precision=HIGH)


def shards(matrix):
    rows_dev, cols_dev = matrix.shape
    assert rows_dev == NB
    n_row, n_col = lax.axis_size("row"), lax.axis_size("col")
    row_here, col_here = lax.axis_index("row"), lax.axis_index("col")

    def send(value, pairs):
        flat = [(r0 * n_col + c0, r1 * n_col + c1) for (r0, c0), (r1, c1) in pairs]
        return lax.ppermute(value, ("row", "col"), flat)

    def blocks(matrix):
        return matrix[:, :NB], matrix.astype(jnp.bfloat16)

    def no_blocks(matrix):
        return jnp.zeros((NB, NB), matrix.dtype), jnp.zeros(matrix.shape, jnp.bfloat16)

    sends_columns = (col_here == 0) & (row_here & APART != 0)
    pivot_columns, first_upper = lax.cond(
        sends_columns | (row_here == 0), blocks, no_blocks, matrix
    )
    upper = lax.optimization_barrier(jnp.where(row_here == 0, first_upper, 0))

    down = strides(n_row)
    middle = n_row // 2
    orders = [[down[-1]] + down[:-1], down]
    held = [[0], [0]]
    beside_steps = [[(0, middle)], [(middle, middle + 1)]]
    for stride in down[1:-1]:
        far = [b for step in beside_steps for _, b in step]
        beside_steps.append([(h, h + stride) for h in far])
    beside_steps[-1].append((0, 1))
    beside_back = [(middle + r - 2, r) for r in range(2, middle)]

    def among(rows):
        found = jnp.bool_(False)
        for row in rows:
            found = found | (row_here == row)
        return found

    def upper_step(value, step, sent):
        pairs = [((a, 1), (b, 1)) for a, b in beside_steps[step]]
        takes = (col_here == 1) & among([b for _, b in beside_steps[step]])
        for kind in range(2):
            stride = orders[kind][step]
            missing = sum(orders[kind][step + 1 :])
            takes = takes | (
                (col_here != 1)
                & (col_here % 2 == kind)
                & ((row_here & (stride | missing)) == stride)
            )
            hops = [(h, h + stride) for h in held[kind]]
            pairs += [((a, c), (b, c)) for a, b in hops for c in range(2 + kind, n_col, 2)]
            if kind == 0:
                if step == len(down) - 1:
                    crossed = {middle: middle + APART + 1, middle + 1: middle + APART}
                    hops = [(a, crossed.get(a, b)) for a, b in hops]
                pairs += [((a, 0), (b, 0)) for a, b in hops]
            held[kind] = held[kind] + [h + stride for h in held[kind]]
        got = send(sent, pairs)
        return jnp.where(takes, got, value)

    workers = [r for r in range(n_row) if r & APART == 0]
    targets = workers[:0:-1]
    square, partner = matrix[:, :NB], matrix[:, :NB]
    upper = upper_step(upper, 0, first_upper)
    for index, target in reversed(list(enumerate(targets))):
        served = [] if index > 1 else targets[:1] if index else [0] + targets[1:]
        pairs = [((0, 0), (target, 0))] + [((r + APART, 0), (r, 0)) for r in served]
        got = send(pivot_columns, pairs)
        square = jnp.where(row_here == target, got, square)
        for r in served:
            partner = jnp.where(row_here == r, got, partner)
    upper = upper_step(upper, 1, upper)

    def compute(square, partner):
        both = multipliers(square, jnp.concatenate([matrix[:, :NB], partner], axis=0))
        both = both.astype(jnp.bfloat16)
        return jnp.where(row_here == 0, jnp.zeros_like(both[:NB]), both[:NB]), both[NB:]

    def none(square, partner):
        zero = jnp.zeros((NB, NB), jnp.bfloat16)
        return zero, zero

    working = (row_here & APART == 0) & (col_here == 0)
    lower, lower_far = lax.cond(working, compute, none, square, partner)
    received = lower
    far = row_here & APART != 0
    swapped = (row_here == middle) | (row_here == middle + APART)

    def route(rows, c, own):
        return [((r, 0), (r if own != (r == middle) else r + APART, c)) for r in rows]

    def send_far(c):
        sent = jnp.where(row_here == middle, lower, lower_far)
        return send(sent, route(workers, c, False)), (far != swapped) & (col_here == c)

    def send_own(c):
        sent = jnp.where(row_here == middle, lower_far, lower)
        return send(sent, route(targets, c, True)), (~far != swapped) & (col_here == c)

    def send_near(c):
        pairs = [((r, 0), (r + APART, 0)) for r in workers]
        return send(lower_far, pairs), far & (col_here == 0)

    odd = range(3, n_col, 2)
    for step, columns in ((send_near, [0]), (send_own, odd), (send_far, odd)):
        for c in columns:
            got, takes = step(c)
            received = jnp.where(takes, got, received)
    sent = upper
    for step in range(2, len(down)):
        upper = upper_step(upper, step, upper)
    if len(beside_back) > 2:
        sent = upper
    got = send(sent, [((a, 1), (b, 1)) for a, b in beside_back])
    upper = jnp.where((col_here == 1) & (row_here > 1) & (row_here < middle), got, upper)
    got = send(
        received,
        [((r, 0), (r, 1)) for r in range(1, n_row)]
        + [((r, c), (r, c - 1)) for r in range(1, n_row) for c in odd],
    )
    received = jnp.where((col_here == 0) | (col_here > 1) & (col_here % 2 == 1), received, got)

    col_done = col_here * cols_dev + jnp.arange(cols_dev, dtype=jnp.int32) < NB
    upper = jnp.where(col_done[None, :], jnp.zeros_like(upper), upper)
    return matrix - jnp.dot(received, upper, preferred_element_type=jnp.float32)


def solution(mesh):
    return jax.shard_map(
        shards,
        mesh=mesh,
        in_specs=(P("row", "col"),),
        out_specs=P("row", "col"),
        check_vma=False,
    )
```

```python
import jax
import jax.numpy as jnp
from jax import lax
from jax.sharding import PartitionSpec as P

NB = 256
HIGH = lax.Precision.HIGH
APART = 2


def strides(size):
    out, stride = [], size // 2
    while stride:
        out.append(stride)
        stride //= 2
    return out


def multipliers(square, columns):
    identity = jnp.eye(NB, dtype=jnp.float32)
    diagonal = square * identity
    across = 1.0 / jnp.sum(diagonal, axis=0, keepdims=True)
    down = 1.0 / jnp.sum(diagonal, axis=1, keepdims=True)
    approx = down * (2.0 * identity - square * across)
    product = jnp.dot(jnp.concatenate([square, columns], axis=0), approx, precision=HIGH)
    return jnp.dot(product[NB:], 2.0 * identity - product[:NB], precision=HIGH)


def shards(matrix):
    rows_dev, cols_dev = matrix.shape
    assert rows_dev == NB
    n_row, n_col = lax.axis_size("row"), lax.axis_size("col")
    row_here, col_here = lax.axis_index("row"), lax.axis_index("col")

    def send(value, pairs):
        flat = [(r0 * n_col + c0, r1 * n_col + c1) for (r0, c0), (r1, c1) in pairs]
        return lax.ppermute(value, ("row", "col"), flat)

    def blocks(matrix):
        return matrix[:, :NB], matrix.astype(jnp.bfloat16)

    def no_blocks(matrix):
        return jnp.zeros((NB, NB), matrix.dtype), jnp.zeros(matrix.shape, jnp.bfloat16)

    sends_columns = (col_here == 0) & (row_here & APART != 0)
    pivot_columns, first_upper = lax.cond(
        sends_columns | (row_here == 0), blocks, no_blocks, matrix
    )
    upper = lax.optimization_barrier(jnp.where(row_here == 0, first_upper, 0))

    down = strides(n_row)
    middle = n_row // 2
    orders = [[down[-1]] + down[:-1], down]
    held = [[0], [0]]
    beside_steps = [[(0, middle)], [(middle, middle + 1)]]
    for stride in down[1:-1]:
        far = [b for step in beside_steps for _, b in step]
        beside_steps.append([(h, h + stride) for h in far])
    beside_steps[-1].append((0, 1))
    beside_back = [(middle + r - 2, r) for r in range(2, middle)]
    if n_row == 4 * APART:
        beside_steps[-1] = [(middle, n_row - 1), (middle + 1, APART + 1), (0, 1)]
        beside_back = [(middle, middle + APART), (middle + 1, APART)]

    def among(rows):
        found = jnp.bool_(False)
        for row in rows:
            found = found | (row_here == row)
        return found

    def upper_step(value, step, sent):
        pairs = [((a, 1), (b, 1)) for a, b in beside_steps[step]]
        takes = (col_here == 1) & among([b for _, b in beside_steps[step]])
        for kind in range(2):
            stride = orders[kind][step]
            missing = sum(orders[kind][step + 1 :])
            takes = takes | (
                (col_here != 1)
                & (col_here % 2 == kind)
                & ((row_here & (stride | missing)) == stride)
            )
            hops = [(h, h + stride) for h in held[kind]]
            pairs += [((a, c), (b, c)) for a, b in hops for c in range(2 + kind, n_col, 2)]
            if kind == 0:
                if step == len(down) - 1:
                    crossed = {middle: middle + APART + 1, middle + 1: middle + APART}
                    hops = [(a, crossed.get(a, b)) for a, b in hops]
                pairs += [((a, 0), (b, 0)) for a, b in hops]
            held[kind] = held[kind] + [h + stride for h in held[kind]]
        got = send(sent, pairs)
        return jnp.where(takes, got, value)

    workers = [r for r in range(n_row) if r & APART == 0]
    targets = workers[:1:-1]
    targets.insert(1, 1)
    square, partner = matrix[:, :NB], matrix[:, :NB]
    upper = upper_step(upper, 0, first_upper)
    for index, target in reversed(list(enumerate(targets))):
        served = [] if index > 1 else targets[:1] if index else [0] + targets[1:]
        pairs = [((0, 0), (target, 0))] + [((r + APART, 0), (r, 0)) for r in served]
        got = send(pivot_columns, pairs)
        square = jnp.where(row_here == target, got, square)
        for r in served:
            partner = jnp.where(row_here == r, got, partner)
    upper = upper_step(upper, 1, upper)

    def compute(square, partner):
        both = multipliers(square, jnp.concatenate([matrix[:, :NB], partner], axis=0))
        both = both.astype(jnp.bfloat16)
        return jnp.where(row_here == 0, jnp.zeros_like(both[:NB]), both[:NB]), both[NB:]

    def none(square, partner):
        zero = jnp.zeros((NB, NB), jnp.bfloat16)
        return zero, zero

    working = (row_here & APART == 0) & (col_here == 0)
    lower, lower_far = lax.cond(working, compute, none, square, partner)
    received = lower
    far = row_here & APART != 0
    swapped = (row_here == middle) | (row_here == middle + APART)

    def route(rows, c, own):
        return [((r, 0), (r if own != (r == middle) else r + APART, c)) for r in rows]

    def send_far(c):
        sent = jnp.where(row_here == middle, lower, lower_far)
        return send(sent, route(workers, c, False)), (far != swapped) & (col_here == c)

    def send_own(c):
        sent = jnp.where(row_here == middle, lower_far, lower)
        return send(sent, route(targets, c, True)), (~far != swapped) & (col_here == c)

    def send_near(c):
        pairs = [((r, 0), (r + APART, 0)) for r in workers]
        return send(lower_far, pairs), far & (col_here == 0)

    odd = range(3, n_col, 2)
    for step, columns in ((send_near, [0]), (send_own, odd), (send_far, odd)):
        for c in columns:
            got, takes = step(c)
            received = jnp.where(takes, got, received)
    sent = upper
    for step in range(2, len(down)):
        upper = upper_step(upper, step, upper)
    if len(beside_back) > 2:
        sent = upper
    got = send(sent, [((a, 1), (b, 1)) for a, b in beside_back])
    upper = jnp.where((col_here == 1) & among([b for _, b in beside_back]), got, upper)
    got = send(
        received,
        [((r, 0), (r, 1)) for r in range(1, n_row)]
        + [((r, c), (r, c - 1)) for r in range(1, n_row) for c in odd],
    )
    received = jnp.where((col_here == 0) | (col_here > 1) & (col_here % 2 == 1), received, got)

    col_done = col_here * cols_dev + jnp.arange(cols_dev, dtype=jnp.int32) < NB
    upper = jnp.where(col_done[None, :], jnp.zeros_like(upper), upper)
    return matrix - jnp.dot(received, upper, preferred_element_type=jnp.float32)


def solution(mesh):
    return jax.shard_map(
        shards,
        mesh=mesh,
        in_specs=(P("row", "col"),),
        out_specs=P("row", "col"),
        check_vma=False,
    )
```

```python
import jax
import jax.numpy as jnp
from jax import lax
from jax.sharding import PartitionSpec as P

NB = 256
HIGH = lax.Precision.HIGH
APART = 2


def strides(size):
    out, stride = [], size // 2
    while stride:
        out.append(stride)
        stride //= 2
    return out


def multipliers(square, columns):
    identity = jnp.eye(NB, dtype=jnp.float32)
    diagonal = square * identity
    across = 1.0 / jnp.sum(diagonal, axis=0, keepdims=True)
    down = 1.0 / jnp.sum(diagonal, axis=1, keepdims=True)
    approx = down * (2.0 * identity - square * across)
    rest = 2.0 * identity - jnp.dot(square, approx, precision=HIGH)
    return jnp.dot(jnp.dot(columns, approx, precision=HIGH), rest, precision=HIGH)


def shards(matrix):
    rows_dev, cols_dev = matrix.shape
    assert rows_dev == NB
    n_row, n_col = lax.axis_size("row"), lax.axis_size("col")
    row_here, col_here = lax.axis_index("row"), lax.axis_index("col")

    def send(value, pairs):
        flat = [(r0 * n_col + c0, r1 * n_col + c1) for (r0, c0), (r1, c1) in pairs]
        return lax.ppermute(value, ("row", "col"), flat)

    def blocks(matrix):
        return matrix[:, :NB], matrix.astype(jnp.bfloat16)

    def no_blocks(matrix):
        return jnp.zeros((NB, NB), matrix.dtype), jnp.zeros(matrix.shape, jnp.bfloat16)

    sends_columns = (col_here == 0) & (row_here & APART != 0)
    pivot_columns, first_upper = lax.cond(
        sends_columns | (row_here == 0), blocks, no_blocks, matrix
    )
    upper = lax.optimization_barrier(jnp.where(row_here == 0, first_upper, 0))

    down = strides(n_row)
    middle = n_row // 2
    orders = [[down[-1]] + down[:-1], down]
    held = [[0], [0]]
    beside_steps = [[(0, middle)], [(middle, middle + 1)]]
    for stride in down[1:-1]:
        far = [b for step in beside_steps for _, b in step]
        beside_steps.append([(h, h + stride) for h in far])
    beside_steps[-1].append((0, 1))
    beside_back = [(middle + r - 2, r) for r in range(2, middle)]

    def among(rows):
        found = jnp.bool_(False)
        for row in rows:
            found = found | (row_here == row)
        return found

    def upper_step(value, step, sent):
        pairs = [((a, 1), (b, 1)) for a, b in beside_steps[step]]
        takes = (col_here == 1) & among([b for _, b in beside_steps[step]])
        for kind in range(2):
            stride = orders[kind][step]
            missing = sum(orders[kind][step + 1 :])
            takes = takes | (
                (col_here != 1)
                & (col_here % 2 == kind)
                & ((row_here & (stride | missing)) == stride)
            )
            hops = [(h, h + stride) for h in held[kind]]
            pairs += [((a, c), (b, c)) for a, b in hops for c in range(2 + kind, n_col, 2)]
            if kind == 0:
                if step == len(down) - 1:
                    crossed = {middle: middle + APART + 1, middle + 1: middle + APART}
                    hops = [(a, crossed.get(a, b)) for a, b in hops]
                pairs += [((a, 0), (b, 0)) for a, b in hops]
            held[kind] = held[kind] + [h + stride for h in held[kind]]
        got = send(sent, pairs)
        return jnp.where(takes, got, value)

    workers = [r for r in range(n_row) if r & APART == 0]
    targets = workers[:1:-1]
    targets.insert(1, 1)
    square, partner = matrix[:, :NB], matrix[:, :NB]
    upper = upper_step(upper, 0, first_upper)
    for index, target in reversed(list(enumerate(targets))):
        served = [] if index > 1 else targets[:1] if index else [0] + targets[1:]
        pairs = [((0, 0), (target, 0))] + [((r + APART, 0), (r, 0)) for r in served]
        got = send(pivot_columns, pairs)
        square = jnp.where(row_here == target, got, square)
        for r in served:
            partner = jnp.where(row_here == r, got, partner)
    upper = upper_step(upper, 1, upper)

    def compute(square, partner):
        both = multipliers(square, jnp.concatenate([matrix[:, :NB], partner], axis=0))
        both = both.astype(jnp.bfloat16)
        return jnp.where(row_here == 0, jnp.zeros_like(both[:NB]), both[:NB]), both[NB:]

    def none(square, partner):
        zero = jnp.zeros((NB, NB), jnp.bfloat16)
        return zero, zero

    working = (row_here & APART == 0) & (col_here == 0)
    lower, lower_far = lax.cond(working, compute, none, square, partner)
    received = lower
    far = row_here & APART != 0
    swapped = (row_here == middle) | (row_here == middle + APART)

    def route(rows, c, own):
        return [((r, 0), (r if own != (r == middle) else r + APART, c)) for r in rows]

    def send_far(c):
        sent = jnp.where(row_here == middle, lower, lower_far)
        return send(sent, route(workers, c, False)), (far != swapped) & (col_here == c)

    def send_own(c):
        sent = jnp.where(row_here == middle, lower_far, lower)
        return send(sent, route(targets, c, True)), (~far != swapped) & (col_here == c)

    def send_near(c):
        pairs = [((r, 0), (r + APART, 0)) for r in workers]
        return send(lower_far, pairs), far & (col_here == 0)

    odd = range(3, n_col, 2)
    for step, columns in ((send_near, [0]), (send_own, odd), (send_far, odd)):
        for c in columns:
            got, takes = step(c)
            received = jnp.where(takes, got, received)
    sent = upper
    for step in range(2, len(down)):
        upper = upper_step(upper, step, upper)
    if len(beside_back) > 2:
        sent = upper
    got = send(sent, [((a, 1), (b, 1)) for a, b in beside_back])
    upper = jnp.where((col_here == 1) & (row_here > 1) & (row_here < middle), got, upper)
    got = send(
        received,
        [((r, 0), (r, 1)) for r in range(1, n_row)]
        + [((r, c), (r, c - 1)) for r in range(1, n_row) for c in odd],
    )
    received = jnp.where((col_here == 0) | (col_here > 1) & (col_here % 2 == 1), received, got)

    col_done = col_here * cols_dev + jnp.arange(cols_dev, dtype=jnp.int32) < NB
    upper = jnp.where(col_done[None, :], jnp.zeros_like(upper), upper)
    return matrix - jnp.dot(received, upper, preferred_element_type=jnp.float32)


def solution(mesh):
    return jax.shard_map(
        shards,
        mesh=mesh,
        in_specs=(P("row", "col"),),
        out_specs=P("row", "col"),
        check_vma=False,
    )
```
